32 devices in a mesh: patch: 8 (over z, y), chan: 4 (over x, core).
Axes of the slice: x: 2, y: 2, z: 4, core: 2. Of those that a mesh axis runs over, the one named last changes fastest.
Arguments:
- vit_in: bfloat16 [576, 16, 1024], P(None, 'patch'), may hold values from -6 to 6
- conv_in: bfloat16 [1536, 16, 1024], P('chan', 'patch'), may hold values from -6 to 6
- ln_one: bfloat16 [1024], replicated, may hold values from 0.25 to 1.75
- w_qkv: bfloat16 [1024, 3, 1024], P(None, None, 'chan'), may hold values from -0.1875 to 0.1875
- w_attn: bfloat16 [1024, 1024], P(None, 'chan'), may hold values from -0.5 to 0.5
- ln_two: bfloat16 [1024], replicated, may hold values from 0.25 to 1.75
- w_up: bfloat16 [1024, 4096], P(None, 'chan'), may hold values from -0.1875 to 0.1875
- w_down: bfloat16 [1024, 4096], P(None, 'chan'), may hold values from -0.09375 to 0.09375
- conv_kernel: bfloat16 [1536, 49], replicated, may hold values from -0.875 to 0.875
- conv_gain: bfloat16 [1536], replicated, may hold values from 0.25 to 1.75
- conv_up: bfloat16 [1536, 6144], P(None, 'chan'), may hold values from -0.15625 to 0.15625
- conv_down: bfloat16 [1536, 6144], P(None, 'chan'), may hold values from -0.078125 to 0.078125
- layer_scale: bfloat16 [1536], replicated, may hold values from 0.29882812 to 1.5
- w_proj: bfloat16 [1536, 1024], replicated, may hold values from -0.15625 to 0.15625
- adapter_kernel: bfloat16 [1024, 9], replicated, may hold values from -2 to 2
- gate_in: bfloat16 [1024, 512], replicated, may hold values from -0.1875 to 0.1875
- gate_out: bfloat16 [512, 1024], replicated, may hold values from -0.25 to 0.25
- d_merged: bfloat16 [576, 16, 1024], P(None, 'patch'), may hold values from -6 to 6
- d_conv_out: bfloat16 [1536, 16, 1024], P('chan', 'patch'), may hold values from -6 to 6
Outputs:
- merged: bfloat16 [576, 16, 1024], P('chan', 'patch')
- conv_out: bfloat16 [1536, 16, 1024], P('chan', 'patch')
- g_vit_in: float32 [576, 16, 1024], P(None, 'patch')
- g_conv_in: float32 [1536, 16, 1024], P('chan', 'patch')
- g_ln_one: float32 [1024], P(('patch', 'chan'))
- g_qkv: float32 [1024, 3, 1024], P('patch', None, 'chan')
- g_attn: float32 [1024, 1024], P('patch', 'chan')
- g_ln_two: float32 [1024], P(('patch', 'chan'))
- g_up: float32 [1024, 4096], P('patch', 'chan')
- g_down: float32 [1024, 4096], P('patch', 'chan')
- g_conv_kernel: float32 [1536, 49], P(('patch', 'chan'))
- g_conv_gain: float32 [1536], P(('patch', 'chan'))
- g_conv_up: float32 [1536, 6144], P('patch', 'chan')
- g_conv_down: float32 [1536, 6144], P('patch', 'chan')
- g_layer_scale: float32 [1536], P(('patch', 'chan'))
- g_proj: float32 [1536, 1024], P(('patch', 'chan'))
- g_adapter_kernel: float32 [1024, 9], P(('patch', 'chan'))
- g_gate_in: float32 [1024, 512], P(('patch', 'chan'))
- g_gate_out: float32 [512, 1024], P(('patch', 'chan'))
The draws below stay inside these ranges and needn't reach their ends.
All inputs are finite; a program needn't handle non-finite values.
Results may differ from the reference program's by a relative error of at most 0.025.
Values may be sent and summed in bfloat16 or wider, within the bound.
A program may use at most 384 MiB of HBM per device.

```python
import math
import jax
import jax.numpy as jnp
from jax import lax

D = 1024
HEADS = 16
HEAD_DIM = 64
FF = 4096
CC = 1536
CF = 6144
GATE = 512
GRID = 24
MAP = 32
PATCHES = 576
CELLS = 1024
IMAGES = 16


def shard_levels(own_key, shape, cuts, smallest, high):
    gain, own = 1.0, jax.random.fold_in(own_key, 6)
    for position, blocks in cuts:
        steps = jnp.exp(jax.random.uniform(jax.random.fold_in(own, position), (blocks,), jnp.float32, smallest / len(cuts), high / len(cuts)))
        gain = gain * jnp.repeat(steps, shape[position] // blocks).reshape([-1 if axis == position else 1 for axis in range(len(shape))])
    return gain


def scatter_about(own_key, shape, deviation, most, split=(), kind=jnp.bfloat16):
    gain = shard_levels(own_key, shape, split, -0.22, 0.18) if split else 1.0
    entries = jax.random.normal(own_key, shape, jnp.float32) * deviation * gain
    return jnp.minimum(jnp.maximum(entries, -most), most).astype(kind)


def setup_inputs(seed: int = 0) -> dict:
    splits = jax.random.split(jax.random.key(seed), 20)
    return {
        "vit_in": scatter_about(splits[0], (PATCHES, IMAGES, D), 1.0, 6.0, ((1, 8),)),
        "conv_in": scatter_about(splits[1], (CC, IMAGES, CELLS), 1.0, 6.0, ((0, 4), (1, 8))),
        "ln_one": jnp.clip(1.0 + 0.15 * jax.random.normal(splits[2], (D,), jnp.float32), 0.25, 1.75).astype(jnp.bfloat16),
        "w_qkv": scatter_about(splits[3], (D, 3, D), D ** -0.5, 0.1875, ((2, 4),)),
        "w_attn": scatter_about(splits[4], (D, D), (D // 8) ** -0.5, 0.5, ((1, 4),)),
        "ln_two": jnp.clip(1.0 + 0.15 * jax.random.normal(splits[5], (D,), jnp.float32), 0.25, 1.75).astype(jnp.bfloat16),
        "w_up": scatter_about(splits[6], (D, FF), D ** -0.5, 0.1875, ((1, 4),)),
        "w_down": scatter_about(splits[7], (D, FF), FF ** -0.5, 0.09375, ((1, 4),)),
        "conv_kernel": scatter_about(splits[8], (CC, 49), 49 ** -0.5, 0.875),
        "conv_gain": jnp.clip(1.0 + 0.15 * jax.random.normal(splits[9], (CC,), jnp.float32), 0.25, 1.75).astype(jnp.bfloat16),
        "conv_up": scatter_about(splits[10], (CC, CF), CC ** -0.5, 0.15625, ((1, 4),)),
        "conv_down": scatter_about(splits[11], (CC, CF), CF ** -0.5, 0.078125, ((1, 4),)),
        "layer_scale": jnp.clip(jnp.exp(jax.random.uniform(splits[12], (CC,), jnp.float32, math.log(0.29882812), math.log(1.5))), 0.29882812, 1.5).astype(jnp.bfloat16),
        "w_proj": scatter_about(splits[13], (CC, D), CC ** -0.5, 0.15625),
        "adapter_kernel": scatter_about(splits[14], (D, 9), 9 ** -0.5, 2.0),
        "gate_in": scatter_about(splits[15], (D, GATE), D ** -0.5, 0.1875),
        "gate_out": scatter_about(splits[16], (GATE, D), GATE ** -0.5, 0.25),
        "d_merged": scatter_about(splits[17], (PATCHES, IMAGES, D), 1.0, 6.0, ((1, 8),)),
        "d_conv_out": scatter_about(splits[18], (CC, IMAGES, CELLS), 1.0, 6.0, ((0, 4), (1, 8))),
    }


vit_eps = 1e-05
conv_eps = 1e-06
highest = lax.Precision.HIGHEST

@jax.custom_vjp
def low(v):
    return lax.optimization_barrier(v.astype(jnp.bfloat16)).astype(jnp.float32)

@jax.custom_vjp
def low_back(v):
    return v

def low_keep(v):
    return (low(v), None)

def low_pass(kept, grad):
    return (grad,)

def back_keep(v):
    return (v, None)

def back_low(kept, grad):
    return (low(grad),)
low.defvjp(low_keep, low_pass)
low_back.defvjp(back_keep, back_low)

def gelu_exact(values):
    return jax.nn.gelu(values, approximate=False)

def pool_table():
    out_index = jnp.arange(GRID)
    first_row = out_index * MAP // GRID
    last_row = ((out_index + 1) * MAP + GRID - 1) // GRID
    source_index = jnp.arange(MAP)
    inside_rows = (source_index[None, :] >= first_row[:, None]) & (source_index[None, :] < last_row[:, None])
    single = jnp.where(inside_rows, 1.0, 0.0).astype(jnp.float32) / (last_row - first_row)[:, None].astype(jnp.float32)
    table = single[:, None, :, None] * single[None, :, None, :]
    return table.reshape(GRID * GRID, MAP * MAP)

def depthwise_seven(source_field, kernel):
    cell_count = source_field.shape[-1]
    margin = 3 * MAP + 3
    padded = jnp.pad(source_field, ((0, 0), (0, 0), (margin, margin)))
    column = jnp.arange(cell_count) % MAP
    running = jnp.zeros_like(source_field)
    for row_step in range(7):
        for col_step in range(7):
            offset = row_step * MAP + col_step
            shifted = padded[:, :, offset:offset + cell_count]
            inside_mask = ((column + col_step - 3 >= 0) & (column + col_step - 3 < MAP)).astype(source_field.dtype)
            running = running + kernel[:, row_step * 7 + col_step][:, None, None] * (shifted * inside_mask)
    return running

def depthwise_three(extended, kernel):
    out_count = (extended.shape[0] // GRID - 2) * GRID
    padded = jnp.pad(extended, ((1, 1), (0, 0), (0, 0)))
    column = jnp.arange(out_count) % GRID
    running = jnp.zeros((out_count,) + extended.shape[1:], extended.dtype)
    for row_step in range(3):
        for col_step in range(3):
            offset = row_step * GRID + col_step
            shifted = padded[offset:offset + out_count]
            inside_mask = ((column + col_step - 1 >= 0) & (column + col_step - 1 < GRID)).astype(extended.dtype)
            running = running + kernel[:, row_step * 3 + col_step] * (shifted * inside_mask[:, None, None])
    return running

def norm_last(values, gain_vec, epsilon):
    center = values - lax.optimization_barrier(jnp.mean(values, axis=-1, keepdims=True))
    spread = lax.optimization_barrier(jnp.mean(center * center, axis=-1, keepdims=True))
    return center * lax.rsqrt(spread + epsilon) * gain_vec

def norm_first(values, gain_vec, epsilon):
    center = values - lax.optimization_barrier(jnp.mean(values, axis=0, keepdims=True))
    spread = lax.optimization_barrier(jnp.mean(center * center, axis=0, keepdims=True))
    return center * lax.rsqrt(spread + epsilon) * gain_vec[:, None, None]

def forward(vit_x, conv_x, ln_one, w_qkv, w_attn, ln_two, w_up, w_down, conv_kernel, conv_gain, conv_up, conv_down, layer_scale, w_proj, adapter_kernel, gate_in, gate_out):
    patches = vit_x.shape[0]
    images = vit_x.shape[1]
    normed_one = low(norm_last(vit_x, ln_one, vit_eps))
    projected = low(low_back(jnp.einsum('pid,dtc->pitc', normed_one, w_qkv, precision=highest)))
    query_rows = projected[:, :, 0].reshape(patches, images, HEADS, HEAD_DIM)
    key_rows = projected[:, :, 1].reshape(patches, images, HEADS, HEAD_DIM)
    value_rows = projected[:, :, 2].reshape(patches, images, HEADS, HEAD_DIM)
    scores = low_back(jnp.einsum('pihe,qihe->ihpq', query_rows, key_rows, precision=highest) * (1.0 / math.sqrt(HEAD_DIM)))
    attention_weights = low(jax.nn.softmax(scores, axis=-1))
    mixed = low(low_back(jnp.einsum('ihpq,qihe->pihe', attention_weights, value_rows, precision=highest).reshape(patches, images, D)))
    attended = low_back(jnp.einsum('pie,de->pid', mixed, w_attn, precision=highest))
    middle = vit_x + attended
    normed_two = low(norm_last(middle, ln_two, vit_eps))
    hidden_pre = low_back(jnp.einsum('pid,df->pif', normed_two, w_up, precision=highest))
    hidden_act = low(gelu_exact(hidden_pre))
    branch = low_back(jnp.einsum('pif,df->pid', hidden_act, w_down, precision=highest))
    vit_out = middle + branch
    mapped = low(depthwise_seven(conv_x, conv_kernel))
    conv_norm = low(norm_first(mapped, conv_gain, conv_eps))
    conv_pre = low_back(jnp.einsum('cf,cip->fip', conv_up, conv_norm, precision=highest))
    conv_act = low(gelu_exact(conv_pre))
    conv_branch = low_back(jnp.einsum('cf,fip->cip', conv_down, conv_act, precision=highest))
    conv_result = low(conv_x + layer_scale[:, None, None] * conv_branch)
    pooled = low(low_back(jnp.einsum('cip,qp->ciq', conv_result, pool_table(), precision=highest)))
    adapted = low(low_back(jnp.einsum('ciq,cd->qid', pooled, w_proj, precision=highest)))
    border_rows = jnp.zeros((GRID,) + adapted.shape[1:], adapted.dtype)
    smoothed = depthwise_three(jnp.concatenate([border_rows, adapted, border_rows], axis=0), adapter_kernel)
    gate_input = low(smoothed)
    gate_pre = low_back(jnp.einsum('pid,dg->pig', gate_input, gate_in, precision=highest))
    gate_act = low(gelu_exact(gate_pre))
    gate_logit = low_back(jnp.einsum('pig,gd->pid', gate_act, gate_out, precision=highest))
    merged = vit_out + jnp.tanh(gate_logit) * smoothed
    return (merged, conv_result)

def reference(vit_in, conv_in, ln_one, w_qkv, w_attn, ln_two, w_up, w_down, conv_kernel, conv_gain, conv_up, conv_down, layer_scale, w_proj, adapter_kernel, gate_in, gate_out, d_merged, d_conv_out):
    inputs = (vit_in, conv_in, ln_one, w_qkv, w_attn, ln_two, w_up, w_down, conv_kernel, conv_gain, conv_up, conv_down, layer_scale, w_proj, adapter_kernel, gate_in, gate_out)
    floats = [entry.astype(jnp.float32) for entry in inputs]
    outputs, pullback = jax.vjp(forward, *floats)
    grads = pullback((d_merged.astype(jnp.float32), d_conv_out.astype(jnp.float32)))
    return (outputs[0].astype(jnp.bfloat16), outputs[1].astype(jnp.bfloat16), grads[0], grads[1], grads[2], grads[3], grads[4], grads[5], grads[6], grads[7], grads[8], grads[9], grads[10], grads[11], grads[12], grads[13], grads[14], grads[15], grads[16])
```

```python
import math

import jax
import jax.numpy as jnp
from jax import lax
from jax.experimental import pallas as pl
from jax.experimental.pallas import tpu as pltpu
from jax.sharding import PartitionSpec as P

HEAD_DIM = 64
GRID = 24
MAP = 32
TAPS = 7
GROUP = 32
WIDE = 256

vit_eps = 1e-05
conv_eps = 1e-06
f32 = jnp.float32
bf16 = jnp.bfloat16
MIB = 2**20


def bit_count(axis):
    return lax.axis_size(axis).bit_length() - 1


def swap(values, axis, bit):
    count = lax.axis_size(axis)
    return lax.ppermute(values, axis, [(i, i ^ (1 << bit)) for i in range(count)])


def halve(values, axis, bit, dim):
    shape = values.shape
    split = values.reshape(shape[:dim] + (shape[dim] // 2, 2) + shape[dim + 1 :])
    mine = (lax.axis_index(axis) >> bit) & 1
    keep = lax.dynamic_index_in_dim(split, mine, dim + 1, keepdims=False)
    send = lax.dynamic_index_in_dim(split, 1 - mine, dim + 1, keepdims=False)
    return keep.astype(f32) + swap(send.astype(bf16), axis, bit).astype(f32)


def sum_scatter(values, axis, dim=0):
    for bit in range(bit_count(axis)):
        values = halve(values, axis, bit, dim)
    return lax.squeeze(values, (dim,))


def gather(block, axis, dim=0):
    count = lax.axis_size(axis)
    me = lax.axis_index(axis)
    parts = {0: block}
    for bit in reversed(range(bit_count(axis))):
        for offset in list(parts):
            parts[offset | (1 << bit)] = swap(parts[offset], axis, bit)
    shape = block.shape[:dim] + (count,) + block.shape[dim:]
    whole = jnp.zeros(shape, block.dtype)
    for offset in sorted(parts):
        whole = lax.dynamic_update_slice_in_dim(
            whole, lax.expand_dims(parts[offset], (dim,)), me ^ offset, dim
        )
    return whole


def sum_all(values, axis):
    for bit in range(bit_count(axis)):
        values = values + swap(values, axis, bit)
    return values


def lane_shift(values, step):
    count = values.shape[-1]
    step = step % count
    return values if step == 0 else pltpu.roll(values, count - step, 1)


def fill_masks(col_ref, row_ref):
    lanes = col_ref.shape[-1]
    place = lax.broadcasted_iota(jnp.int32, (GROUP, lanes), 1)
    col = place % MAP
    row = (place // MAP) % MAP
    for tap in range(TAPS):
        step = tap - TAPS // 2
        for ref, spot in ((col_ref, col), (row_ref, row)):
            ref[tap] = ((spot + step >= 0) & (spot + step < MAP)).astype(f32).astype(bf16)


def tap_weights(kernel):
    tap = jnp.arange(TAPS * TAPS)[:, None]
    spot = jnp.arange(TAPS * WIDE)[None, :]
    pick = (tap == (spot // WIDE) * TAPS + (spot % WIDE) // GROUP) & (spot % WIDE < TAPS * GROUP)
    own = (jnp.arange(kernel.shape[0])[:, None] % GROUP) == (spot % GROUP)
    spread = jnp.dot(kernel, pick.astype(bf16), preferred_element_type=f32)
    return jnp.where(own, spread, 0.0).astype(bf16)


def stacked_weights(k_ref):
    blocks = [k_ref[:, r * WIDE : r * WIDE + TAPS * GROUP] for r in range(TAPS)]
    return jnp.concatenate(blocks, axis=0)


def depthwise_kernel(x_ref, k_ref, o_ref, s_ref, col_ref, row_ref):
    @pl.when(pl.program_id(0) == 0)
    def _():
        fill_masks(col_ref, row_ref)

    x = x_ref[...]
    lanes = x.shape[1]
    for tap in range(TAPS):
        step = tap - TAPS // 2
        moved = lane_shift(x, step)
        s_ref[tap] = moved if step == 0 else moved * col_ref[tap]
    rows = jnp.dot(
        stacked_weights(k_ref), s_ref[...].reshape(TAPS * GROUP, lanes), preferred_element_type=f32
    )
    total = None
    for tap in range(TAPS):
        step = tap - TAPS // 2
        part = rows[tap * GROUP : (tap + 1) * GROUP]
        if step != 0:
            part = (lane_shift(part.astype(bf16), MAP * step) * row_ref[tap]).astype(f32)
        total = part if total is None else total + part
    o_ref[...] = total.astype(o_ref.dtype)


def depthwise(x, weights):
    channels, lanes = x.shape
    return pl.pallas_call(
        depthwise_kernel,
        grid=(channels // GROUP,),
        in_specs=[
            pl.BlockSpec((GROUP, lanes), lambda i: (i, 0)),
            pl.BlockSpec((GROUP, TAPS * WIDE), lambda i: (i, 0)),
        ],
        out_specs=pl.BlockSpec((GROUP, lanes), lambda i: (i, 0)),
        out_shape=jax.ShapeDtypeStruct((channels, lanes), bf16),
        scratch_shapes=[pltpu.VMEM((TAPS, GROUP, lanes), bf16)] * 3,
        compiler_params=pltpu.CompilerParams(vmem_limit_bytes=32 * MIB),
        cost_estimate=pl.CostEstimate(
            flops=2 * 49 * GROUP * channels * lanes, bytes_accessed=4 * channels * lanes, transcendentals=0
        ),
    )(x, weights)


def depthwise_back_kernel(
    d_ref, x_ref, k_ref, add_ref, gx_ref, gk_ref, t_ref, s_ref, col_ref, row_ref
):
    @pl.when(pl.program_id(0) == 0)
    def _():
        fill_masks(col_ref, row_ref)

    x = x_ref[...]
    lanes = x.shape[1]
    d = d_ref[...].astype(bf16)
    last = TAPS - 1
    for tap in range(TAPS):
        step = tap - TAPS // 2
        moved = lane_shift(d, -step)
        t_ref[tap] = moved if step == 0 else moved * col_ref[last - tap]
        moved = lane_shift(x, MAP * step)
        s_ref[tap] = moved if step == 0 else moved * row_ref[tap]
    t = t_ref[...].reshape(TAPS * GROUP, lanes)
    rows = jnp.dot(stacked_weights(k_ref), t, preferred_element_type=f32)
    total = add_ref[...]
    for tap in range(TAPS):
        step = tap - TAPS // 2
        part = rows[tap * GROUP : (tap + 1) * GROUP]
        if step != 0:
            part = (lane_shift(part.astype(bf16), -MAP * step) * row_ref[last - tap]).astype(f32)
        total = total + part
    gx_ref[...] = total
    pairs = lax.dot_general(
        t, s_ref[...].reshape(TAPS * GROUP, lanes), (((1,), (1,)), ((), ())), preferred_element_type=f32
    )
    side = TAPS * GROUP
    first = lax.broadcasted_iota(jnp.int32, (side, side), 0)
    second = lax.broadcasted_iota(jnp.int32, (side, side), 1)
    own = jnp.where(first % GROUP == second % GROUP, pairs, 0.0)
    source = lax.broadcasted_iota(jnp.int32, (side, 128), 0)
    target = lax.broadcasted_iota(jnp.int32, (side, 128), 1)
    pick = (source // GROUP == target).astype(f32).astype(bf16)
    high = own.astype(bf16)
    low = (own - high.astype(f32)).astype(bf16)
    gk_ref[0] = jnp.dot(high, pick, preferred_element_type=f32) + jnp.dot(
        low, pick, preferred_element_type=f32
    )


def depthwise_back(d, x, weights, add):
    channels, lanes = x.shape
    groups = channels // GROUP
    rows = pl.BlockSpec((GROUP, lanes), lambda i: (i, 0))
    gx, gk = pl.pallas_call(
        depthwise_back_kernel,
        grid=(groups,),
        in_specs=[rows, rows, pl.BlockSpec((GROUP, TAPS * WIDE), lambda i: (i, 0)), rows],
        out_specs=[rows, pl.BlockSpec((1, TAPS * GROUP, 128), lambda i: (i, 0, 0))],
        out_shape=[
            jax.ShapeDtypeStruct((channels, lanes), f32),
            jax.ShapeDtypeStruct((groups, TAPS * GROUP, 128), f32),
        ],
        scratch_shapes=[pltpu.VMEM((TAPS, GROUP, lanes), bf16)] * 4,
        compiler_params=pltpu.CompilerParams(vmem_limit_bytes=32 * MIB),
        cost_estimate=pl.CostEstimate(
            flops=4 * 49 * GROUP * channels * lanes, bytes_accessed=14 * channels * lanes, transcendentals=0
        ),
    )(d, x, weights, add)
    gk = gk[:, :, :TAPS].reshape(groups, TAPS, GROUP, TAPS).transpose(0, 2, 3, 1)
    return gx, gk.reshape(channels, TAPS * TAPS)


def gelu_both(u):
    share = 0.5 * (1.0 + lax.erf(u * (1.0 / math.sqrt(2.0))))
    return u * share, share + u * jnp.exp(-0.5 * u * u) * (1.0 / math.sqrt(2.0 * math.pi))


def block_of(size, most, unit):
    best = unit
    for candidate in range(unit, most + 1, unit):
        if size % candidate == 0:
            best = candidate
    return best if size % best == 0 else size


def gelu_matmul_kernel(a_ref, w_ref, h_ref, s_ref):
    u = jnp.dot(a_ref[...], w_ref[...], preferred_element_type=f32)
    act, slope = gelu_both(u)
    h_ref[...] = act.astype(bf16)
    s_ref[...] = slope.astype(bf16)


def gelu_matmul(a, w):
    rows, depth = a.shape
    columns = w.shape[1]
    bm = block_of(rows, 384, 16)
    bn = block_of(columns, 512, 128)
    out = pl.BlockSpec((bm, bn), lambda j, i: (i, j))
    return pl.pallas_call(
        gelu_matmul_kernel,
        grid=(columns // bn, rows // bm),
        in_specs=[
            pl.BlockSpec((bm, depth), lambda j, i: (i, 0)),
            pl.BlockSpec((depth, bn), lambda j, i: (0, j)),
        ],
        out_specs=[out, out],
        out_shape=[jax.ShapeDtypeStruct((rows, columns), bf16)] * 2,
        compiler_params=pltpu.CompilerParams(vmem_limit_bytes=32 * MIB),
        cost_estimate=pl.CostEstimate(
            flops=2 * rows * depth * columns,
            bytes_accessed=2 * (rows * depth + depth * columns + 2 * rows * columns),
            transcendentals=2 * rows * columns,
        ),
    )(a, w)


def pool_table():
    out_index = jnp.arange(GRID)
    first_row = out_index * MAP // GRID
    last_row = ((out_index + 1) * MAP + GRID - 1) // GRID
    source_index = jnp.arange(MAP)
    inside = (source_index[None, :] >= first_row[:, None]) & (
        source_index[None, :] < last_row[:, None]
    )
    single = jnp.where(inside, 1.0, 0.0).astype(f32) / (last_row - first_row)[:, None].astype(f32)
    table = single[:, None, :, None] * single[None, :, None, :]
    return table.reshape(GRID * GRID, MAP * MAP)


def shifted_rows(field, count, step_row, step_col):
    offset = 1 + (step_row + 1) * GRID + step_col
    part = lax.slice_in_dim(field, offset, offset + count, axis=1)
    column = jnp.arange(count) % GRID
    inside = (column + step_col >= 0) & (column + step_col < GRID)
    return jnp.where(inside[None, :, None], part, 0.0)


def standardize(values, axis, epsilon):
    center = values - jnp.mean(values, axis=axis, keepdims=True)
    inverse = lax.rsqrt(jnp.mean(center * center, axis=axis, keepdims=True) + epsilon)
    return center * inverse, inverse


def norm_back(grad, gain, unit, inverse, axis):
    scaled = grad * gain
    return inverse * (
        scaled
        - jnp.mean(scaled, axis=axis, keepdims=True)
        - unit * jnp.mean(scaled * unit, axis=axis, keepdims=True)
    )


def dot(spec, a, b):
    return jnp.einsum(spec, a, b, preferred_element_type=f32)


def body(
    vit_in,
    conv_in,
    ln_one,
    w_qkv,
    w_attn,
    ln_two,
    w_up,
    w_down,
    conv_kernel,
    conv_gain,
    conv_up,
    conv_down,
    layer_scale,
    w_proj,
    adapter_kernel,
    gate_in,
    gate_out,
    d_merged,
    d_conv_out,
):
    chans = lax.axis_size("chan")
    patchs = lax.axis_size("patch")
    me = lax.axis_index("chan")
    tokens, images, width = vit_in.shape
    band = tokens // chans
    own_channels, _, cells = conv_in.shape
    channels = own_channels * chans
    lanes = images * cells
    scale = 1.0 / math.sqrt(HEAD_DIM)

    def own_rows(values, size):
        return lax.dynamic_slice_in_dim(values, me * size, size, 0)

    def bands(values):
        return values.reshape(images, chans, band, -1)

    def own_band(values):
        return lax.dynamic_index_in_dim(bands(values), me, 1, keepdims=False)

    def whole_rows(values):
        return values.reshape(images, tokens, -1)

    conv_flat = conv_in.reshape(own_channels, lanes)
    weights = tap_weights(own_rows(conv_kernel, own_channels))
    mapped = depthwise(conv_flat, weights)
    mapped_all = gather(mapped, "chan").reshape(channels, lanes)

    vit_x = vit_in.swapaxes(0, 1)
    gain_one = ln_one.astype(f32)
    gain_two = ln_two.astype(f32)
    unit_one, inverse_one = standardize(vit_x.astype(f32), -1, vit_eps)
    normed_one = (unit_one * gain_one).astype(bf16)
    heads = w_qkv.shape[2] // HEAD_DIM
    query, key, value = (
        dot("ipd,dc->ipc", normed_one, w_qkv[:, t]).astype(bf16).reshape(images, tokens, heads, HEAD_DIM)
        for t in range(3)
    )
    scores = dot("iphe,iqhe->ihpq", query, key) * scale
    log_total = jax.nn.logsumexp(scores, axis=-1, keepdims=True)
    weights_soft = jnp.exp(scores - log_total)
    mixed = dot("ihpq,iqhe->iphe", weights_soft.astype(bf16), value).reshape(images, tokens, -1)
    mixed = mixed.astype(bf16)
    attended = sum_scatter(bands(dot("ipe,de->ipd", mixed, w_attn).astype(bf16)), "chan", 1)
    vit_band = own_band(vit_x).astype(f32)
    middle = vit_band + attended
    unit_two, inverse_two = standardize(middle, -1, vit_eps)
    normed_two = whole_rows(gather((unit_two * gain_two).astype(bf16), "chan", 1))

    conv_unit_all, conv_inverse = standardize(mapped_all.astype(f32), 0, conv_eps)
    conv_norm = (conv_unit_all * conv_gain.astype(f32)[:, None]).astype(bf16)
    conv_act, conv_slope = gelu_matmul(conv_up.T, conv_norm)
    conv_branch = sum_scatter(
        dot("cf,fp->cp", conv_down, conv_act).astype(bf16).reshape(chans, own_channels, lanes), "chan"
    )
    own_scale = own_rows(layer_scale, own_channels).astype(f32)[:, None]
    conv_result = (conv_flat.astype(f32) + own_scale * conv_branch).astype(bf16)

    flat_two = normed_two.reshape(images * tokens, width)
    act, slope = gelu_matmul(flat_two, w_up)
    branch = sum_scatter(
        bands(dot("rf,df->rd", act, w_down).astype(bf16)), "chan", 1
    )
    vit_out = middle + branch
    d_rows = d_merged.swapaxes(0, 1)
    d_flat = d_rows.reshape(images * tokens, width)
    d_band = own_band(d_rows).astype(f32)
    g_down = dot("rd,rf->df", d_flat, act).astype(bf16)
    d_pre = (dot("rd,df->rf", d_flat, w_down) * slope.astype(f32)).astype(bf16)
    g_up = dot("rd,rf->df", flat_two, d_pre).astype(bf16)
    d_normed_two = sum_scatter(bands(dot("rf,df->rd", d_pre, w_up).astype(bf16)), "chan", 1)
    d_middle = d_band + norm_back(d_normed_two, gain_two, unit_two, inverse_two, -1)
    g_ln_two = jnp.sum(d_normed_two * unit_two, axis=(0, 1))

    table = pool_table().astype(bf16)
    result_maps = conv_result.reshape(own_channels, images, cells)
    pooled = dot("cip,qp->ciq", result_maps, table).astype(bf16)
    pooled_rows = dot("qp,cip->iqc", table, result_maps).astype(bf16)
    reach = band + 2 * GRID
    padded_rows = jnp.pad(pooled_rows, ((0, 0), (GRID, GRID), (0, 0)))
    adapted = jnp.zeros((images, reach, width), f32)
    for offset in range(chans):
        other = me ^ offset
        piece = lax.dynamic_slice_in_dim(padded_rows, other * band, reach, 1)
        if offset:
            piece = lax.ppermute(piece, "chan", [(i, i ^ offset) for i in range(chans)])
        adapted = adapted + dot(
            "iqc,cd->iqd", piece, lax.dynamic_slice_in_dim(w_proj, other * own_channels, own_channels, 0)
        )
    adapted = adapted.astype(bf16)
    kernel_three = adapter_kernel.astype(f32)
    spare = jnp.pad(adapted, ((0, 0), (1, 1), (0, 0))).astype(f32)
    taps = [(r - 1, c - 1) for r in range(3) for c in range(3)]
    smoothed = sum(
        kernel_three[:, t] * shifted_rows(spare, band, *tap) for t, tap in enumerate(taps)
    )
    gate_rows = smoothed.astype(bf16).reshape(images * band, width)
    gate_act, gate_slope = gelu_matmul(gate_rows, gate_in)
    gate_value = jnp.tanh(dot("rg,gd->rd", gate_act, gate_out).reshape(images, band, width))
    merged = (vit_out + gate_value * smoothed).astype(bf16)
    d_logit = (d_band * smoothed * (1.0 - gate_value * gate_value)).astype(bf16)
    d_logit = d_logit.reshape(images * band, width)
    d_gate = (dot("rd,gd->rg", d_logit, gate_out) * gate_slope.astype(f32)).astype(bf16)
    d_smooth = d_band * gate_value + dot("rg,dg->rd", d_gate, gate_in).reshape(images, band, width)
    g_gate_out = dot("rg,rd->gd", gate_act, d_logit).astype(bf16)
    g_gate_in = dot("rd,rg->dg", gate_rows, d_gate).astype(bf16)
    g_adapter = jnp.stack(
        [jnp.sum(d_smooth * shifted_rows(spare, band, *tap), axis=(0, 1)) for tap in taps], axis=1
    )
    d_smooth_all = whole_rows(gather(d_smooth.astype(bf16), "chan", 1))
    d_spare = jnp.pad(d_smooth_all, ((0, 0), (GRID + 1, GRID + 1), (0, 0))).astype(f32)
    d_adapted = sum(
        kernel_three[:, t] * shifted_rows(d_spare, tokens, -tap[0], -tap[1])
        for t, tap in enumerate(taps)
    ).astype(bf16)
    g_proj = dot("ciq,iqd->cd", pooled, d_adapted).astype(bf16)
    d_pooled = dot("cd,iqd->ciq", own_rows(w_proj, own_channels), d_adapted).astype(bf16)
    d_result = d_conv_out.reshape(own_channels, lanes).astype(f32) + dot(
        "ciq,qp->cip", d_pooled, table
    ).reshape(own_channels, lanes)

    g_scale = jnp.sum(d_result * conv_branch, axis=1)
    d_branch = gather((own_scale * d_result).astype(bf16), "chan").reshape(channels, lanes)

    d_attended = whole_rows(gather(d_middle.astype(bf16), "chan", 1))
    g_attn = dot("ipd,ipe->de", d_attended, mixed).astype(bf16)
    d_mixed = dot("ipd,de->ipe", d_attended, w_attn).astype(bf16)
    d_mixed = d_mixed.reshape(images, tokens, heads, HEAD_DIM)
    soft_again = jnp.exp(dot("iphe,iqhe->ihpq", query, key) * scale - log_total)
    d_soft = dot("iphe,iqhe->ihpq", d_mixed, value)
    d_scores = (soft_again * (d_soft - jnp.sum(d_soft * soft_again, axis=-1, keepdims=True))).astype(bf16)
    d_query = (dot("ihpq,iqhe->iphe", d_scores, key) * scale).astype(bf16)
    d_key = (dot("ihpq,iphe->iqhe", d_scores, query) * scale).astype(bf16)
    d_value = dot("ihpq,iphe->iqhe", soft_again.astype(bf16), d_mixed).astype(bf16)
    d_parts = [v.reshape(images, tokens, -1) for v in (d_query, d_key, d_value)]
    g_qkv = jnp.concatenate(
        [dot("ipd,ipc->dc", normed_one, v).astype(bf16) for v in d_parts], axis=1
    )
    d_normed_one = sum(dot("ipc,dc->ipd", v, w_qkv[:, t]) for t, v in enumerate(d_parts))
    d_normed_one = sum_scatter(bands(d_normed_one.astype(bf16)), "chan", 1)
    unit_band, inverse_band = standardize(vit_band, -1, vit_eps)
    g_vit = d_middle + norm_back(d_normed_one, gain_one, unit_band, inverse_band, -1)
    g_vit_in = whole_rows(gather(g_vit.astype(bf16), "chan", 1)).swapaxes(0, 1).astype(f32)
    g_ln_one = jnp.sum(d_normed_one * unit_band, axis=(0, 1))

    d_pre_conv = (dot("cf,cp->fp", conv_down, d_branch) * conv_slope.astype(f32)).astype(bf16)
    d_norm = sum_scatter(
        dot("cf,fp->cp", conv_up, d_pre_conv).astype(bf16).reshape(chans, own_channels, lanes), "chan"
    )
    g_conv_down = dot("cp,fp->cf", d_branch, conv_act).astype(bf16)
    g_conv_up = dot("cp,fp->cf", conv_norm, d_pre_conv).astype(bf16)
    own_unit = own_rows(conv_unit_all, own_channels)
    scaled = d_norm * own_rows(conv_gain, own_channels).astype(f32)[:, None]
    sums = jnp.stack([jnp.sum(scaled, axis=0), jnp.sum(scaled * own_unit, axis=0)])
    sums = sum_all(sums, "chan") * (1.0 / channels)
    d_mapped = conv_inverse * (scaled - sums[0] - own_unit * sums[1])
    g_gain = jnp.sum(d_norm * own_unit, axis=1)
    g_conv_flat, g_kernel = depthwise_back(d_mapped, conv_flat, weights, d_result)

    def over_patch(values):
        return sum_scatter(values.reshape(patchs, values.shape[0] // patchs, -1), "patch")

    vit_grads = over_patch(jnp.concatenate([g_up, g_down], axis=1))
    att_grads = over_patch(jnp.concatenate([g_qkv, g_attn], axis=1))
    g_conv_down = over_patch(g_conv_down)
    g_conv_up = over_patch(g_conv_up)

    own_grads = jnp.concatenate(
        [g_proj.astype(f32), g_kernel, g_gain[:, None], g_scale[:, None]], axis=1
    )
    own_grads = jnp.pad(own_grads, ((0, 0), (0, -own_grads.shape[1] % 128)))
    own_grads = over_patch(own_grads)
    places = [
        (p * chans + c, c * patchs + p) for p in range(patchs) for c in range(chans)
    ]
    own_grads = lax.ppermute(own_grads, ("patch", "chan"), places)

    everywhere = patchs * chans

    def spread(values):
        return values.reshape(patchs, chans, -1)

    shares = [g_ln_one, g_ln_two, g_adapter, g_gate_in.astype(f32), g_gate_out.astype(f32)]
    sizes = [v.size // everywhere for v in shares]
    flat = jnp.concatenate([spread(v) for v in shares], axis=2)
    flat = jnp.pad(flat, ((0, 0), (0, 0), (0, -flat.shape[2] % 1024)))
    flat = sum_scatter(sum_scatter(flat, "chan", 1), "patch")
    ends = [sum(sizes[: k + 1]) for k in range(len(sizes))]
    pieces = [
        flat[end - size : end].reshape((v.shape[0] // everywhere,) + v.shape[1:])
        for end, size, v in zip(ends, sizes, shares)
    ]
    ff = w_up.shape[1]
    qkv_width = g_qkv.shape[1]
    return (
        merged.swapaxes(0, 1),
        conv_result.reshape(conv_in.shape),
        g_vit_in,
        g_conv_flat.reshape(conv_in.shape),
        pieces[0],
        att_grads[:, :qkv_width].reshape(-1, 3, w_qkv.shape[2]),
        att_grads[:, qkv_width:],
        pieces[1],
        vit_grads[:, :ff],
        vit_grads[:, ff:],
        own_grads[:, width : width + 49],
        own_grads[:, width + 49],
        g_conv_up,
        g_conv_down,
        own_grads[:, width + 50],
        own_grads[:, :width],
        pieces[2],
        pieces[3],
        pieces[4],
    )


def solution(mesh):
    in_specs = (
        P(None, "patch", None),
        P("chan", "patch", None),
        P(),
        P(None, None, "chan"),
        P(None, "chan"),
        P(),
        P(None, "chan"),
        P(None, "chan"),
        P(),
        P(),
        P(None, "chan"),
        P(None, "chan"),
        P(),
        P(),
        P(),
        P(),
        P(),
        P(None, "patch", None),
        P("chan", "patch", None),
    )
    out_specs = (
        P("chan", "patch", None),
        P("chan", "patch", None),
        P(None, "patch", None),
        P("chan", "patch", None),
        P(("patch", "chan")),
        P("patch", None, "chan"),
        P("patch", "chan"),
        P(("patch", "chan")),
        P("patch", "chan"),
        P("patch", "chan"),
        P(("patch", "chan"), None),
        P(("patch", "chan")),
        P("patch", "chan"),
        P("patch", "chan"),
        P(("patch", "chan")),
        P(("patch", "chan"), None),
        P(("patch", "chan"), None),
        P(("patch", "chan"), None),
        P(("patch", "chan"), None),
    )
    return jax.shard_map(body, mesh=mesh, in_specs=in_specs, out_specs=out_specs, check_vma=False)
```

```python
import math

import jax
import jax.numpy as jnp
import numpy as np
from jax import lax
from jax.experimental import pallas as pl
from jax.experimental.pallas import tpu as pltpu
from jax.sharding import PartitionSpec as P

HEAD_DIM = 64
GRID = 24
MAP = 32
TAPS = 7
GROUP = 32
WIDE = 256

vit_eps = 1e-05
conv_eps = 1e-06
f32 = jnp.float32
bf16 = jnp.bfloat16
MIB = 2**20


def bit_count(size):
    return size.bit_length() - 1


def reverse_bits(value, bits):
    return sum(((value >> k) & 1) << (bits - 1 - k) for k in range(bits))


def swap(values, axis, bit):
    count = lax.axis_size(axis)
    return lax.ppermute(values, axis, [(i, i ^ (1 << bit)) for i in range(count)])


def sum_rest(keep, send, axis):
    total = (keep, swap(send, axis, 0))
    for bit in range(1, bit_count(lax.axis_size(axis))):
        mine = (lax.axis_index(axis) >> bit) & 1
        half = total[0].shape[0] // 2
        keep, send = (
            sum(lax.dynamic_slice_in_dim(v, which * half, half, 0).astype(f32) for v in total)
            for which in (mine, 1 - mine)
        )
        total = (keep.astype(bf16), swap(send.astype(bf16), axis, bit))
    return tuple(v[0] for v in total)


def sum_scatter(values, axis):
    for bit in range(bit_count(lax.axis_size(axis))):
        mine = (lax.axis_index(axis) >> bit) & 1
        half = values.shape[0] // 2
        keep = lax.dynamic_slice_in_dim(values, mine * half, half, 0)
        send = lax.dynamic_slice_in_dim(values, (1 - mine) * half, half, 0)
        values = keep + swap(send, axis, bit)
    return values[0]


def halving_order(values, axis):
    count = lax.axis_size(axis)
    bits = bit_count(count)
    return jnp.stack([values[reverse_bits(j, bits)] for j in range(count)])


def gather_parts(block, axis):
    parts = {0: block}
    for bit in reversed(range(bit_count(lax.axis_size(axis)))):
        for offset in list(parts):
            parts[offset | (1 << bit)] = swap(parts[offset], axis, bit)
    return [parts[offset] for offset in sorted(parts)]


def sum_all(values, axis):
    for bit in range(bit_count(lax.axis_size(axis))):
        values = values + swap(values, axis, bit)
    return values


def lane_shift(values, step):
    count = values.shape[-1]
    step = step % count
    return values if step == 0 else pltpu.roll(values, count - step, 1)


def fill_masks(col_ref, row_ref):
    lanes = col_ref.shape[-1]
    place = lax.broadcasted_iota(jnp.int32, (GROUP, lanes), 1)
    col = place % MAP
    row = (place // MAP) % MAP
    for tap in range(TAPS):
        step = tap - TAPS // 2
        for ref, spot in ((col_ref, col), (row_ref, row)):
            ref[tap] = ((spot + step >= 0) & (spot + step < MAP)).astype(f32).astype(bf16)


def tap_weights(kernel):
    tap = np.arange(TAPS * TAPS)[:, None]
    spot = np.arange(TAPS * WIDE)[None, :]
    pick = (tap == (spot // WIDE) * TAPS + (spot % WIDE) // GROUP) & (spot % WIDE < TAPS * GROUP)
    own = (jnp.arange(kernel.shape[0])[:, None] % GROUP) == jnp.asarray(spot % GROUP)
    spread = jnp.dot(kernel, jnp.asarray(pick.astype(bf16)), preferred_element_type=f32)
    return jnp.where(own, spread, 0.0).astype(bf16)


def stacked_weights(k_ref):
    blocks = [k_ref[:, r * WIDE : r * WIDE + TAPS * GROUP] for r in range(TAPS)]
    return jnp.concatenate(blocks, axis=0)


def depthwise_kernel(x_ref, k_ref, o_ref, s_ref, col_ref, row_ref):
    @pl.when(pl.program_id(0) == 0)
    def _():
        fill_masks(col_ref, row_ref)

    x = x_ref[...]
    lanes = x.shape[1]
    for tap in range(TAPS):
        step = tap - TAPS // 2
        moved = lane_shift(x, step)
        s_ref[tap] = moved if step == 0 else moved * col_ref[tap]
    rows = jnp.dot(
        stacked_weights(k_ref), s_ref[...].reshape(TAPS * GROUP, lanes), preferred_element_type=f32
    )
    total = None
    for tap in range(TAPS):
        step = tap - TAPS // 2
        part = rows[tap * GROUP : (tap + 1) * GROUP]
        if step != 0:
            part = (lane_shift(part.astype(bf16), MAP * step) * row_ref[tap]).astype(f32)
        total = part if total is None else total + part
    o_ref[...] = total.astype(o_ref.dtype)


def depthwise(x, weights):
    channels, lanes = x.shape
    return pl.pallas_call(
        depthwise_kernel,
        grid=(channels // GROUP,),
        in_specs=[
            pl.BlockSpec((GROUP, lanes), lambda i: (i, 0)),
            pl.BlockSpec((GROUP, TAPS * WIDE), lambda i: (i, 0)),
        ],
        out_specs=pl.BlockSpec((GROUP, lanes), lambda i: (i, 0)),
        out_shape=jax.ShapeDtypeStruct((channels, lanes), bf16),
        scratch_shapes=[pltpu.VMEM((TAPS, GROUP, lanes), bf16)] * 3,
        compiler_params=pltpu.CompilerParams(vmem_limit_bytes=32 * MIB),
        cost_estimate=pl.CostEstimate(
            flops=2 * 49 * GROUP * channels * lanes, bytes_accessed=4 * channels * lanes, transcendentals=0
        ),
    )(x, weights)


def depthwise_back_kernel(
    keep_ref, got_ref, m_ref, stat_ref, sum_ref, gain_ref, x_ref, k_ref, add_ref,
    gx_ref, gk_ref, gg_ref, t_ref, s_ref, col_ref, row_ref,
):
    @pl.when(pl.program_id(0) == 0)
    def _():
        fill_masks(col_ref, row_ref)

    x = x_ref[...]
    lanes = x.shape[1]
    inverse = stat_ref[1:2]
    unit = (m_ref[...].astype(f32) - stat_ref[0:1]) * inverse
    grad = keep_ref[...].astype(f32) + got_ref[...].astype(f32)
    gg_ref[...] = jnp.broadcast_to(jnp.sum(grad * unit, axis=1, keepdims=True), gg_ref.shape)
    d = (inverse * (grad * gain_ref[...] - sum_ref[0:1] - unit * sum_ref[1:2])).astype(bf16)
    last = TAPS - 1
    for tap in range(TAPS):
        step = tap - TAPS // 2
        moved = lane_shift(d, -step)
        t_ref[tap] = moved if step == 0 else moved * col_ref[last - tap]
        moved = lane_shift(x, MAP * step)
        s_ref[tap] = moved if step == 0 else moved * row_ref[tap]
    t = t_ref[...].reshape(TAPS * GROUP, lanes)
    rows = jnp.dot(stacked_weights(k_ref), t, preferred_element_type=f32)
    total = add_ref[...]
    for tap in range(TAPS):
        step = tap - TAPS // 2
        part = rows[tap * GROUP : (tap + 1) * GROUP]
        if step != 0:
            part = (lane_shift(part.astype(bf16), -MAP * step) * row_ref[last - tap]).astype(f32)
        total = total + part
    gx_ref[...] = total
    pairs = lax.dot_general(
        t, s_ref[...].reshape(TAPS * GROUP, lanes), (((1,), (1,)), ((), ())), preferred_element_type=f32
    )
    side = TAPS * GROUP
    first = lax.broadcasted_iota(jnp.int32, (side, side), 0)
    second = lax.broadcasted_iota(jnp.int32, (side, side), 1)
    own = jnp.where(first % GROUP == second % GROUP, pairs, 0.0)
    source = lax.broadcasted_iota(jnp.int32, (side, 128), 0)
    target = lax.broadcasted_iota(jnp.int32, (side, 128), 1)
    pick = (source // GROUP == target).astype(f32).astype(bf16)
    high = own.astype(bf16)
    low = (own - high.astype(f32)).astype(bf16)
    gk_ref[0] = jnp.dot(high, pick, preferred_element_type=f32) + jnp.dot(
        low, pick, preferred_element_type=f32
    )


def depthwise_back(keep, got, mapped, stats, sums, gain, x, weights, add):
    channels, lanes = x.shape
    groups = channels // GROUP
    rows = pl.BlockSpec((GROUP, lanes), lambda i: (i, 0))
    fixed = pl.BlockSpec((8, lanes), lambda i: (0, 0))
    gx, gk, gg = pl.pallas_call(
        depthwise_back_kernel,
        grid=(groups,),
        in_specs=[
            rows, rows, rows, fixed, fixed,
            pl.BlockSpec((GROUP, 1), lambda i: (i, 0)),
            rows,
            pl.BlockSpec((GROUP, TAPS * WIDE), lambda i: (i, 0)),
            rows,
        ],
        out_specs=[
            rows,
            pl.BlockSpec((1, TAPS * GROUP, 128), lambda i: (i, 0, 0)),
            pl.BlockSpec((GROUP, 128), lambda i: (i, 0)),
        ],
        out_shape=[
            jax.ShapeDtypeStruct((channels, lanes), f32),
            jax.ShapeDtypeStruct((groups, TAPS * GROUP, 128), f32),
            jax.ShapeDtypeStruct((channels, 128), f32),
        ],
        scratch_shapes=[pltpu.VMEM((TAPS, GROUP, lanes), bf16)] * 4,
        compiler_params=pltpu.CompilerParams(vmem_limit_bytes=56 * MIB),
        cost_estimate=pl.CostEstimate(
            flops=4 * 49 * GROUP * channels * lanes, bytes_accessed=14 * channels * lanes, transcendentals=0
        ),
    )(keep, got, mapped, stats, sums, gain, x, weights, add)
    gk = gk[:, :, :TAPS].reshape(groups, TAPS, GROUP, TAPS).transpose(0, 2, 3, 1)
    return gx, gk.reshape(channels, TAPS * TAPS), gg[:, 0]


def gelu_both(u):
    share = 0.5 * (1.0 + lax.erf(u * (1.0 / math.sqrt(2.0))))
    return u * share, share + u * jnp.exp(-0.5 * u * u) * (1.0 / math.sqrt(2.0 * math.pi))


def block_of(size, most, unit):
    best = unit
    for candidate in range(unit, most + 1, unit):
        if size % candidate == 0:
            best = candidate
    return best if size % best == 0 else size


def pool_table():
    out_index = np.arange(GRID)
    first_row = out_index * MAP // GRID
    last_row = ((out_index + 1) * MAP + GRID - 1) // GRID
    source_index = np.arange(MAP)
    inside = (source_index[None, :] >= first_row[:, None]) & (
        source_index[None, :] < last_row[:, None]
    )
    single = inside.astype(np.float32) / (last_row - first_row)[:, None].astype(np.float32)
    table = single[:, None, :, None] * single[None, :, None, :]
    return table.reshape(GRID * GRID, MAP * MAP)


def mm(a, b):
    return jnp.dot(a, b, preferred_element_type=f32)


def mm_nt(a, b):
    return lax.dot_general(a, b, (((1,), (1,)), ((), ())), preferred_element_type=f32)


def mm_tn(a, b):
    return lax.dot_general(a, b, (((0,), (0,)), ((), ())), preferred_element_type=f32)


def whole(shape):
    return pl.BlockSpec(shape, lambda *_: (0,) * len(shape), pipeline_mode=pl.Buffered(1))


def shape_of(shape, dtype=bf16):
    return jax.ShapeDtypeStruct(shape, dtype)


def call(kernel, ids, grid, args, in_specs, outs, out_specs, scratch=(), flops=0, vmem=56):
    bytes_accessed = sum(v.size * v.dtype.itemsize for v in list(args) + list(outs))
    return pl.pallas_call(
        kernel,
        grid_spec=pltpu.PrefetchScalarGridSpec(
            num_scalar_prefetch=1,
            grid=grid,
            in_specs=in_specs,
            out_specs=out_specs,
            scratch_shapes=scratch,
        ),
        out_shape=outs,
        compiler_params=pltpu.CompilerParams(vmem_limit_bytes=vmem * MIB),
        cost_estimate=pl.CostEstimate(flops=int(flops), bytes_accessed=int(bytes_accessed), transcendentals=0),
    )(ids, *args)


def deal(stack_ref, keep_ref, send_ref, mine, lead=()):
    half = stack_ref.shape[0] // 2
    for j in range(half):
        block = 2 * reverse_bits(j, bit_count(half))
        keep_ref[(j,) + lead] = stack_ref[block + mine]
        send_ref[(j,) + lead] = stack_ref[block + 1 - mine]


def dealt_rows(w_ref, own, refs, operand, mine):
    half = refs[0].shape[0]
    for ref, bit in zip(refs, (mine, 1 - mine)):
        for j in range(half):
            block = 2 * reverse_bits(j, bit_count(half)) + bit
            rows = w_ref[pl.ds(pl.multiple_of(block * own, 16), own), :]
            ref[j] = mm(rows, operand[...]).astype(bf16)


def conv_forward(parts, up_t, down, gain, ids):
    count = len(parts)
    own, lanes = parts[0].shape
    channels = own * count
    hidden = up_t.shape[0]
    bn = block_of(lanes, 512, 128)
    step = block_of(hidden, 256, 128)

    def kernel(ids_ref, *refs):
        part_refs = refs[:count]
        up_ref, down_ref, gain_ref, cn_ref, h_ref, s_ref, stat_ref, keep_ref, send_ref = refs[count:]
        me = ids_ref[0]
        mean = sum(jnp.sum(part[...].astype(f32), axis=0, keepdims=True) for part in part_refs) * (1.0 / channels)
        square = sum(
            jnp.sum((part[...].astype(f32) - mean) ** 2, axis=0, keepdims=True) for part in part_refs
        ) * (1.0 / channels)
        inverse = lax.rsqrt(square + conv_eps)
        stat_ref[...] = jnp.concatenate([mean, inverse, jnp.zeros((6, bn), f32)], axis=0)
        for offset, part in enumerate(part_refs):
            rows = pl.ds(pl.multiple_of((me ^ offset) * own, 16), own)
            cn_ref[rows, :] = ((part[...].astype(f32) - mean) * inverse * gain_ref[rows, :]).astype(bf16)
        for f in range(0, hidden, step):
            act, slope = gelu_both(mm(up_ref[f : f + step], cn_ref[...]))
            h_ref[f : f + step] = act.astype(bf16)
            s_ref[f : f + step] = slope.astype(bf16)
        dealt_rows(down_ref, own, (keep_ref, send_ref), h_ref, me & 1)

    tall = lambda rows: pl.BlockSpec((rows, bn), lambda j, _: (0, j))
    half = pl.BlockSpec((count // 2, own, bn), lambda j, _: (0, 0, j))
    return call(
        kernel,
        ids,
        (lanes // bn,),
        (*parts, up_t, down, gain),
        [tall(own)] * count + [whole(up_t.shape), whole(down.shape), whole(gain.shape)],
        [
            shape_of((channels, lanes)),
            shape_of((hidden, lanes)),
            shape_of((hidden, lanes)),
            shape_of((8, lanes), f32),
            shape_of((count // 2, own, lanes)),
            shape_of((count // 2, own, lanes)),
        ],
        [tall(channels), tall(hidden), tall(hidden), tall(8), half, half],
        flops=4 * channels * hidden * lanes,
    )


def conv_backward(d_all, down_t, up, slope, ids):
    channels, lanes = d_all.shape
    hidden = down_t.shape[0]
    count = lax.axis_size("chan")
    own = channels // count
    bn = block_of(lanes, 512, 128)
    step = block_of(hidden, 512, 128)

    def kernel(ids_ref, d_ref, down_ref, up_ref, s_ref, du_ref, keep_ref, send_ref):
        for f in range(0, hidden, step):
            du = mm(down_ref[f : f + step], d_ref[...]) * s_ref[f : f + step].astype(f32)
            du_ref[f : f + step] = du.astype(bf16)
        dealt_rows(up_ref, own, (keep_ref, send_ref), du_ref, ids_ref[0] & 1)

    tall = lambda rows: pl.BlockSpec((rows, bn), lambda j, _: (0, j))
    half = pl.BlockSpec((count // 2, own, bn), lambda j, _: (0, 0, j))
    return call(
        kernel,
        ids,
        (lanes // bn,),
        (d_all, down_t, up, slope),
        [tall(channels), whole(down_t.shape), whole(up.shape), tall(hidden)],
        [
            shape_of((hidden, lanes)),
            shape_of((count // 2, own, lanes)),
            shape_of((count // 2, own, lanes)),
        ],
        [tall(hidden), half, half],
        flops=4 * channels * hidden * lanes,
    )


def down_gradient(parts, act, patchs, ids):
    count = len(parts)
    own, lanes = parts[0].shape
    channels = own * count
    hidden = act.shape[0]
    bn = block_of(hidden, 512, 128)
    size = channels // patchs

    def kernel(ids_ref, *refs):
        part_refs = refs[:count]
        b_ref, d_ref, keep_ref, send_ref, o_ref = refs[count:]

        @pl.when(pl.program_id(0) == 0)
        def _():
            for offset, part in enumerate(part_refs):
                d_ref[pl.ds(pl.multiple_of((ids_ref[0] ^ offset) * own, 16), own), :] = part[...]

        o_ref[...] = mm_nt(d_ref[...], b_ref[...]).astype(bf16).reshape(patchs, size, bn)
        deal(o_ref, keep_ref, send_ref, ids_ref[1] & 1)

    half = pl.BlockSpec((patchs // 2, size, bn), lambda j, _: (0, 0, j))
    d_all, keep, send = call(
        kernel,
        ids,
        (hidden // bn,),
        (*parts, act),
        [whole(parts[0].shape)] * count + [pl.BlockSpec((bn, lanes), lambda j, _: (j, 0))],
        [shape_of((channels, lanes))] + [shape_of((patchs // 2, size, hidden))] * 2,
        [whole((channels, lanes)), half, half],
        [pltpu.VMEM((patchs, size, bn), bf16)],
        flops=2 * channels * lanes * hidden,
    )
    return d_all, (keep, send)


def weight_gradient(a, b, patchs, ids):
    rows, depth = a.shape
    columns = b.shape[0]
    bn = block_of(columns, 512, 128)
    size = rows // patchs

    def kernel(ids_ref, a_ref, b_ref, keep_ref, send_ref, o_ref):
        o_ref[...] = mm_nt(a_ref[...], b_ref[...]).astype(bf16).reshape(patchs, size, bn)
        deal(o_ref, keep_ref, send_ref, ids_ref[1] & 1)

    half = pl.BlockSpec((patchs // 2, size, bn), lambda j, _: (0, 0, j))
    return call(
        kernel,
        ids,
        (columns // bn,),
        (a, b),
        [whole(a.shape), pl.BlockSpec((bn, depth), lambda j, _: (j, 0))],
        [shape_of((patchs // 2, size, columns))] * 2,
        [half, half],
        [pltpu.VMEM((patchs, size, bn), bf16)],
        flops=2 * rows * depth * columns,
    )


def pool_forward(keep, got, conv_flat, scale, images, band, chans, ids):
    own, lanes = keep.shape
    cells = lanes // images
    table = pool_table()
    tokens = table.shape[0]
    reach = band + 2 * GRID
    padded = jnp.asarray(np.pad(table, ((GRID, GRID), (0, 0))))

    def kernel(ids_ref, keep_ref, got_ref, c_ref, scale_ref, t_ref, p_ref, branch_ref, result_ref, pooled_ref, *pieces):
        branch = keep_ref[...].astype(f32) + got_ref[...].astype(f32)
        branch_ref[...] = branch.astype(bf16)
        result = (c_ref[...].astype(f32) + scale_ref[...] * branch).astype(bf16)
        result_ref[...] = result
        pooled_ref[0] = mm(result, t_ref[...]).astype(bf16)
        for offset, piece in enumerate(pieces):
            start = pl.multiple_of((ids_ref[0] ^ offset) * band, 8)
            rows = p_ref[pl.ds(start, reach), :].astype(bf16)
            piece[0] = mm_nt(rows, result).astype(bf16)

    flat = pl.BlockSpec((own, cells), lambda i, _: (0, i))
    return call(
        kernel,
        ids,
        (images,),
        (keep, got, conv_flat, scale, jnp.asarray(table.T.astype(bf16)), padded),
        [flat, flat, flat, whole(scale.shape), whole((cells, tokens)), whole(padded.shape)],
        [shape_of((own, lanes))] * 2
        + [shape_of((images, own, tokens))]
        + [shape_of((images, reach, own))] * chans,
        [flat, flat, pl.BlockSpec((1, own, tokens), lambda i, _: (i, 0, 0))]
        + [pl.BlockSpec((1, reach, own), lambda i, _: (i, 0, 0))] * chans,
        flops=2 * images * own * cells * (tokens + chans * reach),
    )


def row_moves(field, spots, step):
    if step == 0:
        return field
    count = field.shape[0]
    moved = pltpu.roll(field, (-step) % count, 0)
    column = spots % GRID + step
    return jnp.where((column >= 0) & (column < GRID), moved, 0.0)


def adapter(pieces, w_proj, kernel_three, gate_in, gate_out, d_band, ids):
    chans = len(pieces)
    images, reach, own = pieces[0].shape
    width = w_proj.shape[1]
    gate = gate_in.shape[1]
    band = reach - 2 * GRID

    def kernel(ids_ref, *refs):
        piece_refs = refs[:chans]
        proj_ref, k_ref, in_ref, out_ref, d_ref, gs_ref, ds_ref, gi_ref, go_ref, gk_ref = refs[chans:]
        me = ids_ref[0]

        @pl.when(pl.program_id(0) == 0)
        def _():
            gi_ref[...] = jnp.zeros_like(gi_ref)
            go_ref[...] = jnp.zeros_like(go_ref)
            gk_ref[...] = jnp.zeros_like(gk_ref)

        field = None
        for offset, piece in enumerate(piece_refs):
            start = pl.multiple_of((me ^ offset) * own, 16)
            term = mm(piece[0], proj_ref[pl.ds(start, own), :])
            field = term if field is None else field + term
        field = field.astype(bf16).astype(f32)
        spots = lax.broadcasted_iota(jnp.int32, (reach, 1), 0)
        moved = [row_moves(field, spots, step) for step in (-1, 0, 1)]
        smooth = None
        for t in range(9):
            term = k_ref[t : t + 1, :] * moved[t % 3][GRID * (t // 3) : GRID * (t // 3) + band]
            smooth = term if smooth is None else smooth + term
        rows = smooth.astype(bf16)
        act, slope = gelu_both(mm(rows, in_ref[...]))
        act = act.astype(bf16)
        value = jnp.tanh(mm(act, out_ref[...]))
        gs_ref[0] = value * smooth
        d = d_ref[0].astype(f32)
        d_logit = (d * smooth * (1.0 - value * value)).astype(bf16)
        d_gate = (mm_nt(d_logit, out_ref[...]) * slope).astype(bf16)
        d_smooth = d * value + mm_nt(d_gate, in_ref[...])
        ds_ref[0] = d_smooth.astype(bf16)
        go_ref[...] += mm_tn(act, d_logit)
        gi_ref[...] += mm_tn(rows, d_gate)
        for t in range(9):
            seen = moved[t % 3][GRID * (t // 3) : GRID * (t // 3) + band]
            gk_ref[t : t + 1, :] += jnp.sum(d_smooth * seen, axis=0, keepdims=True)

    per = lambda rows, cols: pl.BlockSpec((1, rows, cols), lambda i, _: (i, 0, 0))
    kept = lambda *shape: pl.BlockSpec(shape, lambda i, _: (0, 0))
    return call(
        kernel,
        ids,
        (images,),
        (*pieces, w_proj, kernel_three, gate_in, gate_out, d_band),
        [per(reach, own)] * chans
        + [whole(w_proj.shape), whole(kernel_three.shape), whole(gate_in.shape), whole(gate_out.shape), per(band, width)],
        [
            shape_of((images, band, width), f32),
            shape_of((images, band, width)),
            shape_of((width, gate), f32),
            shape_of((gate, width), f32),
            shape_of((16, width), f32),
        ],
        [per(band, width), per(band, width), kept(width, gate), kept(gate, width), kept(16, width)],
        flops=2 * images * (reach * own * chans + 6 * band * gate) * width,
    )


def adapter_back(parts, w_own, kernel_three, pooled, d_out, branch, scale, ids):
    chans = len(parts)
    images, band, width = parts[0].shape
    own, lanes = d_out.shape
    cells = lanes // images
    tokens = band * chans
    table = jnp.asarray(pool_table().astype(bf16))

    def kernel(ids_ref, *refs):
        part_refs = refs[:chans]
        w_ref, k_ref, pooled_ref, do_ref, branch_ref, scale_ref, t_ref, dr_ref, db_ref, gp_ref, gs_ref, f_ref = refs[chans:]
        me = ids_ref[0]

        @pl.when(pl.program_id(0) == 0)
        def _():
            gp_ref[...] = jnp.zeros_like(gp_ref)
            gs_ref[...] = jnp.zeros_like(gs_ref)
            f_ref[:GRID] = jnp.zeros((GRID, width), f32)
            f_ref[GRID + tokens :] = jnp.zeros((GRID, width), f32)

        for offset, part in enumerate(part_refs):
            start = pl.multiple_of((me ^ offset) * band + GRID, 8)
            f_ref[pl.ds(start, band), :] = part[0].astype(f32)
        field = f_ref[...]
        spots = lax.broadcasted_iota(jnp.int32, (tokens + 2 * GRID, 1), 0)
        moved = [row_moves(field, spots, -step) for step in (-1, 0, 1)]
        d_adapted = None
        for t in range(9):
            start = GRID * (2 - t // 3)
            term = k_ref[t : t + 1, :] * moved[t % 3][start : start + tokens]
            d_adapted = term if d_adapted is None else d_adapted + term
        d_adapted = d_adapted.astype(bf16)
        d_pooled = mm_nt(w_ref[...], d_adapted).astype(bf16)
        gp_ref[...] += mm(pooled_ref[0], d_adapted)
        d_result = do_ref[...].astype(f32) + mm(d_pooled, t_ref[...])
        dr_ref[...] = d_result
        db_ref[...] = (scale_ref[...] * d_result).astype(bf16)
        gs_ref[...] += jnp.sum(d_result * branch_ref[...].astype(f32), axis=1, keepdims=True)

    flat = pl.BlockSpec((own, cells), lambda i, _: (0, i))
    per = lambda rows, cols: pl.BlockSpec((1, rows, cols), lambda i, _: (i, 0, 0))
    return call(
        kernel,
        ids,
        (images,),
        (*parts, w_own, kernel_three, pooled, d_out, branch, scale, table),
        [per(band, width)] * chans
        + [whole(w_own.shape), whole(kernel_three.shape), per(own, tokens), flat, flat, whole(scale.shape), whole(table.shape)],
        [
            shape_of((own, lanes), f32),
            shape_of((own, lanes)),
            shape_of((own, width), f32),
            shape_of((own, 128), f32),
        ],
        [flat, flat, pl.BlockSpec((own, width), lambda i, _: (0, 0)), pl.BlockSpec((own, 128), lambda i, _: (0, 0))],
        [pltpu.VMEM((tokens + 2 * GRID, width), f32)],
        flops=2 * images * own * tokens * (2 * width + cells),
    )


def row_standard(values):
    center = values - jnp.mean(values, axis=-1, keepdims=True)
    inverse = lax.rsqrt(jnp.mean(center * center, axis=-1, keepdims=True) + vit_eps)
    return center * inverse


def stack_bands(stack_ref, values):
    count, band, _ = stack_ref.shape
    for b in range(count):
        stack_ref[b] = values[b * band : (b + 1) * band].astype(bf16)


def take_bands(rows_ref, part_refs, me):
    for offset, part in enumerate(part_refs):
        band = part.shape[1]
        start = pl.multiple_of((me ^ offset) * band, 8)
        rows_ref[pl.ds(start, band), :] = part[0].astype(f32)
    return rows_ref[...].astype(bf16)


def attention_forward(x, gain, w_qkv, w_attn, chans, ids):
    images, tokens, width = x.shape
    own = w_qkv.shape[2]
    heads = own // HEAD_DIM
    band = tokens // chans
    scale = 1.0 / math.sqrt(HEAD_DIM)

    def kernel(ids_ref, x_ref, gain_ref, qkv_w_ref, attn_ref, n_ref, qkv_ref, o_ref, log_ref, keep_ref, send_ref, stack_ref):
        normed = (row_standard(x_ref[0].astype(f32)) * gain_ref[...]).astype(bf16)
        n_ref[0] = normed
        q, k, v = (mm(normed, qkv_w_ref[t]).astype(bf16) for t in range(3))
        for t, part in enumerate((q, k, v)):
            qkv_ref[t, 0] = part
        mixed = []
        spot = lax.broadcasted_iota(jnp.int32, (tokens, 128), 1)
        logs = jnp.zeros((tokens, 128), f32)
        for h in range(heads):
            at = slice(h * HEAD_DIM, (h + 1) * HEAD_DIM)
            scores = mm_nt(q[:, at], k[:, at]) * scale
            most = jnp.max(scores, axis=-1, keepdims=True)
            powers = jnp.exp(scores - most)
            total = jnp.sum(powers, axis=-1, keepdims=True)
            logs = jnp.where(spot == h, most + jnp.log(total), logs)
            mixed.append(mm((powers * (1.0 / total)).astype(bf16), v[:, at]).astype(bf16))
        mixed = jnp.concatenate(mixed, axis=1)
        log_ref[0] = logs
        o_ref[0] = mixed
        stack_bands(stack_ref, mm_nt(mixed, attn_ref[...]))
        deal(stack_ref, keep_ref, send_ref, ids_ref[0] & 1, (0,))

    per = lambda cols: pl.BlockSpec((1, tokens, cols), lambda i, _: (i, 0, 0))
    half = pl.BlockSpec((chans // 2, 1, band, width), lambda i, _: (0, i, 0, 0))
    return call(
        kernel,
        ids,
        (images,),
        (x, gain, w_qkv, w_attn),
        [per(width), whole(gain.shape), whole(w_qkv.shape), whole(w_attn.shape)],
        [
            shape_of((images, tokens, width)),
            shape_of((3, images, tokens, own)),
            shape_of((images, tokens, own)),
            shape_of((images, tokens, 128), f32),
            shape_of((chans // 2, images, band, width)),
            shape_of((chans // 2, images, band, width)),
        ],
        [per(width), pl.BlockSpec((3, 1, tokens, own), lambda i, _: (0, i, 0, 0)), per(own), per(128), half, half],
        [pltpu.VMEM((chans, band, width), bf16)],
        flops=images * tokens * own * (8 * width + 4 * tokens * 4),
    )


def feed_forward(parts, d_rows, w_up, w_down, patchs, ids):
    chans = len(parts)
    images, band, width = parts[0].shape
    tokens = band * chans
    hidden = w_up.shape[1]
    size = width // patchs

    def kernel(ids_ref, *refs):
        part_refs = refs[:chans]
        (
            d_ref, up_ref, down_ref, keep_ref, send_ref, dkeep_ref, dsend_ref, gkeep_ref, gsend_ref,
            rows_ref, stack_ref, gu_ref, gd_ref, g_ref,
        ) = refs[chans:]
        me = ids_ref[0]
        step = pl.program_id(0)
        normed = take_bands(rows_ref, part_refs, me)
        act, slope = gelu_both(mm(normed, up_ref[...]))
        act = act.astype(bf16)
        stack_bands(stack_ref, mm_nt(act, down_ref[...]))
        deal(stack_ref, keep_ref, send_ref, me & 1, (0,))
        d = d_ref[0]
        d_pre = (mm(d, down_ref[...]) * slope).astype(bf16)
        stack_bands(stack_ref, mm_nt(d_pre, up_ref[...]))
        deal(stack_ref, dkeep_ref, dsend_ref, me & 1, (0,))
        gu = mm_tn(normed, d_pre)
        gd = mm_tn(d, act)

        @pl.when(step == 0)
        def _():
            gu_ref[...] = gu
            gd_ref[...] = gd

        @pl.when(step > 0)
        def _():
            gu_ref[...] += gu
            gd_ref[...] += gd

        @pl.when(step == images - 1)
        def _():
            for b in range(patchs):
                g_ref[b, :, :hidden] = gu_ref[b * size : (b + 1) * size].astype(bf16)
                g_ref[b, :, hidden:] = gd_ref[b * size : (b + 1) * size].astype(bf16)
            deal(g_ref, gkeep_ref, gsend_ref, ids_ref[1] & 1)

    per = lambda rows: pl.BlockSpec((1, rows, width), lambda i, _: (i, 0, 0))
    half = pl.BlockSpec((chans // 2, 1, band, width), lambda i, _: (0, i, 0, 0))
    halves = shape_of((chans // 2, images, band, width))
    grads = (patchs // 2, size, 2 * hidden)
    return call(
        kernel,
        ids,
        (images,),
        (*parts, d_rows, w_up, w_down),
        [per(band)] * chans + [per(tokens), whole(w_up.shape), whole(w_down.shape)],
        [halves] * 4 + [shape_of(grads)] * 2,
        [half] * 4 + [pl.BlockSpec(grads, lambda i, _: (0, 0, 0))] * 2,
        [
            pltpu.VMEM((tokens, width), f32),
            pltpu.VMEM((chans, band, width), bf16),
            pltpu.VMEM((width, hidden), f32),
            pltpu.VMEM((width, hidden), f32),
            pltpu.VMEM((patchs, size, 2 * hidden), bf16),
        ],
        flops=12 * images * tokens * width * hidden,
    )


def attention_backward(parts, normed, qkv, mixed, logs, w_qkv, w_attn, patchs, ids):
    chans = len(parts)
    images, band, width = parts[0].shape
    tokens = band * chans
    own = w_attn.shape[1]
    heads = own // HEAD_DIM
    size = width // patchs
    scale = 1.0 / math.sqrt(HEAD_DIM)

    def kernel(ids_ref, *refs):
        part_refs = refs[:chans]
        (
            n_ref, qkv_ref, o_ref, log_ref, qkv_w_ref, attn_ref, keep_ref, send_ref, gkeep_ref, gsend_ref,
            rows_ref, stack_ref, acc_ref, g_ref,
        ) = refs[chans:]
        me = ids_ref[0]
        step = pl.program_id(0)
        d = take_bands(rows_ref, part_refs, me)
        d_mixed = mm(d, attn_ref[...]).astype(bf16)
        q, k, v = (qkv_ref[t, 0] for t in range(3))
        grads = ([], [], [])
        for h in range(heads):
            at = slice(h * HEAD_DIM, (h + 1) * HEAD_DIM)
            soft = jnp.exp(mm_nt(q[:, at], k[:, at]) * scale - log_ref[0, :, h : h + 1])
            d_soft = mm_nt(d_mixed[:, at], v[:, at])
            across = jnp.sum(d_soft * soft, axis=-1, keepdims=True)
            d_scores = (soft * (d_soft - across)).astype(bf16)
            grads[0].append((mm(d_scores, k[:, at]) * scale).astype(bf16))
            grads[1].append((mm_tn(d_scores, q[:, at]) * scale).astype(bf16))
            grads[2].append(mm_tn(soft.astype(bf16), d_mixed[:, at]).astype(bf16))
        grads = [jnp.concatenate(v, axis=1) for v in grads]
        total = None
        for t in range(3):
            term = mm_nt(grads[t], qkv_w_ref[t])
            total = term if total is None else total + term
        stack_bands(stack_ref, total)
        deal(stack_ref, keep_ref, send_ref, me & 1, (0,))
        new = [mm_tn(n_ref[0], g) for g in grads] + [mm_tn(d, o_ref[0])]

        @pl.when(step == 0)
        def _():
            for t in range(4):
                acc_ref[:, t * own : (t + 1) * own] = new[t]

        @pl.when(step > 0)
        def _():
            for t in range(4):
                acc_ref[:, t * own : (t + 1) * own] += new[t]

        @pl.when(step == images - 1)
        def _():
            for b in range(patchs):
                g_ref[b] = acc_ref[b * size : (b + 1) * size].astype(bf16)
            deal(g_ref, gkeep_ref, gsend_ref, ids_ref[1] & 1)

    per = lambda rows, cols: pl.BlockSpec((1, rows, cols), lambda i, _: (i, 0, 0))
    half = pl.BlockSpec((chans // 2, 1, band, width), lambda i, _: (0, i, 0, 0))
    halves = shape_of((chans // 2, images, band, width))
    out = (patchs // 2, size, 4 * own)
    return call(
        kernel,
        ids,
        (images,),
        (*parts, normed, qkv, mixed, logs, w_qkv, w_attn),
        [per(band, width)] * chans
        + [
            per(tokens, width),
            pl.BlockSpec((3, 1, tokens, own), lambda i, _: (0, i, 0, 0)),
            per(tokens, own),
            per(tokens, 128),
            whole(w_qkv.shape),
            whole(w_attn.shape),
        ],
        [halves] * 2 + [shape_of(out)] * 2,
        [half] * 2 + [pl.BlockSpec(out, lambda i, _: (0, 0, 0))] * 2,
        [
            pltpu.VMEM((tokens, width), f32),
            pltpu.VMEM((chans, band, width), bf16),
            pltpu.VMEM((width, 4 * own), f32),
            pltpu.VMEM((patchs, size, 4 * own), bf16),
        ],
        flops=images * tokens * own * (18 * width + 10 * tokens * 4),
    )


def standardize(values, epsilon):
    center = values - jnp.mean(values, axis=-1, keepdims=True)
    inverse = lax.rsqrt(jnp.mean(center * center, axis=-1, keepdims=True) + epsilon)
    return center * inverse, inverse


def norm_back(grad, gain, unit, inverse):
    scaled = grad * gain
    return inverse * (
        scaled
        - jnp.mean(scaled, axis=-1, keepdims=True)
        - unit * jnp.mean(scaled * unit, axis=-1, keepdims=True)
    )


def body(
    vit_in,
    conv_in,
    ln_one,
    w_qkv,
    w_attn,
    ln_two,
    w_up,
    w_down,
    conv_kernel,
    conv_gain,
    conv_up,
    conv_down,
    layer_scale,
    w_proj,
    adapter_kernel,
    gate_in,
    gate_out,
    d_merged,
    d_conv_out,
):
    chans = lax.axis_size("chan")
    patchs = lax.axis_size("patch")
    me = lax.axis_index("chan")
    ids = jnp.stack([me, lax.axis_index("patch")]).astype(jnp.int32)
    tokens, images, width = vit_in.shape
    band = tokens // chans
    own_channels, _, cells = conv_in.shape
    channels = own_channels * chans
    lanes = images * cells
    hidden = w_up.shape[1]
    own_width = w_attn.shape[1]

    def own_rows(values, size):
        return lax.dynamic_slice_in_dim(values, me * size, size, 0)

    def own_band(values):
        return lax.dynamic_slice_in_dim(values, me * band, band, 0).swapaxes(0, 1)

    def after(values, *earlier):
        return lax.optimization_barrier((values,) + earlier)[0]

    def summed(pair):
        return pair[0].astype(f32) + pair[1].astype(f32)

    conv_flat = conv_in.reshape(own_channels, lanes)
    weights = tap_weights(own_rows(conv_kernel, own_channels))
    mapped = depthwise(conv_flat, weights)
    mapped_parts = gather_parts(mapped, "chan")

    gain_one = ln_one.astype(f32)[None]
    gain_two = ln_two.astype(f32)[None]
    w_three = w_qkv.swapaxes(0, 1)
    normed_one, qkv, mixed, logs, keep, send = attention_forward(
        vit_in.swapaxes(0, 1), gain_one, w_three, w_attn, chans, after(ids, mapped)
    )
    vit_band = own_band(vit_in).astype(f32)
    middle = vit_band + summed(sum_rest(keep, send, "chan"))
    unit_two, inverse_two = standardize(middle, vit_eps)
    normed_parts = gather_parts((unit_two * gain_two).astype(bf16), "chan")

    gain_all = conv_gain.astype(f32)[:, None]
    conv_norm, conv_act, conv_slope, stats, conv_keep, conv_send = conv_forward(
        mapped_parts, conv_up.T, conv_down, gain_all, after(ids, keep)
    )
    d_rows = d_merged.swapaxes(0, 1)
    out_keep, out_send, d_keep, d_send, vit_keep, vit_send = feed_forward(
        normed_parts, d_rows, w_up, w_down, patchs, after(ids, stats)
    )

    keep, got = sum_rest(conv_keep, conv_send, "chan")
    own_scale = own_rows(layer_scale, own_channels).astype(f32)[:, None]
    branch_maps, conv_result, pooled, *pieces = pool_forward(
        keep, got, conv_flat, own_scale, images, band, chans, after(ids, vit_keep)
    )
    for offset in range(1, chans):
        pieces[offset] = lax.ppermute(pieces[offset], "chan", [(i, i ^ offset) for i in range(chans)])

    d_normed_two = summed(sum_rest(d_keep, d_send, "chan"))
    branch = summed(sum_rest(out_keep, out_send, "chan"))
    d_band = own_band(d_merged)
    d_middle = d_band.astype(f32) + norm_back(d_normed_two, gain_two, unit_two, inverse_two)
    g_ln_two = jnp.sum(d_normed_two * unit_two, axis=(0, 1))
    d_parts = gather_parts(d_middle.astype(bf16), "chan")

    kernel_three = jnp.pad(adapter_kernel.astype(f32).T, ((0, 7), (0, 0)))
    gated, d_smooth, g_gate_in, g_gate_out, g_adapter = adapter(
        pieces, w_proj, kernel_three, gate_in, gate_out, d_band, after(ids, pooled)
    )
    merged = (middle + branch + gated).astype(bf16)
    smooth_parts = gather_parts(d_smooth, "chan")
    d_result, d_branch, g_proj, g_scale = adapter_back(
        smooth_parts,
        own_rows(w_proj, own_channels),
        kernel_three,
        pooled,
        d_conv_out.reshape(own_channels, lanes),
        branch_maps,
        own_scale,
        ids,
    )
    branch_parts = gather_parts(d_branch, "chan")

    keep, send, att_keep, att_send = attention_backward(
        d_parts, normed_one, qkv, mixed, logs, w_three, w_attn, patchs, after(ids, d_branch)
    )
    d_normed_one = summed(sum_rest(keep, send, "chan"))
    unit_one, inverse_one = standardize(vit_band, vit_eps)
    g_vit = d_middle + norm_back(d_normed_one, gain_one, unit_one, inverse_one)
    g_ln_one = jnp.sum(d_normed_one * unit_one, axis=(0, 1))
    g_vit_in = jnp.zeros((tokens, images, width), f32)
    for offset, part in enumerate(gather_parts(g_vit.astype(bf16), "chan")):
        g_vit_in = lax.dynamic_update_slice_in_dim(
            g_vit_in, part.swapaxes(0, 1).astype(f32), (me ^ offset) * band, 0
        )

    d_all, conv_down_pair = down_gradient(branch_parts, conv_act, patchs, after(ids, att_keep))
    d_pre, keep, send = conv_backward(d_all, conv_down.T, conv_up, conv_slope, after(ids, conv_down_pair[0]))
    conv_up_pair = weight_gradient(conv_norm, d_pre, patchs, after(ids, keep))
    keep, got = sum_rest(keep, send, "chan")
    own_gain = own_rows(conv_gain, own_channels).astype(f32)[:, None]
    scaled = summed((keep, got)) * own_gain
    own_unit = (mapped.astype(f32) - stats[0]) * stats[1]
    sums = jnp.stack([jnp.sum(scaled, axis=0), jnp.sum(scaled * own_unit, axis=0)])
    sums = jnp.pad(sum_all(sums, "chan") * (1.0 / channels), ((0, 6), (0, 0)))
    g_conv_flat, g_kernel, g_gain = depthwise_back(
        keep, got, mapped, stats, sums, own_gain, conv_flat, weights, d_result
    )

    vit_grads = summed(sum_rest(vit_keep, vit_send, "patch"))
    att_grads = summed(sum_rest(att_keep, att_send, "patch"))
    g_conv_down = summed(sum_rest(*conv_down_pair, "patch"))
    g_conv_up = summed(sum_rest(*conv_up_pair, "patch"))

    places = [(p * chans + c, c * patchs + p) for p in range(patchs) for c in range(chans)]

    def own_sum(values):
        blocks = values.reshape(patchs, own_channels // patchs, -1)
        total = sum_scatter(halving_order(blocks, "patch"), "patch")
        return lax.ppermute(total, ("patch", "chan"), places)

    everywhere = patchs * chans
    rows = own_channels // patchs

    def share(shares, kind):
        flat = [v.astype(kind).reshape(chans, patchs, -1) for v in shares]
        flat = jnp.concatenate(flat, axis=2)
        flat = jnp.pad(flat, ((0, 0), (0, 0), (0, -flat.shape[2] % (rows * 128))))
        flat = flat.reshape(chans, patchs, rows, -1)
        return sum_scatter(halving_order(flat, "chan"), "chan").reshape(own_channels, -1)

    def unshare(values, shares):
        flat = values.reshape(-1)
        out = []
        for v in shares:
            size = v.size // everywhere
            out.append(flat[:size].reshape((v.shape[0] // everywhere,) + v.shape[1:]).astype(f32))
            flat = flat[size:]
        return out

    early = [g_gate_in, g_gate_out, g_adapter[:9].T, g_ln_two]
    own_early = own_sum(jnp.concatenate([g_proj.astype(bf16), share(early, bf16)], axis=1))
    g_proj = own_early[:, :width].astype(f32)
    g_gate_in, g_gate_out, g_adapter, g_ln_two = unshare(own_early[:, width:], early)
    own_late = own_sum(
        jnp.concatenate([g_kernel, g_gain[:, None], g_scale[:, :78], share([g_ln_one], f32)], axis=1)
    )
    (g_ln_one,) = unshare(own_late[:, 128:], [g_ln_one])
    qkv_width = 3 * own_width
    return (
        merged.swapaxes(0, 1),
        conv_result.reshape(conv_in.shape),
        g_vit_in,
        g_conv_flat.reshape(conv_in.shape),
        g_ln_one,
        att_grads[:, :qkv_width].reshape(-1, 3, own_width),
        att_grads[:, qkv_width:],
        g_ln_two,
        vit_grads[:, :hidden],
        vit_grads[:, hidden:],
        own_late[:, :49],
        own_late[:, 49],
        g_conv_up,
        g_conv_down,
        own_late[:, 50],
        g_proj,
        g_adapter,
        g_gate_in,
        g_gate_out,
    )


def solution(mesh):
    in_specs = (
        P(None, "patch", None),
        P("chan", "patch", None),
        P(),
        P(None, None, "chan"),
        P(None, "chan"),
        P(),
        P(None, "chan"),
        P(None, "chan"),
        P(),
        P(),
        P(None, "chan"),
        P(None, "chan"),
        P(),
        P(),
        P(),
        P(),
        P(),
        P(None, "patch", None),
        P("chan", "patch", None),
    )
    out_specs = (
        P("chan", "patch", None),
        P("chan", "patch", None),
        P(None, "patch", None),
        P("chan", "patch", None),
        P(("patch", "chan")),
        P("patch", None, "chan"),
        P("patch", "chan"),
        P(("patch", "chan")),
        P("patch", "chan"),
        P("patch", "chan"),
        P(("patch", "chan"), None),
        P(("patch", "chan")),
        P("patch", "chan"),
        P("patch", "chan"),
        P(("patch", "chan")),
        P(("patch", "chan"), None),
        P(("patch", "chan"), None),
        P(("patch", "chan"), None),
        P(("patch", "chan"), None),
    )
    return jax.shard_map(body, mesh=mesh, in_specs=in_specs, out_specs=out_specs, check_vma=False)
```

```python
import math

import jax
import jax.numpy as jnp
import numpy as np
from jax import lax
from jax.experimental import pallas as pl
from jax.experimental.layout import Layout, with_layout_constraint
from jax.experimental.pallas import tpu as pltpu
from jax.sharding import PartitionSpec as P

HEAD_DIM = 64
GRID = 24
MAP = 32
TAPS = 7
GROUP = 32
WIDE = 256

vit_eps = 1e-05
conv_eps = 1e-06
f32 = jnp.float32
bf16 = jnp.bfloat16
MIB = 2**20


def bit_count(size):
    return size.bit_length() - 1


def reverse_bits(value, bits):
    return sum(((value >> k) & 1) << (bits - 1 - k) for k in range(bits))


def swap(values, axis, other):
    count = lax.axis_size(axis)
    return lax.ppermute(values, axis, [(i, i ^ other) for i in range(count)])


def move(values, axis, other):
    return swap(values, axis, other) if isinstance(other, int) else lax.ppermute(values, axis, other)


def beside(work, sends):
    def run():
        return work(), [move(*send) for send in sends]

    def skip():
        return jax.tree.map(lambda v: jnp.zeros(v.shape, v.dtype), jax.eval_shape(run))

    return lax.optimization_barrier(lax.cond(lax.axis_index("chan") < lax.axis_size("chan"), run, skip))


def fold(keep, got, axis, bit):
    mine = (lax.axis_index(axis) >> (bit + 1)) & 1
    half = keep.shape[0] // 2
    return tuple(
        sum(lax.dynamic_slice_in_dim(v, which * half, half, 0).astype(f32) for v in (keep, got)).astype(keep.dtype)
        for which in (mine, 1 - mine)
    )


def finish(keep, got, axis, bit):
    while bit + 1 < bit_count(lax.axis_size(axis)):
        keep, send = fold(keep, got, axis, bit)
        bit += 1
        got = swap(send, axis, 1 << bit)
    return keep[0], got[0]


def plain(values):
    return with_layout_constraint(values, Layout(tuple(range(values.ndim))))


def halves(blocks, axis):
    return halves_at(blocks, axis, 0)


def halves_at(blocks, axis, bit):
    mine = (lax.axis_index(axis) >> bit) & 1
    half = blocks.shape[0] // 2
    return tuple(lax.dynamic_slice_in_dim(blocks, which * half, half, 0) for which in (mine, 1 - mine))


def sum_scatter(values, axis, first=0):
    for bit in range(first, bit_count(lax.axis_size(axis))):
        mine = (lax.axis_index(axis) >> bit) & 1
        half = values.shape[0] // 2
        keep = lax.dynamic_slice_in_dim(values, mine * half, half, 0)
        send = lax.dynamic_slice_in_dim(values, (1 - mine) * half, half, 0)
        values = keep + swap(send, axis, 1 << bit)
    return values[0]


def halving_order(values, axis):
    count = lax.axis_size(axis)
    bits = bit_count(count)
    return jnp.stack([values[reverse_bits(j, bits)] for j in range(count)])


def parts_beside(block, far):
    top = bit_count(lax.axis_size("chan")) - 1
    parts = {0: block, 1 << top: far}
    for bit in reversed(range(top)):
        for offset in list(parts):
            parts[offset | (1 << bit)] = swap(parts[offset], "chan", 1 << bit)
    return [parts[offset] for offset in sorted(parts)]


def sum_all(values, axis, first=0):
    for bit in range(first, bit_count(lax.axis_size(axis))):
        values = values + swap(values, axis, 1 << bit)
    return values


def lane_shift(values, step):
    count = values.shape[-1]
    step = step % count
    return values if step == 0 else pltpu.roll(values, count - step, 1)


def fill_masks(col_ref, row_ref):
    lanes = col_ref.shape[-1]
    place = lax.broadcasted_iota(jnp.int32, (GROUP, lanes), 1)
    col = place % MAP
    row = (place // MAP) % MAP
    for tap in range(TAPS):
        step = tap - TAPS // 2
        for ref, spot in ((col_ref, col), (row_ref, row)):
            ref[tap] = ((spot + step >= 0) & (spot + step < MAP)).astype(f32).astype(bf16)


def tap_weights(kernel):
    tap = np.arange(TAPS * TAPS)[:, None]
    spot = np.arange(TAPS * WIDE)[None, :]
    pick = (tap == (spot // WIDE) * TAPS + (spot % WIDE) // GROUP) & (spot % WIDE < TAPS * GROUP)
    own = (jnp.arange(kernel.shape[0])[:, None] % GROUP) == jnp.asarray(spot % GROUP)
    spread = jnp.dot(kernel, jnp.asarray(pick.astype(bf16)), preferred_element_type=f32)
    return jnp.where(own, spread, 0.0).astype(bf16)


def stacked_weights(k_ref):
    blocks = [k_ref[:, r * WIDE : r * WIDE + TAPS * GROUP] for r in range(TAPS)]
    return jnp.concatenate(blocks, axis=0)


def depthwise_kernel(x_ref, k_ref, o_ref, s_ref, col_ref, row_ref):
    @pl.when(pl.program_id(0) == 0)
    def _():
        fill_masks(col_ref, row_ref)

    x = x_ref[...]
    lanes = x.shape[1]
    for tap in range(TAPS):
        step = tap - TAPS // 2
        moved = lane_shift(x, step)
        s_ref[tap] = moved if step == 0 else moved * col_ref[tap]
    rows = jnp.dot(
        stacked_weights(k_ref), s_ref[...].reshape(TAPS * GROUP, lanes), preferred_element_type=f32
    )
    total = None
    for tap in range(TAPS):
        step = tap - TAPS // 2
        part = rows[tap * GROUP : (tap + 1) * GROUP]
        if step != 0:
            part = (lane_shift(part.astype(bf16), MAP * step) * row_ref[tap]).astype(f32)
        total = part if total is None else total + part
    o_ref[...] = total.astype(o_ref.dtype)


def depthwise(x, weights):
    channels, lanes = x.shape
    return pl.pallas_call(
        depthwise_kernel,
        grid=(channels // GROUP,),
        in_specs=[
            pl.BlockSpec((GROUP, lanes), lambda i: (i, 0)),
            pl.BlockSpec((GROUP, TAPS * WIDE), lambda i: (i, 0)),
        ],
        out_specs=pl.BlockSpec((GROUP, lanes), lambda i: (i, 0)),
        out_shape=jax.ShapeDtypeStruct((channels, lanes), bf16),
        scratch_shapes=[pltpu.VMEM((TAPS, GROUP, lanes), bf16)] * 3,
        compiler_params=pltpu.CompilerParams(vmem_limit_bytes=32 * MIB),
        cost_estimate=pl.CostEstimate(
            flops=int(8 * 1.1e9), bytes_accessed=4 * channels * lanes, transcendentals=0
        ),
    )(x, weights)


def depthwise_back_kernel(
    keep_ref, near_ref, far_ref, m_ref, stat_ref, sum_ref, gain_ref, x_ref, k_ref, add_ref,
    gx_ref, gk_ref, gg_ref, t_ref, s_ref, col_ref, row_ref,
):
    @pl.when(pl.program_id(0) == 0)
    def _():
        fill_masks(col_ref, row_ref)

    x = x_ref[...]
    lanes = x.shape[1]
    inverse = stat_ref[1:2]
    unit = (m_ref[...].astype(f32) - stat_ref[0:1]) * inverse
    got = jnp.concatenate([near_ref[...], far_ref[...]], axis=1)
    grad = keep_ref[...].astype(f32) + got.astype(f32)
    gg_ref[...] = jnp.broadcast_to(jnp.sum(grad * unit, axis=1, keepdims=True), gg_ref.shape)
    d = (inverse * (grad * gain_ref[...] - sum_ref[0:1] - unit * sum_ref[1:2])).astype(bf16)
    last = TAPS - 1
    for tap in range(TAPS):
        step = tap - TAPS // 2
        moved = lane_shift(d, -step)
        t_ref[tap] = moved if step == 0 else moved * col_ref[last - tap]
        moved = lane_shift(x, MAP * step)
        s_ref[tap] = moved if step == 0 else moved * row_ref[tap]
    t = t_ref[...].reshape(TAPS * GROUP, lanes)
    rows = jnp.dot(stacked_weights(k_ref), t, preferred_element_type=f32)
    total = add_ref[...]
    for tap in range(TAPS):
        step = tap - TAPS // 2
        part = rows[tap * GROUP : (tap + 1) * GROUP]
        if step != 0:
            part = (lane_shift(part.astype(bf16), -MAP * step) * row_ref[last - tap]).astype(f32)
        total = total + part
    cells = gx_ref.shape[2]
    for i in range(gx_ref.shape[1]):
        gx_ref[:, i, :] = total[:, i * cells : (i + 1) * cells]
    pairs = lax.dot_general(
        t, s_ref[...].reshape(TAPS * GROUP, lanes), (((1,), (1,)), ((), ())), preferred_element_type=f32
    )
    side = TAPS * GROUP
    first = lax.broadcasted_iota(jnp.int32, (side, side), 0)
    second = lax.broadcasted_iota(jnp.int32, (side, side), 1)
    own = jnp.where(first % GROUP == second % GROUP, pairs, 0.0)
    source = lax.broadcasted_iota(jnp.int32, (side, 128), 0)
    target = lax.broadcasted_iota(jnp.int32, (side, 128), 1)
    pick = (source // GROUP == target).astype(f32).astype(bf16)
    high = own.astype(bf16)
    low = (own - high.astype(f32)).astype(bf16)
    gk_ref[0] = jnp.dot(high, pick, preferred_element_type=f32) + jnp.dot(
        low, pick, preferred_element_type=f32
    )


def depthwise_back(keep, near, far, mapped, stats, sums, gain, x, weights, add, images):
    channels, lanes = x.shape
    groups = channels // GROUP
    rows = pl.BlockSpec((GROUP, lanes), lambda i: (i, 0))
    half = pl.BlockSpec((GROUP, lanes // 2), lambda i: (i, 0))
    fixed = pl.BlockSpec((8, lanes), lambda i: (0, 0))
    gx, gk, gg = pl.pallas_call(
        depthwise_back_kernel,
        grid=(groups,),
        in_specs=[
            rows, half, half, rows, fixed, fixed,
            pl.BlockSpec((GROUP, 1), lambda i: (i, 0)),
            rows,
            pl.BlockSpec((GROUP, TAPS * WIDE), lambda i: (i, 0)),
            rows,
        ],
        out_specs=[
            pl.BlockSpec((GROUP, images, lanes // images), lambda i: (i, 0, 0)),
            pl.BlockSpec((1, TAPS * GROUP, 128), lambda i: (i, 0, 0)),
            pl.BlockSpec((GROUP, 128), lambda i: (i, 0)),
        ],
        out_shape=[
            jax.ShapeDtypeStruct((channels, images, lanes // images), f32),
            jax.ShapeDtypeStruct((groups, TAPS * GROUP, 128), f32),
            jax.ShapeDtypeStruct((channels, 128), f32),
        ],
        scratch_shapes=[pltpu.VMEM((TAPS, GROUP, lanes), bf16)] * 4,
        compiler_params=pltpu.CompilerParams(vmem_limit_bytes=56 * MIB),
        cost_estimate=pl.CostEstimate(
            flops=int(16 * 1.1e9), bytes_accessed=14 * channels * lanes, transcendentals=0
        ),
    )(keep, near, far, mapped, stats, sums, gain, x, weights, add)
    gk = gk[:, :, :TAPS].reshape(groups, TAPS, GROUP, TAPS).transpose(0, 2, 3, 1)
    return gx, gk.reshape(channels, TAPS * TAPS), gg[:, 0]


def gelu_both(u):
    share = 0.5 * (1.0 + lax.erf(u * (1.0 / math.sqrt(2.0))))
    return u * share, share + u * jnp.exp(-0.5 * u * u) * (1.0 / math.sqrt(2.0 * math.pi))


def block_of(size, most, unit):
    best = unit
    for candidate in range(unit, most + 1, unit):
        if size % candidate == 0:
            best = candidate
    return best if size % best == 0 else size


def pool_table():
    out_index = np.arange(GRID)
    first_row = out_index * MAP // GRID
    last_row = ((out_index + 1) * MAP + GRID - 1) // GRID
    source_index = np.arange(MAP)
    inside = (source_index[None, :] >= first_row[:, None]) & (
        source_index[None, :] < last_row[:, None]
    )
    single = inside.astype(np.float32) / (last_row - first_row)[:, None].astype(np.float32)
    table = single[:, None, :, None] * single[None, :, None, :]
    return table.reshape(GRID * GRID, MAP * MAP)


PACE = 1.1e9


def mm(a, b):
    return jnp.dot(a, b, preferred_element_type=f32)


def mm_nt(a, b):
    return lax.dot_general(a, b, (((1,), (1,)), ((), ())), preferred_element_type=f32)


def mm_tn(a, b):
    return lax.dot_general(a, b, (((0,), (0,)), ((), ())), preferred_element_type=f32)


def whole(shape):
    return pl.BlockSpec(shape, lambda *_: (0,) * len(shape), pipeline_mode=pl.Buffered(1))


def shape_of(shape, dtype=bf16):
    return jax.ShapeDtypeStruct(shape, dtype)


def call(kernel, ids, grid, args, in_specs, outs, out_specs, scratch=(), micros=10, vmem=56, earlier=(), through=()):
    count = len(earlier)
    passed = len(through)
    ins = len(args)
    results = len(outs)

    def run(ids_ref, *refs):
        refs = refs[count + passed :]
        kernel(ids_ref, *refs[: ins + results], *refs[ins + results + passed :])

    bytes_accessed = sum(v.size * v.dtype.itemsize for v in list(args) + list(outs))
    return pl.pallas_call(
        run,
        grid_spec=pltpu.PrefetchScalarGridSpec(
            num_scalar_prefetch=1,
            grid=grid,
            in_specs=[pl.BlockSpec(memory_space=pl.ANY)] * (count + passed) + in_specs,
            out_specs=out_specs + [pl.BlockSpec(memory_space=pl.ANY)] * passed,
            scratch_shapes=scratch,
        ),
        out_shape=outs + [jax.ShapeDtypeStruct(v.shape, v.dtype) for v in through],
        input_output_aliases={1 + count + i: results + i for i in range(passed)},
        compiler_params=pltpu.CompilerParams(vmem_limit_bytes=vmem * MIB),
        cost_estimate=pl.CostEstimate(flops=int(micros * PACE), bytes_accessed=int(bytes_accessed), transcendentals=0),
    )(ids, *earlier, *through, *args)


def deal(stack_ref, keep_ref, send_ref, mine, lead=()):
    half = stack_ref.shape[0] // 2
    for j in range(half):
        block = 2 * reverse_bits(j, bit_count(half))
        keep_ref[(j,) + lead] = stack_ref[block + mine]
        send_ref[(j,) + lead] = stack_ref[block + 1 - mine]


def dealt_rows(w_ref, own, refs, operand, mine):
    half = refs[0].shape[0]
    for ref, bit in zip(refs, (mine, 1 - mine)):
        for j in range(half):
            block = 2 * reverse_bits(j, bit_count(half)) + bit
            rows = w_ref[pl.ds(pl.multiple_of(block * own, 16), own), :]
            ref[j] = mm(rows, operand[...]).astype(bf16)


def conv_forward(parts, up_t, down, gain, ids, earlier=(), through=()):
    count = len(parts)
    own, lanes = parts[0].shape
    channels = own * count
    hidden = up_t.shape[0]
    bn = block_of(lanes, 512, 128)
    step = block_of(hidden, 256, 128)

    def kernel(ids_ref, *refs):
        part_refs = refs[:count]
        up_ref, down_ref, gain_ref, cn_ref, h_ref, s_ref, stat_ref, keep_ref, send_ref = refs[count:]
        me = ids_ref[0]
        mean = sum(jnp.sum(part[...].astype(f32), axis=0, keepdims=True) for part in part_refs) * (1.0 / channels)
        square = sum(
            jnp.sum((part[...].astype(f32) - mean) ** 2, axis=0, keepdims=True) for part in part_refs
        ) * (1.0 / channels)
        inverse = lax.rsqrt(square + conv_eps)
        stat_ref[...] = jnp.concatenate([mean, inverse, jnp.zeros((6, bn), f32)], axis=0)
        for offset, part in enumerate(part_refs):
            rows = pl.ds(pl.multiple_of((me ^ offset) * own, 16), own)
            cn_ref[rows, :] = ((part[...].astype(f32) - mean) * inverse * gain_ref[rows, :]).astype(bf16)
        for f in range(0, hidden, step):
            act, slope = gelu_both(mm(up_ref[f : f + step], cn_ref[...]))
            h_ref[f : f + step] = act.astype(bf16)
            s_ref[f : f + step] = slope.astype(bf16)
        dealt_rows(down_ref, own, (keep_ref, send_ref), h_ref, me & 1)

    tall = lambda rows: pl.BlockSpec((rows, bn), lambda j, _: (0, j))
    half = pl.BlockSpec((count // 2, own, bn), lambda j, _: (0, 0, j))
    return call(
        kernel,
        ids,
        (lanes // bn,),
        (*parts, up_t, down, gain),
        [tall(own)] * count + [whole(up_t.shape), whole(down.shape), whole(gain.shape)],
        [
            shape_of((channels, lanes)),
            shape_of((hidden, lanes)),
            shape_of((hidden, lanes)),
            shape_of((8, lanes), f32),
            shape_of((count // 2, own, lanes)),
            shape_of((count // 2, own, lanes)),
        ],
        [tall(channels), tall(hidden), tall(hidden), tall(8), half, half],
        micros=36,
        earlier=earlier,
        through=through,
    )


def conv_backward(d_all, down_t, up, slope, normed, gain, ids, earlier=(), through=()):
    channels, lanes = d_all.shape
    hidden = down_t.shape[0]
    count = lax.axis_size("chan")
    own = channels // count
    bn = block_of(lanes, 512, 128)
    step = block_of(hidden, 512, 128)

    def kernel(ids_ref, d_ref, down_ref, up_ref, s_ref, n_ref, gain_ref, du_ref, keep_ref, send_ref, sum_ref):
        for f in range(0, hidden, step):
            du = mm(down_ref[f : f + step], d_ref[...]) * s_ref[f : f + step].astype(f32)
            du_ref[f : f + step] = du.astype(bf16)
        mine = ids_ref[0] & 1
        first = second = jnp.zeros((1, bn), f32)
        for ref, bit in ((keep_ref, mine), (send_ref, 1 - mine)):
            for j in range(count // 2):
                block = 2 * reverse_bits(j, bit_count(count // 2)) + bit
                rows = pl.ds(pl.multiple_of(block * own, 16), own)
                part = mm(up_ref[rows, :], du_ref[...])
                ref[j] = part.astype(bf16)
                first += jnp.sum(part * gain_ref[rows, :], axis=0, keepdims=True)
                second += jnp.sum(part * n_ref[rows, :].astype(f32), axis=0, keepdims=True)
        sum_ref[...] = jnp.concatenate([first, second, jnp.zeros((6, bn), f32)], axis=0)

    tall = lambda rows: pl.BlockSpec((rows, bn), lambda j, _: (0, j))
    half = pl.BlockSpec((count // 2, own, bn), lambda j, _: (0, 0, j))
    return call(
        kernel,
        ids,
        (lanes // bn,),
        (d_all, down_t, up, slope, normed, gain),
        [tall(channels), whole(down_t.shape), whole(up.shape), tall(hidden), tall(channels), whole(gain.shape)],
        [
            shape_of((hidden, lanes)),
            shape_of((count // 2, own, lanes)),
            shape_of((count // 2, own, lanes)),
            shape_of((8, lanes), f32),
        ],
        [tall(hidden), half, half, tall(8)],
        micros=28,
        earlier=earlier,
        through=through,
    )


def dealt_halves(size, patchs, columns, bn):
    half = pl.BlockSpec((patchs // 2, size, bn), lambda j, _: (0, 0, 0))

    def deal_columns(product, stack_ref, refs, mine):
        stack_ref[...] = product.astype(bf16).reshape(patchs, size, bn)
        for part in range(2):

            @pl.when(pl.program_id(0) == part)
            def _(part=part):
                deal(stack_ref, refs[2 * part], refs[2 * part + 1], mine)

    return [half] * 4, [shape_of((patchs // 2, size, columns // 2))] * 4, deal_columns


def down_gradient(parts, act, patchs, ids):
    count = len(parts)
    own, lanes = parts[0].shape
    channels = own * count
    hidden = act.shape[0]
    bn = hidden // 2
    size = channels // patchs
    specs, shapes, deal_columns = dealt_halves(size, patchs, hidden, bn)

    def kernel(ids_ref, *refs):
        part_refs = refs[:count]
        b_ref, d_ref, *out_refs, o_ref = refs[count:]

        @pl.when(pl.program_id(0) == 0)
        def _():
            for offset, part in enumerate(part_refs):
                d_ref[pl.ds(pl.multiple_of((ids_ref[0] ^ offset) * own, 16), own), :] = part[...]

        deal_columns(mm_nt(d_ref[...], b_ref[...]), o_ref, out_refs, ids_ref[1] & 1)

    return call(
        kernel,
        ids,
        (2,),
        (*parts, act),
        [whole(parts[0].shape)] * count + [pl.BlockSpec((bn, lanes), lambda j, _: (j, 0))],
        [shape_of((channels, lanes))] + shapes,
        [whole((channels, lanes))] + specs,
        [pltpu.VMEM((patchs, size, bn), bf16)],
        micros=18,
    )


def weight_gradient(a, b, patchs, ids):
    rows, depth = a.shape
    columns = b.shape[0]
    bn = columns // 2
    size = rows // patchs
    specs, shapes, deal_columns = dealt_halves(size, patchs, columns, bn)

    def kernel(ids_ref, a_ref, b_ref, *refs):
        deal_columns(mm_nt(a_ref[...], b_ref[...]), refs[-1], refs[:-1], ids_ref[1] & 1)

    return call(
        kernel,
        ids,
        (2,),
        (a, b),
        [whole(a.shape), pl.BlockSpec((bn, depth), lambda j, _: (j, 0))],
        shapes,
        specs,
        [pltpu.VMEM((patchs, size, bn), bf16)],
        micros=18,
    )


def pool_forward(keep, got, conv_flat, scale, images, band, chans, ids, earlier=(), through=()):
    own, lanes = keep.shape
    cells = lanes // images
    table = pool_table()
    tokens = table.shape[0]
    reach = band + 2 * GRID
    padded = jnp.asarray(np.pad(table, ((GRID, GRID), (0, 0))))

    def kernel(ids_ref, keep_ref, got_ref, c_ref, scale_ref, t_ref, p_ref, branch_ref, result_ref, pooled_ref, *pieces):
        branch = keep_ref[...].astype(f32) + got_ref[...].astype(f32)
        branch_ref[...] = branch.astype(bf16)
        result = (c_ref[...].astype(f32) + scale_ref[...] * branch).astype(bf16)
        result_ref[...] = result
        pooled_ref[0] = mm(result, t_ref[...]).astype(bf16)
        for offset, piece in enumerate(pieces):
            start = pl.multiple_of((ids_ref[0] ^ offset) * band, 8)
            rows = p_ref[pl.ds(start, reach), :].astype(bf16)
            piece[0] = mm_nt(rows, result).astype(bf16)

    flat = pl.BlockSpec((own, cells), lambda i, _: (0, i))
    return call(
        kernel,
        ids,
        (images,),
        (keep, got, conv_flat, scale, jnp.asarray(table.T.astype(bf16)), padded),
        [flat, flat, flat, whole(scale.shape), whole((cells, tokens)), whole(padded.shape)],
        [shape_of((own, lanes))] * 2
        + [shape_of((images, own, tokens))]
        + [shape_of((images, reach, own))] * chans,
        [flat, flat, pl.BlockSpec((1, own, tokens), lambda i, _: (i, 0, 0))]
        + [pl.BlockSpec((1, reach, own), lambda i, _: (i, 0, 0))] * chans,
        micros=9,
        earlier=earlier,
        through=through,
    )


def row_moves(field, spots, step):
    if step == 0:
        return field
    count = field.shape[0]
    moved = pltpu.roll(field, (-step) % count, 0)
    column = spots % GRID + step
    return jnp.where((column >= 0) & (column < GRID), moved, 0.0)


def adapter(pieces, w_proj, kernel_three, gate_in, gate_out, d_band, ids, earlier=(), through=()):
    chans = len(pieces)
    images, reach, own = pieces[0].shape
    width = w_proj.shape[1]
    gate = gate_in.shape[1]
    band = reach - 2 * GRID

    def kernel(ids_ref, *refs):
        piece_refs = refs[:chans]
        proj_ref, k_ref, in_ref, out_ref, d_ref, gs_ref, ds_ref, gib_ref, gob_ref, gk_ref, gi_ref, go_ref = refs[chans:]
        me = ids_ref[0]

        @pl.when(pl.program_id(0) == 0)
        def _():
            gi_ref[...] = jnp.zeros_like(gi_ref)
            go_ref[...] = jnp.zeros_like(go_ref)
            gk_ref[...] = jnp.zeros_like(gk_ref)

        field = None
        for offset, piece in enumerate(piece_refs):
            start = pl.multiple_of((me ^ offset) * own, 16)
            term = mm(piece[0], proj_ref[pl.ds(start, own), :])
            field = term if field is None else field + term
        field = field.astype(bf16).astype(f32)
        spots = lax.broadcasted_iota(jnp.int32, (reach, 1), 0)
        moved = [row_moves(field, spots, step) for step in (-1, 0, 1)]
        smooth = None
        for t in range(9):
            term = k_ref[t : t + 1, :] * moved[t % 3][GRID * (t // 3) : GRID * (t // 3) + band]
            smooth = term if smooth is None else smooth + term
        rows = smooth.astype(bf16)
        act, slope = gelu_both(mm(rows, in_ref[...]))
        act = act.astype(bf16)
        value = jnp.tanh(mm(act, out_ref[...]))
        gs_ref[0] = value * smooth
        d = d_ref[0].astype(f32)
        d_logit = (d * smooth * (1.0 - value * value)).astype(bf16)
        d_gate = (mm_nt(d_logit, out_ref[...]) * slope).astype(bf16)
        d_smooth = d * value + mm_nt(d_gate, in_ref[...])
        ds_ref[0] = d_smooth.astype(bf16)
        go_ref[...] += mm_tn(act, d_logit)
        gi_ref[...] += mm_tn(rows, d_gate)
        for t in range(9):
            seen = moved[t % 3][GRID * (t // 3) : GRID * (t // 3) + band]
            gk_ref[t : t + 1, :] += jnp.sum(d_smooth * seen, axis=0, keepdims=True)

        @pl.when(pl.program_id(0) == images - 1)
        def _():
            gib_ref[...] = gi_ref[...].astype(bf16)
            gob_ref[...] = go_ref[...].astype(bf16)

    per = lambda rows, cols: pl.BlockSpec((1, rows, cols), lambda i, _: (i, 0, 0))
    kept = lambda *shape: pl.BlockSpec(shape, lambda i, _: (0, 0))
    return call(
        kernel,
        ids,
        (images,),
        (*pieces, w_proj, kernel_three, gate_in, gate_out, d_band),
        [per(reach, own)] * chans
        + [whole(w_proj.shape), whole(kernel_three.shape), whole(gate_in.shape), whole(gate_out.shape), per(band, width)],
        [
            shape_of((images, band, width), f32),
            shape_of((images, band, width)),
            shape_of((width, gate)),
            shape_of((gate, width)),
            shape_of((16, width), f32),
        ],
        [per(band, width), per(band, width), kept(width, gate), kept(gate, width), kept(16, width)],
        [pltpu.VMEM((width, gate), f32), pltpu.VMEM((gate, width), f32)],
        micros=13,
        earlier=earlier,
        through=through,
    )


def adapter_back(parts, w_own, kernel_three, pooled, d_out, branch, scale, ids, earlier=(), through=()):
    chans = len(parts)
    images, band, width = parts[0].shape
    own, lanes = d_out.shape
    cells = lanes // images
    tokens = band * chans
    table = jnp.asarray(pool_table().astype(bf16))

    def kernel(ids_ref, *refs):
        part_refs = refs[:chans]
        w_ref, k_ref, pooled_ref, do_ref, branch_ref, scale_ref, t_ref, dr_ref, db_ref, gpb_ref, gs_ref, f_ref, gp_ref = refs[chans:]
        me = ids_ref[0]

        @pl.when(pl.program_id(0) == 0)
        def _():
            gp_ref[...] = jnp.zeros_like(gp_ref)
            gs_ref[...] = jnp.zeros_like(gs_ref)
            f_ref[:GRID] = jnp.zeros((GRID, width), f32)
            f_ref[GRID + tokens :] = jnp.zeros((GRID, width), f32)

        for offset, part in enumerate(part_refs):
            start = pl.multiple_of((me ^ offset) * band + GRID, 8)
            f_ref[pl.ds(start, band), :] = part[0].astype(f32)
        field = f_ref[...]
        spots = lax.broadcasted_iota(jnp.int32, (tokens + 2 * GRID, 1), 0)
        moved = [row_moves(field, spots, -step) for step in (-1, 0, 1)]
        d_adapted = None
        for t in range(9):
            start = GRID * (2 - t // 3)
            term = k_ref[t : t + 1, :] * moved[t % 3][start : start + tokens]
            d_adapted = term if d_adapted is None else d_adapted + term
        d_adapted = d_adapted.astype(bf16)
        d_pooled = mm_nt(w_ref[...], d_adapted).astype(bf16)
        gp_ref[...] += mm(pooled_ref[0], d_adapted)
        d_result = do_ref[...].astype(f32) + mm(d_pooled, t_ref[...])
        dr_ref[...] = d_result
        db_ref[...] = (scale_ref[...] * d_result).astype(bf16)
        gs_ref[...] += jnp.sum(d_result * branch_ref[...].astype(f32), axis=1, keepdims=True)

        @pl.when(pl.program_id(0) == images - 1)
        def _():
            gpb_ref[...] = gp_ref[...].astype(bf16)

    flat = pl.BlockSpec((own, cells), lambda i, _: (0, i))
    per = lambda rows, cols: pl.BlockSpec((1, rows, cols), lambda i, _: (i, 0, 0))
    return call(
        kernel,
        ids,
        (images,),
        (*parts, w_own, kernel_three, pooled, d_out, branch, scale, table),
        [per(band, width)] * chans
        + [whole(w_own.shape), whole(kernel_three.shape), per(own, tokens), flat, flat, whole(scale.shape), whole(table.shape)],
        [
            shape_of((own, lanes), f32),
            shape_of((own, lanes)),
            shape_of((own, width)),
            shape_of((own, 128), f32),
        ],
        [flat, flat, pl.BlockSpec((own, width), lambda i, _: (0, 0)), pl.BlockSpec((own, 128), lambda i, _: (0, 0))],
        [pltpu.VMEM((tokens + 2 * GRID, width), f32), pltpu.VMEM((own, width), f32)],
        micros=14,
        earlier=earlier,
        through=through,
    )


def row_standard(values):
    center = values - jnp.mean(values, axis=-1, keepdims=True)
    inverse = lax.rsqrt(jnp.mean(center * center, axis=-1, keepdims=True) + vit_eps)
    return center * inverse


def stack_bands(stack_ref, values):
    count, band, _ = stack_ref.shape
    for b in range(count):
        stack_ref[b] = values[b * band : (b + 1) * band].astype(bf16)


def take_bands(rows_ref, part_refs, me):
    for offset, part in enumerate(part_refs):
        band = part.shape[1]
        start = pl.multiple_of((me ^ offset) * band, 8)
        rows_ref[pl.ds(start, band), :] = part[0].astype(f32)
    return rows_ref[...].astype(bf16)


def attention_forward(x, gain, w_qkv, w_attn, chans, ids, earlier=(), through=()):
    images, tokens, width = x.shape
    own = w_qkv.shape[2]
    heads = own // HEAD_DIM
    band = tokens // chans
    scale = 1.0 / math.sqrt(HEAD_DIM)

    def kernel(ids_ref, x_ref, gain_ref, qkv_w_ref, attn_ref, n_ref, qkv_ref, o_ref, log_ref, keep_ref, send_ref, stack_ref):
        normed = (row_standard(x_ref[0].astype(f32)) * gain_ref[...]).astype(bf16)
        n_ref[0] = normed
        q, k, v = (mm(normed, qkv_w_ref[t]).astype(bf16) for t in range(3))
        for t, part in enumerate((q, k, v)):
            qkv_ref[t, 0] = part
        mixed = []
        spot = lax.broadcasted_iota(jnp.int32, (tokens, 128), 1)
        logs = jnp.zeros((tokens, 128), f32)
        for h in range(heads):
            at = slice(h * HEAD_DIM, (h + 1) * HEAD_DIM)
            scores = mm_nt(q[:, at], k[:, at]) * scale
            most = jnp.max(scores, axis=-1, keepdims=True)
            powers = jnp.exp(scores - most)
            total = jnp.sum(powers, axis=-1, keepdims=True)
            logs = jnp.where(spot == h, most + jnp.log(total), logs)
            mixed.append(mm((powers * (1.0 / total)).astype(bf16), v[:, at]).astype(bf16))
        mixed = jnp.concatenate(mixed, axis=1)
        log_ref[0] = logs
        o_ref[0] = mixed
        stack_bands(stack_ref, mm_nt(mixed, attn_ref[...]))
        deal(stack_ref, keep_ref, send_ref, ids_ref[0] & 1, (0,))

    per = lambda cols: pl.BlockSpec((1, tokens, cols), lambda i, _: (i, 0, 0))
    half = pl.BlockSpec((chans // 2, 1, band, width), lambda i, _: (0, i, 0, 0))
    return call(
        kernel,
        ids,
        (images,),
        (x, gain, w_qkv, w_attn),
        [per(width), whole(gain.shape), whole(w_qkv.shape), whole(w_attn.shape)],
        [
            shape_of((images, tokens, width)),
            shape_of((3, images, tokens, own)),
            shape_of((images, tokens, own)),
            shape_of((images, tokens, 128), f32),
            shape_of((chans // 2, images, band, width)),
            shape_of((chans // 2, images, band, width)),
        ],
        [per(width), pl.BlockSpec((3, 1, tokens, own), lambda i, _: (0, i, 0, 0)), per(own), per(128), half, half],
        [pltpu.VMEM((chans, band, width), bf16)],
        micros=16,
        earlier=earlier,
        through=through,
    )


def feed_forward(parts, d_rows, w_up, w_down, patchs, ids, earlier=(), through=()):
    chans = len(parts)
    images, band, width = parts[0].shape
    tokens = band * chans
    hidden = w_up.shape[1]

    def kernel(ids_ref, *refs):
        part_refs = refs[:chans]
        (
            d_ref, up_ref, down_ref, keep_ref, send_ref, dkeep_ref, dsend_ref, *grad_refs,
            rows_ref, stack_ref, gu_ref, gd_ref, g_ref,
        ) = refs[chans:]
        me = ids_ref[0]
        step = pl.program_id(0)
        normed = take_bands(rows_ref, part_refs, me)
        act, slope = gelu_both(mm(normed, up_ref[...]))
        act = act.astype(bf16)
        stack_bands(stack_ref, mm_nt(act, down_ref[...]))
        deal(stack_ref, keep_ref, send_ref, me & 1, (0,))
        d = d_ref[0]
        d_pre = (mm(d, down_ref[...]) * slope).astype(bf16)
        stack_bands(stack_ref, mm_nt(d_pre, up_ref[...]))
        deal(stack_ref, dkeep_ref, dsend_ref, me & 1, (0,))
        gu = mm_tn(normed, d_pre)
        gd = mm_tn(d, act)

        @pl.when(step == 0)
        def _():
            gu_ref[...] = gu
            gd_ref[...] = gd

        @pl.when(step > 0)
        def _():
            gu_ref[...] += gu
            gd_ref[...] += gd

        @pl.when(step == images - 1)
        def _():
            for part in range(4):
                source = (gu_ref, gd_ref)[part // 2]
                columns = slice((part % 2) * part_width, (part % 2 + 1) * part_width)
                for b in range(patchs):
                    g_ref[b] = source[b * size : (b + 1) * size, columns].astype(bf16)
                deal(g_ref, grad_refs[2 * part], grad_refs[2 * part + 1], ids_ref[1] & 1)

    per = lambda rows: pl.BlockSpec((1, rows, width), lambda i, _: (i, 0, 0))
    half = pl.BlockSpec((chans // 2, 1, band, width), lambda i, _: (0, i, 0, 0))
    halves = shape_of((chans // 2, images, band, width))
    size = width // patchs
    part_width = hidden // 2
    grads = (patchs // 2, size, part_width)
    return call(
        kernel,
        ids,
        (images,),
        (*parts, d_rows, w_up, w_down),
        [per(band)] * chans + [per(tokens), whole(w_up.shape), whole(w_down.shape)],
        [halves] * 4 + [shape_of(grads)] * 8,
        [half] * 4 + [pl.BlockSpec(grads, lambda i, _: (0, 0, 0))] * 8,
        [
            pltpu.VMEM((tokens, width), f32),
            pltpu.VMEM((chans, band, width), bf16),
            pltpu.VMEM((width, hidden), f32),
            pltpu.VMEM((width, hidden), f32),
            pltpu.VMEM((patchs, size, part_width), bf16),
        ],
        micros=26,
        earlier=earlier,
        through=through,
    )


def attention_backward(parts, normed, qkv, mixed, logs, w_qkv, w_attn, patchs, ids, earlier=(), through=()):
    chans = len(parts)
    images, band, width = parts[0].shape
    tokens = band * chans
    own = w_attn.shape[1]
    heads = own // HEAD_DIM
    scale = 1.0 / math.sqrt(HEAD_DIM)

    def kernel(ids_ref, *refs):
        part_refs = refs[:chans]
        (
            n_ref, qkv_ref, o_ref, log_ref, qkv_w_ref, attn_ref, keep_ref, send_ref, gkeep_ref, gsend_ref,
            rows_ref, stack_ref, acc_ref, g_ref,
        ) = refs[chans:]
        me = ids_ref[0]
        step = pl.program_id(0)
        d = take_bands(rows_ref, part_refs, me)
        d_mixed = mm(d, attn_ref[...]).astype(bf16)
        q, k, v = (qkv_ref[t, 0] for t in range(3))
        grads = ([], [], [])
        for h in range(heads):
            at = slice(h * HEAD_DIM, (h + 1) * HEAD_DIM)
            soft = jnp.exp(mm_nt(q[:, at], k[:, at]) * scale - log_ref[0, :, h : h + 1])
            d_soft = mm_nt(d_mixed[:, at], v[:, at])
            across = jnp.sum(d_soft * soft, axis=-1, keepdims=True)
            d_scores = (soft * (d_soft - across)).astype(bf16)
            grads[0].append((mm(d_scores, k[:, at]) * scale).astype(bf16))
            grads[1].append((mm_tn(d_scores, q[:, at]) * scale).astype(bf16))
            grads[2].append(mm_tn(soft.astype(bf16), d_mixed[:, at]).astype(bf16))
        grads = [jnp.concatenate(v, axis=1) for v in grads]
        total = None
        for t in range(3):
            term = mm_nt(grads[t], qkv_w_ref[t])
            total = term if total is None else total + term
        stack_bands(stack_ref, total)
        deal(stack_ref, keep_ref, send_ref, me & 1, (0,))
        new = [mm_tn(n_ref[0], g) for g in grads] + [mm_tn(d, o_ref[0])]

        @pl.when(step == 0)
        def _():
            for t in range(4):
                acc_ref[:, t * own : (t + 1) * own] = new[t]

        @pl.when(step > 0)
        def _():
            for t in range(4):
                acc_ref[:, t * own : (t + 1) * own] += new[t]

        @pl.when(step == images - 1)
        def _():
            for b in range(patchs):
                g_ref[b] = acc_ref[b * size : (b + 1) * size].astype(bf16)
            deal(g_ref, gkeep_ref, gsend_ref, ids_ref[1] & 1)

    per = lambda rows, cols: pl.BlockSpec((1, rows, cols), lambda i, _: (i, 0, 0))
    half = pl.BlockSpec((chans // 2, 1, band, width), lambda i, _: (0, i, 0, 0))
    halves = shape_of((chans // 2, images, band, width))
    size = width // patchs
    out = (patchs // 2, size, 4 * own)
    return call(
        kernel,
        ids,
        (images,),
        (*parts, normed, qkv, mixed, logs, w_qkv, w_attn),
        [per(band, width)] * chans
        + [
            per(tokens, width),
            pl.BlockSpec((3, 1, tokens, own), lambda i, _: (0, i, 0, 0)),
            per(tokens, own),
            per(tokens, 128),
            whole(w_qkv.shape),
            whole(w_attn.shape),
        ],
        [halves] * 2 + [shape_of(out)] * 2,
        [half] * 2 + [pl.BlockSpec(out, lambda i, _: (0, 0, 0))] * 2,
        [
            pltpu.VMEM((tokens, width), f32),
            pltpu.VMEM((chans, band, width), bf16),
            pltpu.VMEM((width, 4 * own), f32),
            pltpu.VMEM((patchs, size, 4 * own), bf16),
        ],
        micros=24,
        earlier=earlier,
        through=through,
    )


def standardize(values, epsilon):
    center = values - jnp.mean(values, axis=-1, keepdims=True)
    inverse = lax.rsqrt(jnp.mean(center * center, axis=-1, keepdims=True) + epsilon)
    return center * inverse, inverse


def norm_back(grad, gain, unit, inverse):
    scaled = grad * gain
    return inverse * (
        scaled
        - jnp.mean(scaled, axis=-1, keepdims=True)
        - unit * jnp.mean(scaled * unit, axis=-1, keepdims=True)
    )


def body(
    vit_in,
    conv_in,
    ln_one,
    w_qkv,
    w_attn,
    ln_two,
    w_up,
    w_down,
    conv_kernel,
    conv_gain,
    conv_up,
    conv_down,
    layer_scale,
    w_proj,
    adapter_kernel,
    gate_in,
    gate_out,
    d_merged,
    d_conv_out,
):
    chans = lax.axis_size("chan")
    patchs = lax.axis_size("patch")
    me = lax.axis_index("chan")
    ids = jnp.stack([me, lax.axis_index("patch")]).astype(jnp.int32)
    tokens, images, width = vit_in.shape
    band = tokens // chans
    own_channels, _, cells = conv_in.shape
    channels = own_channels * chans
    lanes = images * cells
    hidden = w_up.shape[1]
    own_width = w_attn.shape[1]

    def own_rows(values, size):
        return lax.dynamic_slice_in_dim(values, me * size, size, 0)

    def own_band(values):
        return lax.dynamic_slice_in_dim(values, me * band, band, 0).swapaxes(0, 1)

    places = [(p * chans + c, c * patchs + p) for p in range(patchs) for c in range(chans)]

    def placed(values):
        return lax.ppermute(values, ("patch", "chan"), places)

    everywhere = patchs * chans
    rows = own_channels // patchs

    def share(shares, kind):
        flat = [v.astype(kind).reshape(chans, patchs, -1) for v in shares]
        flat = jnp.concatenate(flat, axis=2)
        flat = jnp.pad(flat, ((0, 0), (0, 0), (0, -flat.shape[2] % (rows * 128))))
        flat = flat.reshape(chans, patchs, rows, -1)
        return halving_order(flat, "chan")

    def unshare(values, shares):
        flat = values.reshape(-1)
        out = []
        for v in shares:
            size = v.size // everywhere
            out.append(flat[:size].reshape((v.shape[0] // everywhere,) + v.shape[1:]).astype(f32))
            flat = flat[size:]
        return out

    def summed(pair):
        return pair[0].astype(f32) + pair[1].astype(f32)

    top = 1 << (bit_count(chans) - 1)

    conv_flat = conv_in.reshape(own_channels, lanes)
    weights = tap_weights(own_rows(conv_kernel, own_channels))
    mapped = depthwise(conv_flat, weights)

    gain_one = ln_one.astype(f32)[None]
    gain_two = ln_two.astype(f32)[None]
    w_three = w_qkv.swapaxes(0, 1)

    def attend():
        normed, qkv, mixed, logs, keep, send = attention_forward(
            vit_in.swapaxes(0, 1), gain_one, w_three, w_attn, chans, ids
        )
        pair = fold(keep, swap(send, "chan", 1), "chan", 0)
        return (normed, qkv, mixed, logs), pair, plain(conv_up.T)

    ((normed_one, qkv, mixed, logs), (keep, send), conv_up_t), (far,) = beside(attend, [(mapped, "chan", top)])
    mapped_parts = parts_beside(mapped, far)

    gain_all = conv_gain.astype(f32)[:, None]
    (conv_norm, conv_act, conv_slope, stats, conv_keep, conv_send), (got,) = beside(
        lambda: conv_forward(mapped_parts, conv_up_t, conv_down, gain_all, ids), [(send, "chan", 2)]
    )
    vit_band = own_band(vit_in).astype(f32)
    middle = vit_band + summed(finish(keep, got, "chan", 1))
    unit_two, inverse_two = standardize(middle, vit_eps)
    normed_band = (unit_two * gain_two).astype(bf16)
    ((conv_keep, conv_send), d_rows), (far,) = beside(
        lambda: (fold(conv_keep, swap(conv_send, "chan", 1), "chan", 0), plain(d_merged.swapaxes(0, 1))),
        [(normed_band, "chan", top)],
    )
    normed_parts = parts_beside(normed_band, far)

    def forward():
        out_keep, out_send, keep, send, *grads = feed_forward(
            normed_parts, d_rows, w_up, w_down, patchs, ids
        )
        out = fold(out_keep, swap(out_send, "chan", 1), "chan", 0)
        return out, fold(keep, swap(send, "chan", 1), "chan", 0), grads

    ((out_keep, out_send), (keep, send), grads), (got,) = beside(
        forward, [(conv_send, "chan", 2)]
    )

    own_scale = own_rows(layer_scale, own_channels).astype(f32)[:, None]
    conv_sum = finish(conv_keep, got, "chan", 1)
    vit = list(zip(grads[::2], grads[1::2]))
    (branch_maps, conv_result, pooled, *pieces), (got, vit_0) = beside(
        lambda: pool_forward(*conv_sum, conv_flat, own_scale, images, band, chans, ids),
        [(send, "chan", 2), (vit[0][1], "patch", 1)],
    )

    d_band = own_band(d_merged)
    d_two = finish(keep, got, "chan", 1)

    d_normed_two = summed(d_two)
    d_middle = d_band.astype(f32) + norm_back(d_normed_two, gain_two, unit_two, inverse_two)
    d_attended = d_middle.astype(bf16)
    g_ln_two = jnp.sum(d_normed_two * unit_two, axis=(0, 1))
    (w_own, conv_down_t, d_out), (vit_1, *got) = beside(
        lambda: (
            own_rows(w_proj, own_channels),
            plain(conv_down.T),
            plain(d_conv_out.reshape(own_channels, lanes)),
        ),
        [(vit[1][1], "patch", 1)] + [(pieces[offset], "chan", offset) for offset in range(1, chans)],
    )
    pieces[1:] = got

    kernel_three = jnp.pad(adapter_kernel.astype(f32).T, ((0, 7), (0, 0)))
    (gated, d_smooth, g_gate_in, g_gate_out, g_adapter), (far, vit_2) = beside(
        lambda: adapter(pieces, w_proj, kernel_three, gate_in, gate_out, d_band, ids),
        [(d_attended, "chan", top), (vit[2][1], "patch", 1)],
    )
    d_parts = parts_beside(d_attended, far)
    shares = [g_gate_in, g_gate_out, g_adapter[:9].T, g_ln_two]
    (shared_keep, shared_send), (far, vit_3) = beside(
        lambda: halves(share(shares, bf16), "chan"), [(d_smooth, "chan", top), (vit[3][1], "patch", 1)]
    )
    smooth_parts = parts_beside(d_smooth, far)

    (d_result, d_branch, g_proj, g_scale), (got, shared_got) = beside(
        lambda: adapter_back(
            smooth_parts, w_own, kernel_three, pooled, d_out, branch_maps, own_scale, ids
        ),
        [(out_send, "chan", 2), (shared_send, "chan", 1)],
    )
    shared = shared_keep + shared_got
    out_sum = finish(out_keep, got, "chan", 1)
    merged = (middle + summed(out_sum) + gated).astype(bf16)

    vit_keep, vit_send = (
        jnp.concatenate(v, axis=2)
        for v in zip(*(fold(vit[q][0], v, "patch", 0) for q, v in enumerate((vit_0, vit_1, vit_2, vit_3))))
    )
    shared_keep, shared_send = halves_at(shared, "chan", 1)

    def attend_back():
        keep, send, *grads = attention_backward(
            d_parts, normed_one, qkv, mixed, logs, w_three, w_attn, patchs, ids
        )
        return fold(keep, swap(send, "chan", 1), "chan", 0), grads

    ((keep, send), (att_keep, att_send)), (far, vit_got) = beside(
        attend_back, [(d_branch, "chan", top), (vit_send, "patch", 2)]
    )
    vit_keep, vit_send = fold(vit_keep, vit_got, "patch", 1)
    branch_parts = parts_beside(d_branch, far)

    (d_all, *down), (one_got, att_got, vit_got, shared_got) = beside(
        lambda: down_gradient(branch_parts, conv_act, patchs, ids),
        [
            (send, "chan", 2),
            (att_send, "patch", 1),
            (vit_send, "patch", 4),
            (shared_send, "chan", 2),
        ],
    )
    one_keep = keep
    vit_sum = finish(vit_keep, vit_got, "patch", 2)
    att_keep, att_send = fold(att_keep, att_got, "patch", 0)
    shared = sum_scatter(shared_keep + shared_got, "chan", 2).reshape(own_channels, -1)
    early = jnp.concatenate([g_proj, shared], axis=1).reshape(patchs, rows, -1)
    early_keep, early_send = halves(halving_order(early, "patch"), "patch")

    (d_pre, conv_keep, conv_send, sums), (first_got, early_got, att_got) = beside(
        lambda: conv_backward(d_all, conv_down_t, conv_up, conv_slope, conv_norm, gain_all, ids),
        [(down[1], "patch", 1), (early_send, "patch", 1), (att_send, "patch", 2)],
    )
    att_keep, att_send = fold(att_keep, att_got, "patch", 1)

    def dealt():
        got = swap(conv_send, "chan", 1)
        keep, _ = fold(conv_keep, got, "chan", 0)
        sends = [fold(v[..., : lanes // 2], w[..., : lanes // 2], "chan", 0)[1] for v, w in ((conv_keep, got),)]
        sends += [fold(v[..., lanes // 2 :], w[..., lanes // 2 :], "chan", 0)[1] for v, w in ((conv_keep, got),)]
        first = fold(down[0], first_got, "patch", 0)
        return keep, sends, first, sums + swap(sums, "chan", 1), fold(early_keep, early_got, "patch", 0)

    (conv_keep, sends, (first_keep, first_send), sums, (early_keep, early_send)), (att_got,) = beside(
        dealt, [(att_send, "patch", 4)]
    )
    att_sum = finish(att_keep, att_got, "patch", 2)
    up, (near_got, sums_got, second_got, first_got, early_got) = beside(
        lambda: weight_gradient(conv_norm, d_pre, patchs, ids),
        [
            (sends[0], "chan", 2),
            (sums, "chan", 2),
            (down[3], "patch", 1),
            (first_send, "patch", 2),
            (early_send, "patch", 2),
        ],
    )
    first_keep, first_send = fold(first_keep, first_got, "patch", 1)
    second_keep, second_send = fold(down[2], second_got, "patch", 0)

    def back_one():
        d_normed_one = summed(finish(one_keep, one_got, "chan", 1))
        unit_one, inverse_one = standardize(vit_band, vit_eps)
        g_vit = d_middle + norm_back(d_normed_one, gain_one, unit_one, inverse_one)
        return (
            g_vit.astype(bf16),
            halves(share([jnp.sum(d_normed_one * unit_one, axis=(0, 1))], f32), "chan"),
            fold(early_keep, early_got, "patch", 1),
            sum_all(sums + sums_got, "chan", 2) * (1.0 / channels),
        )

    (g_vit, (one_keep, one_send), (early_keep, early_send), sums), (far_got, third_got, first_got, second_got) = beside(
        back_one,
        [
            (sends[1], "chan", 2),
            (up[1], "patch", 1),
            (first_send, "patch", 4),
            (second_send, "patch", 2),
        ],
    )
    first_sum = finish(first_keep, first_got, "patch", 2)
    second_keep, second_send = fold(second_keep, second_got, "patch", 1)
    third_keep, third_send = fold(up[0], third_got, "patch", 0)
    keep_near, keep_far = conv_keep[..., : lanes // 2], conv_keep[..., lanes // 2 :]
    (near, near_got), (far, far_got) = (
        finish(keep_near, near_got, "chan", 1), finish(keep_far, far_got, "chan", 1)
    ) if chans > 4 else ((conv_keep[0], near_got[0]), (None, far_got[0]))

    own_gain = own_rows(conv_gain, own_channels).astype(f32)[:, None]
    conv_sum = near if far is None else jnp.concatenate([near, far], axis=1)
    (g_conv_in, g_kernel, g_gain), (fourth_got, second_got, third_got, early_got, vit_far, one_got) = beside(
        lambda: depthwise_back(
            conv_sum, near_got, far_got, mapped, stats, sums, own_gain, conv_flat, weights, d_result, images
        ),
        [
            (up[3], "patch", 1),
            (second_send, "patch", 4),
            (third_send, "patch", 2),
            (early_send, "patch", 4),
            (g_vit, "chan", top),
            (one_send, "chan", 1),
        ],
    )
    second_sum = finish(second_keep, second_got, "patch", 2)
    third_keep, third_send = fold(third_keep, third_got, "patch", 1)
    fourth_keep, fourth_send = fold(up[2], fourth_got, "patch", 0)
    early = summed(finish(early_keep, early_got, "patch", 2)).astype(bf16)
    shared_one = sum_scatter(one_keep + one_got, "chan", 1).reshape(own_channels, -1)
    late = jnp.concatenate([g_kernel, g_gain[:, None], g_scale[:, :78], shared_one], axis=1)
    late = halving_order(late.reshape(patchs, rows, -1), "patch")
    late_keep, late_send = halves(late, "patch")

    def place_rows():
        whole_rows = jnp.zeros((tokens, images, width), f32)
        for offset, part in enumerate(parts_beside(g_vit, vit_far)):
            whole_rows = lax.dynamic_update_slice_in_dim(
                whole_rows, part.swapaxes(0, 1).astype(f32), (me ^ offset) * band, 0
            )
        return whole_rows

    finals = lambda: (summed(vit_sum), summed(att_sum), conv_result.reshape(conv_in.shape))
    (vit_grads, att_grads, conv_out), (fourth_got, third_got, late_got, own_early) = beside(
        finals,
        [
            (fourth_send, "patch", 2),
            (third_send, "patch", 4),
            (late_send, "patch", 1),
            (early, ("patch", "chan"), places),
        ],
    )
    g_vit_in = place_rows()
    fourth_keep, fourth_send = fold(fourth_keep, fourth_got, "patch", 1)
    third_sum = finish(third_keep, third_got, "patch", 2)
    late = late_keep + late_got

    def last():
        total = placed(sum_scatter(late, "patch", 1))
        return total, jnp.concatenate([summed(first_sum), summed(second_sum)], axis=1)

    (own_late, g_conv_down), (fourth_got,) = beside(last, [(fourth_send, "patch", 4)])
    fourth_sum = finish(fourth_keep, fourth_got, "patch", 2)
    g_conv_up = jnp.concatenate([summed(third_sum), summed(fourth_sum)], axis=1)
    g_proj = own_early[:, :width].astype(f32)
    g_gate_in, g_gate_out, g_adapter, g_ln_two = unshare(own_early[:, width:], shares)
    (g_ln_one,) = unshare(own_late[:, 128:], [ln_one])
    qkv_width = 3 * own_width
    return (
        merged.swapaxes(0, 1),
        conv_out,
        g_vit_in,
        g_conv_in,
        g_ln_one,
        att_grads[:, :qkv_width].reshape(-1, 3, own_width),
        att_grads[:, qkv_width:],
        g_ln_two,
        vit_grads[:, :hidden],
        vit_grads[:, hidden:],
        own_late[:, :49],
        own_late[:, 49],
        g_conv_up,
        g_conv_down,
        own_late[:, 50],
        g_proj,
        g_adapter,
        g_gate_in,
        g_gate_out,
    )


def solution(mesh):
    in_specs = (
        P(None, "patch", None),
        P("chan", "patch", None),
        P(),
        P(None, None, "chan"),
        P(None, "chan"),
        P(),
        P(None, "chan"),
        P(None, "chan"),
        P(),
        P(),
        P(None, "chan"),
        P(None, "chan"),
        P(),
        P(),
        P(),
        P(),
        P(),
        P(None, "patch", None),
        P("chan", "patch", None),
    )
    out_specs = (
        P("chan", "patch", None),
        P("chan", "patch", None),
        P(None, "patch", None),
        P("chan", "patch", None),
        P(("patch", "chan")),
        P("patch", None, "chan"),
        P("patch", "chan"),
        P(("patch", "chan")),
        P("patch", "chan"),
        P("patch", "chan"),
        P(("patch", "chan"), None),
        P(("patch", "chan")),
        P("patch", "chan"),
        P("patch", "chan"),
        P(("patch", "chan")),
        P(("patch", "chan"), None),
        P(("patch", "chan"), None),
        P(("patch", "chan"), None),
        P(("patch", "chan"), None),
    )
    return jax.shard_map(body, mesh=mesh, in_specs=in_specs, out_specs=out_specs, check_vma=False)
```

```python
import math

import jax
import jax.numpy as jnp
import numpy as np
from jax import lax
from jax.experimental import pallas as pl
from jax.experimental.layout import Layout, with_layout_constraint
from jax.experimental.pallas import tpu as pltpu
from jax.sharding import PartitionSpec as P

HEAD_DIM = 64
GRID = 24
MAP = 32
TAPS = 7
GROUP = 32
WIDE = 256

vit_eps = 1e-05
conv_eps = 1e-06
f32 = jnp.float32
bf16 = jnp.bfloat16
MIB = 2**20


def block_of(size, most, unit):
    best = unit
    for candidate in range(unit, most + 1, unit):
        if size % candidate == 0:
            best = candidate
    return best if size % best == 0 else size


def bit_count(size):
    return size.bit_length() - 1


def reverse_bits(value, bits):
    return sum(((value >> k) & 1) << (bits - 1 - k) for k in range(bits))


def swap(values, axis, other):
    count = lax.axis_size(axis)
    return lax.ppermute(values, axis, [(i, i ^ other) for i in range(count)])


def move(values, axis, other):
    return swap(values, axis, other) if isinstance(other, int) else lax.ppermute(values, axis, other)


def beside(work, sends):
    def run():
        return work(), [move(*send) for send in sends]

    def skip():
        return jax.tree.map(lambda v: jnp.zeros(v.shape, v.dtype), jax.eval_shape(run))

    return lax.optimization_barrier(lax.cond(lax.axis_index("chan") < lax.axis_size("chan"), run, skip))


def fold(keep, got, axis, bit, parts=1):
    shape = keep.shape
    half = shape[0] // 2
    flat = [v.reshape(shape[0], -1, shape[-1]) for v in (keep, got)]
    rows, columns = flat[0].shape[1:]
    step = block_of(rows, max(16, MIB // (2 * columns)), 8)
    mine = ((lax.axis_index(axis) >> (bit + 1)) & 1).astype(jnp.int32)[None]

    def kernel(_, kept, came, kept_far, came_far, keep_ref, *send_refs):
        keep_ref[...] = (kept[...].astype(f32) + came[...].astype(f32)).astype(keep_ref.dtype)
        total = (kept_far[...].astype(f32) + came_far[...].astype(f32)).astype(keep_ref.dtype)
        for part, ref in enumerate(send_refs):
            ref[...] = total[..., part * (columns // parts) : (part + 1) * (columns // parts)]

    near = pl.BlockSpec((1, step, columns), lambda i, r, own: (own[0] * half + i, r, 0))
    far = pl.BlockSpec((1, step, columns), lambda i, r, own: ((1 - own[0]) * half + i, r, 0))
    place = lambda width: pl.BlockSpec((1, step, width), lambda i, r, own: (i, r, 0))
    shape_of_part = lambda width: jax.ShapeDtypeStruct((half, rows, width), keep.dtype)
    out = pl.pallas_call(
        kernel,
        grid_spec=pltpu.PrefetchScalarGridSpec(
            num_scalar_prefetch=1,
            grid=(half, rows // step),
            in_specs=[near, near, far, far],
            out_specs=[place(columns)] + [place(columns // parts)] * parts,
        ),
        out_shape=[shape_of_part(columns)] + [shape_of_part(columns // parts)] * parts,
        compiler_params=pltpu.CompilerParams(vmem_limit_bytes=32 * MIB),
        cost_estimate=pl.CostEstimate(flops=int(2e9), bytes_accessed=6 * keep.size, transcendentals=0),
    )(mine, *flat, *flat)
    out = [v.reshape((half,) + shape[1:-1] + v.shape[-1:]) for v in out]
    return (out[0], out[1]) if parts == 1 else (out[0], out[1:])


def finish(keep, got, axis, bit):
    while bit + 1 < bit_count(lax.axis_size(axis)):
        keep, send = fold(keep, got, axis, bit)
        bit += 1
        got = swap(send, axis, 1 << bit)
    return keep[0], got[0]


def plain(values):
    return with_layout_constraint(values, Layout(tuple(range(values.ndim))))


def halves(blocks, axis):
    return halves_at(blocks, axis, 0)


def halves_at(blocks, axis, bit):
    mine = (lax.axis_index(axis) >> bit) & 1
    half = blocks.shape[0] // 2
    return tuple(lax.dynamic_slice_in_dim(blocks, which * half, half, 0) for which in (mine, 1 - mine))


def sum_scatter(values, axis, first=0):
    for bit in range(first, bit_count(lax.axis_size(axis))):
        mine = (lax.axis_index(axis) >> bit) & 1
        half = values.shape[0] // 2
        keep = lax.dynamic_slice_in_dim(values, mine * half, half, 0)
        send = lax.dynamic_slice_in_dim(values, (1 - mine) * half, half, 0)
        values = keep + swap(send, axis, 1 << bit)
    return values[0]


def halving_order(values, axis):
    count = lax.axis_size(axis)
    bits = bit_count(count)
    return jnp.stack([values[reverse_bits(j, bits)] for j in range(count)])


def parts_beside(block, near, far):
    top = bit_count(lax.axis_size("chan")) - 1
    parts = {0: block, 1 << top: far}
    for bit in reversed(range(1, top)):
        for offset in list(parts):
            parts[offset | (1 << bit)] = swap(parts[offset], "chan", 1 << bit)
    parts[1] = near
    for offset in list(parts):
        if offset > 1:
            parts[offset | 1] = swap(parts[offset], "chan", 1)
    return [parts[offset] for offset in sorted(parts)]


def sum_all(values, axis, first=0):
    for bit in range(first, bit_count(lax.axis_size(axis))):
        values = values + swap(values, axis, 1 << bit)
    return values


def lane_shift(values, step):
    count = values.shape[-1]
    step = step % count
    return values if step == 0 else pltpu.roll(values, count - step, 1)


def fill_masks(col_ref, row_ref):
    lanes = col_ref.shape[-1]
    place = lax.broadcasted_iota(jnp.int32, (GROUP, lanes), 1)
    col = place % MAP
    row = (place // MAP) % MAP
    for tap in range(TAPS):
        step = tap - TAPS // 2
        for ref, spot in ((col_ref, col), (row_ref, row)):
            ref[tap] = ((spot + step >= 0) & (spot + step < MAP)).astype(f32).astype(bf16)


def tap_weights(kernel):
    tap = np.arange(TAPS * TAPS)[:, None]
    spot = np.arange(TAPS * WIDE)[None, :]
    pick = (tap == (spot // WIDE) * TAPS + (spot % WIDE) // GROUP) & (spot % WIDE < TAPS * GROUP)
    own = (jnp.arange(kernel.shape[0])[:, None] % GROUP) == jnp.asarray(spot % GROUP)
    spread = jnp.dot(kernel, jnp.asarray(pick.astype(bf16)), preferred_element_type=f32)
    return jnp.where(own, spread, 0.0).astype(bf16)


def stacked_weights(k_ref):
    blocks = [k_ref[:, r * WIDE : r * WIDE + TAPS * GROUP] for r in range(TAPS)]
    return jnp.concatenate(blocks, axis=0)


def depthwise_kernel(x_ref, k_ref, o_ref, s_ref, col_ref, row_ref):
    @pl.when(pl.program_id(0) == 0)
    def _():
        fill_masks(col_ref, row_ref)

    x = x_ref[...]
    lanes = x.shape[1]
    for tap in range(TAPS):
        step = tap - TAPS // 2
        moved = lane_shift(x, step)
        s_ref[tap] = moved if step == 0 else moved * col_ref[tap]
    rows = jnp.dot(
        stacked_weights(k_ref), s_ref[...].reshape(TAPS * GROUP, lanes), preferred_element_type=f32
    )
    total = None
    for tap in range(TAPS):
        step = tap - TAPS // 2
        part = rows[tap * GROUP : (tap + 1) * GROUP]
        if step != 0:
            part = (lane_shift(part.astype(bf16), MAP * step) * row_ref[tap]).astype(f32)
        total = part if total is None else total + part
    o_ref[...] = total.astype(o_ref.dtype)


def depthwise(x, weights):
    channels, lanes = x.shape
    return pl.pallas_call(
        depthwise_kernel,
        grid=(channels // GROUP,),
        in_specs=[
            pl.BlockSpec((GROUP, lanes), lambda i: (i, 0)),
            pl.BlockSpec((GROUP, TAPS * WIDE), lambda i: (i, 0)),
        ],
        out_specs=pl.BlockSpec((GROUP, lanes), lambda i: (i, 0)),
        out_shape=jax.ShapeDtypeStruct((channels, lanes), bf16),
        scratch_shapes=[pltpu.VMEM((TAPS, GROUP, lanes), bf16)] * 3,
        compiler_params=pltpu.CompilerParams(vmem_limit_bytes=32 * MIB),
        cost_estimate=pl.CostEstimate(
            flops=int(8 * 1.1e9), bytes_accessed=4 * channels * lanes, transcendentals=0
        ),
    )(x, weights)


def depthwise_back_kernel(
    keep_ref, near_ref, far_ref, m_ref, stat_ref, sum_ref, gain_ref, x_ref, k_ref, add_ref,
    gx_ref, gk_ref, gg_ref, t_ref, s_ref, col_ref, row_ref,
):
    @pl.when(pl.program_id(0) == 0)
    def _():
        fill_masks(col_ref, row_ref)

    x = x_ref[...]
    lanes = x.shape[1]
    inverse = stat_ref[1:2]
    unit = (m_ref[...].astype(f32) - stat_ref[0:1]) * inverse
    got = jnp.concatenate([near_ref[...], far_ref[...]], axis=1)
    grad = keep_ref[...].astype(f32) + got.astype(f32)
    gg_ref[...] = jnp.broadcast_to(jnp.sum(grad * unit, axis=1, keepdims=True), gg_ref.shape)
    d = (inverse * (grad * gain_ref[...] - sum_ref[0:1] - unit * sum_ref[1:2])).astype(bf16)
    last = TAPS - 1
    for tap in range(TAPS):
        step = tap - TAPS // 2
        moved = lane_shift(d, -step)
        t_ref[tap] = moved if step == 0 else moved * col_ref[last - tap]
        moved = lane_shift(x, MAP * step)
        s_ref[tap] = moved if step == 0 else moved * row_ref[tap]
    t = t_ref[...].reshape(TAPS * GROUP, lanes)
    rows = jnp.dot(stacked_weights(k_ref), t, preferred_element_type=f32)
    total = add_ref[...]
    for tap in range(TAPS):
        step = tap - TAPS // 2
        part = rows[tap * GROUP : (tap + 1) * GROUP]
        if step != 0:
            part = (lane_shift(part.astype(bf16), -MAP * step) * row_ref[last - tap]).astype(f32)
        total = total + part
    cells = gx_ref.shape[2]
    for i in range(gx_ref.shape[1]):
        gx_ref[:, i, :] = total[:, i * cells : (i + 1) * cells]
    pairs = lax.dot_general(
        t, s_ref[...].reshape(TAPS * GROUP, lanes), (((1,), (1,)), ((), ())), preferred_element_type=f32
    )
    side = TAPS * GROUP
    first = lax.broadcasted_iota(jnp.int32, (side, side), 0)
    second = lax.broadcasted_iota(jnp.int32, (side, side), 1)
    own = jnp.where(first % GROUP == second % GROUP, pairs, 0.0)
    source = lax.broadcasted_iota(jnp.int32, (side, 128), 0)
    target = lax.broadcasted_iota(jnp.int32, (side, 128), 1)
    pick = (source // GROUP == target).astype(f32).astype(bf16)
    high = own.astype(bf16)
    low = (own - high.astype(f32)).astype(bf16)
    gk_ref[0] = jnp.dot(high, pick, preferred_element_type=f32) + jnp.dot(
        low, pick, preferred_element_type=f32
    )


def depthwise_back(keep, near, far, mapped, stats, sums, gain, x, weights, add, images):
    channels, lanes = x.shape
    groups = channels // GROUP
    rows = pl.BlockSpec((GROUP, lanes), lambda i: (i, 0))
    half = pl.BlockSpec((GROUP, lanes // 2), lambda i: (i, 0))
    fixed = pl.BlockSpec((8, lanes), lambda i: (0, 0))
    gx, gk, gg = pl.pallas_call(
        depthwise_back_kernel,
        grid=(groups,),
        in_specs=[
            rows, half, half, rows, fixed, fixed,
            pl.BlockSpec((GROUP, 1), lambda i: (i, 0)),
            rows,
            pl.BlockSpec((GROUP, TAPS * WIDE), lambda i: (i, 0)),
            rows,
        ],
        out_specs=[
            pl.BlockSpec((GROUP, images, lanes // images), lambda i: (i, 0, 0)),
            pl.BlockSpec((1, TAPS * GROUP, 128), lambda i: (i, 0, 0)),
            pl.BlockSpec((GROUP, 128), lambda i: (i, 0)),
        ],
        out_shape=[
            jax.ShapeDtypeStruct((channels, images, lanes // images), f32),
            jax.ShapeDtypeStruct((groups, TAPS * GROUP, 128), f32),
            jax.ShapeDtypeStruct((channels, 128), f32),
        ],
        scratch_shapes=[pltpu.VMEM((TAPS, GROUP, lanes), bf16)] * 4,
        compiler_params=pltpu.CompilerParams(vmem_limit_bytes=56 * MIB),
        cost_estimate=pl.CostEstimate(
            flops=int(16 * 1.1e9), bytes_accessed=14 * channels * lanes, transcendentals=0
        ),
    )(keep, near, far, mapped, stats, sums, gain, x, weights, add)
    gk = gk[:, :, :TAPS].reshape(groups, TAPS, GROUP, TAPS).transpose(0, 2, 3, 1)
    return gx, gk.reshape(channels, TAPS * TAPS), gg[:, 0]


def gelu_both(u):
    share = 0.5 * (1.0 + lax.erf(u * (1.0 / math.sqrt(2.0))))
    return u * share, share + u * jnp.exp(-0.5 * u * u) * (1.0 / math.sqrt(2.0 * math.pi))


def pool_table():
    out_index = np.arange(GRID)
    first_row = out_index * MAP // GRID
    last_row = ((out_index + 1) * MAP + GRID - 1) // GRID
    source_index = np.arange(MAP)
    inside = (source_index[None, :] >= first_row[:, None]) & (
        source_index[None, :] < last_row[:, None]
    )
    single = inside.astype(np.float32) / (last_row - first_row)[:, None].astype(np.float32)
    table = single[:, None, :, None] * single[None, :, None, :]
    return table.reshape(GRID * GRID, MAP * MAP)


PACE = 1.1e9


def mm(a, b):
    return jnp.dot(a, b, preferred_element_type=f32)


def mm_nt(a, b):
    return lax.dot_general(a, b, (((1,), (1,)), ((), ())), preferred_element_type=f32)


def mm_tn(a, b):
    return lax.dot_general(a, b, (((0,), (0,)), ((), ())), preferred_element_type=f32)


def whole(shape):
    return pl.BlockSpec(shape, lambda *_: (0,) * len(shape), pipeline_mode=pl.Buffered(1))


def shape_of(shape, dtype=bf16):
    return jax.ShapeDtypeStruct(shape, dtype)


def call(kernel, ids, grid, args, in_specs, outs, out_specs, scratch=(), micros=10, vmem=56, earlier=(), through=()):
    count = len(earlier)
    passed = len(through)
    ins = len(args)
    results = len(outs)

    def run(ids_ref, *refs):
        refs = refs[count + passed :]
        kernel(ids_ref, *refs[: ins + results], *refs[ins + results + passed :])

    bytes_accessed = sum(v.size * v.dtype.itemsize for v in list(args) + list(outs))
    return pl.pallas_call(
        run,
        grid_spec=pltpu.PrefetchScalarGridSpec(
            num_scalar_prefetch=1,
            grid=grid,
            in_specs=[pl.BlockSpec(memory_space=pl.ANY)] * (count + passed) + in_specs,
            out_specs=out_specs + [pl.BlockSpec(memory_space=pl.ANY)] * passed,
            scratch_shapes=scratch,
        ),
        out_shape=outs + [jax.ShapeDtypeStruct(v.shape, v.dtype) for v in through],
        input_output_aliases={1 + count + i: results + i for i in range(passed)},
        compiler_params=pltpu.CompilerParams(vmem_limit_bytes=vmem * MIB),
        cost_estimate=pl.CostEstimate(flops=int(micros * PACE), bytes_accessed=int(bytes_accessed), transcendentals=0),
    )(ids, *earlier, *through, *args)


def deal(stack_ref, keep_ref, send_ref, mine, lead=()):
    half = stack_ref.shape[0] // 2
    for j in range(half):
        block = 2 * reverse_bits(j, bit_count(half))
        keep_ref[(j,) + lead] = stack_ref[block + mine]
        send_ref[(j,) + lead] = stack_ref[block + 1 - mine]


def dealt_rows(w_ref, own, refs, operand, mine):
    half = refs[0].shape[0]
    for ref, bit in zip(refs, (mine, 1 - mine)):
        for j in range(half):
            block = 2 * reverse_bits(j, bit_count(half)) + bit
            rows = w_ref[pl.ds(pl.multiple_of(block * own, 16), own), :]
            ref[j] = mm(rows, operand[...]).astype(bf16)


def conv_forward(parts, up_t, down, gain, ids, earlier=(), through=()):
    count = len(parts)
    own, lanes = parts[0].shape
    channels = own * count
    hidden = up_t.shape[0]
    bn = block_of(lanes, 512, 128)
    step = block_of(hidden, 256, 128)

    def kernel(ids_ref, *refs):
        part_refs = refs[:count]
        up_ref, down_ref, gain_ref, cn_ref, h_ref, s_ref, stat_ref, keep_ref, send_ref = refs[count:]
        me = ids_ref[0]
        mean = sum(jnp.sum(part[...].astype(f32), axis=0, keepdims=True) for part in part_refs) * (1.0 / channels)
        square = sum(
            jnp.sum((part[...].astype(f32) - mean) ** 2, axis=0, keepdims=True) for part in part_refs
        ) * (1.0 / channels)
        inverse = lax.rsqrt(square + conv_eps)
        stat_ref[...] = jnp.concatenate([mean, inverse, jnp.zeros((6, bn), f32)], axis=0)
        for offset, part in enumerate(part_refs):
            rows = pl.ds(pl.multiple_of((me ^ offset) * own, 16), own)
            cn_ref[rows, :] = ((part[...].astype(f32) - mean) * inverse * gain_ref[rows, :]).astype(bf16)
        for f in range(0, hidden, step):
            act, slope = gelu_both(mm(up_ref[f : f + step], cn_ref[...]))
            h_ref[f : f + step] = act.astype(bf16)
            s_ref[f : f + step] = slope.astype(bf16)
        dealt_rows(down_ref, own, (keep_ref, send_ref), h_ref, me & 1)

    tall = lambda rows: pl.BlockSpec((rows, bn), lambda j, _: (0, j))
    half = pl.BlockSpec((count // 2, own, bn), lambda j, _: (0, 0, j))
    return call(
        kernel,
        ids,
        (lanes // bn,),
        (*parts, up_t, down, gain),
        [tall(own)] * count + [whole(up_t.shape), whole(down.shape), whole(gain.shape)],
        [
            shape_of((channels, lanes)),
            shape_of((hidden, lanes)),
            shape_of((hidden, lanes)),
            shape_of((8, lanes), f32),
            shape_of((count // 2, own, lanes)),
            shape_of((count // 2, own, lanes)),
        ],
        [tall(channels), tall(hidden), tall(hidden), tall(8), half, half],
        micros=36,
        earlier=earlier,
        through=through,
    )


def conv_backward(d_all, down_t, up, slope, normed, gain, ids, earlier=(), through=()):
    channels, lanes = d_all.shape
    hidden = down_t.shape[0]
    count = lax.axis_size("chan")
    own = channels // count
    bn = block_of(lanes, 512, 128)
    step = block_of(hidden, 512, 128)

    def kernel(ids_ref, d_ref, down_ref, up_ref, s_ref, n_ref, gain_ref, du_ref, keep_ref, send_ref, sum_ref):
        for f in range(0, hidden, step):
            du = mm(down_ref[f : f + step], d_ref[...]) * s_ref[f : f + step].astype(f32)
            du_ref[f : f + step] = du.astype(bf16)
        mine = ids_ref[0] & 1
        first = second = jnp.zeros((1, bn), f32)
        for ref, bit in ((keep_ref, mine), (send_ref, 1 - mine)):
            for j in range(count // 2):
                block = 2 * reverse_bits(j, bit_count(count // 2)) + bit
                rows = pl.ds(pl.multiple_of(block * own, 16), own)
                part = mm(up_ref[rows, :], du_ref[...])
                ref[j] = part.astype(bf16)
                first += jnp.sum(part * gain_ref[rows, :], axis=0, keepdims=True)
                second += jnp.sum(part * n_ref[rows, :].astype(f32), axis=0, keepdims=True)
        sum_ref[...] = jnp.concatenate([first, second, jnp.zeros((6, bn), f32)], axis=0)

    tall = lambda rows: pl.BlockSpec((rows, bn), lambda j, _: (0, j))
    half = pl.BlockSpec((count // 2, own, bn), lambda j, _: (0, 0, j))
    return call(
        kernel,
        ids,
        (lanes // bn,),
        (d_all, down_t, up, slope, normed, gain),
        [tall(channels), whole(down_t.shape), whole(up.shape), tall(hidden), tall(channels), whole(gain.shape)],
        [
            shape_of((hidden, lanes)),
            shape_of((count // 2, own, lanes)),
            shape_of((count // 2, own, lanes)),
            shape_of((8, lanes), f32),
        ],
        [tall(hidden), half, half, tall(8)],
        micros=28,
        earlier=earlier,
        through=through,
    )


def dealt_halves(size, patchs, columns, bn):
    half = pl.BlockSpec((patchs // 2, size, bn), lambda j, _: (0, 0, 0))

    def deal_columns(product, stack_ref, refs, mine):
        stack_ref[...] = product.astype(bf16).reshape(patchs, size, bn)
        for part in range(2):

            @pl.when(pl.program_id(0) == part)
            def _(part=part):
                deal(stack_ref, refs[2 * part], refs[2 * part + 1], mine)

    return [half] * 4, [shape_of((patchs // 2, size, columns // 2))] * 4, deal_columns


def down_gradient(parts, act, patchs, ids):
    count = len(parts)
    own, lanes = parts[0].shape
    channels = own * count
    hidden = act.shape[0]
    bn = hidden // 2
    size = channels // patchs
    specs, shapes, deal_columns = dealt_halves(size, patchs, hidden, bn)

    def kernel(ids_ref, *refs):
        part_refs = refs[:count]
        b_ref, d_ref, *out_refs, o_ref = refs[count:]

        @pl.when(pl.program_id(0) == 0)
        def _():
            for offset, part in enumerate(part_refs):
                d_ref[pl.ds(pl.multiple_of((ids_ref[0] ^ offset) * own, 16), own), :] = part[...]

        deal_columns(mm_nt(d_ref[...], b_ref[...]), o_ref, out_refs, ids_ref[1] & 1)

    return call(
        kernel,
        ids,
        (2,),
        (*parts, act),
        [whole(parts[0].shape)] * count + [pl.BlockSpec((bn, lanes), lambda j, _: (j, 0))],
        [shape_of((channels, lanes))] + shapes,
        [whole((channels, lanes))] + specs,
        [pltpu.VMEM((patchs, size, bn), bf16)],
        micros=18,
    )


def weight_gradient(a, b, patchs, ids):
    rows, depth = a.shape
    columns = b.shape[0]
    bn = columns // 2
    size = rows // patchs
    specs, shapes, deal_columns = dealt_halves(size, patchs, columns, bn)

    def kernel(ids_ref, a_ref, b_ref, *refs):
        deal_columns(mm_nt(a_ref[...], b_ref[...]), refs[-1], refs[:-1], ids_ref[1] & 1)

    return call(
        kernel,
        ids,
        (2,),
        (a, b),
        [whole(a.shape), pl.BlockSpec((bn, depth), lambda j, _: (j, 0))],
        shapes,
        specs,
        [pltpu.VMEM((patchs, size, bn), bf16)],
        micros=18,
    )


def pool_forward(keep, got, conv_flat, scale, images, band, chans, ids, earlier=(), through=()):
    own, lanes = keep.shape
    cells = lanes // images
    table = pool_table()
    tokens = table.shape[0]
    reach = band + 2 * GRID
    padded = jnp.asarray(np.pad(table, ((GRID, GRID), (0, 0))))

    def kernel(ids_ref, keep_ref, got_ref, c_ref, scale_ref, t_ref, p_ref, branch_ref, result_ref, pooled_ref, *pieces):
        branch = keep_ref[...].astype(f32) + got_ref[...].astype(f32)
        branch_ref[...] = branch.astype(bf16)
        result = (c_ref[...].astype(f32) + scale_ref[...] * branch).astype(bf16)
        result_ref[...] = result
        pooled_ref[0] = mm(result, t_ref[...]).astype(bf16)
        for offset, piece in enumerate(pieces):
            start = pl.multiple_of((ids_ref[0] ^ offset) * band, 8)
            rows = p_ref[pl.ds(start, reach), :].astype(bf16)
            piece[0] = mm_nt(rows, result).astype(bf16)

    flat = pl.BlockSpec((own, cells), lambda i, _: (0, i))
    return call(
        kernel,
        ids,
        (images,),
        (keep, got, conv_flat, scale, jnp.asarray(table.T.astype(bf16)), padded),
        [flat, flat, flat, whole(scale.shape), whole((cells, tokens)), whole(padded.shape)],
        [shape_of((own, lanes))] * 2
        + [shape_of((images, own, tokens))]
        + [shape_of((images, reach, own))] * chans,
        [flat, flat, pl.BlockSpec((1, own, tokens), lambda i, _: (i, 0, 0))]
        + [pl.BlockSpec((1, reach, own), lambda i, _: (i, 0, 0))] * chans,
        micros=9,
        earlier=earlier,
        through=through,
    )


def row_moves(field, spots, step):
    if step == 0:
        return field
    count = field.shape[0]
    moved = pltpu.roll(field, (-step) % count, 0)
    column = spots % GRID + step
    return jnp.where((column >= 0) & (column < GRID), moved, 0.0)


def adapter(pieces, w_proj, kernel_three, gate_in, gate_out, d_band, ids, earlier=(), through=()):
    chans = len(pieces)
    images, reach, own = pieces[0].shape
    width = w_proj.shape[1]
    gate = gate_in.shape[1]
    band = reach - 2 * GRID

    def kernel(ids_ref, *refs):
        piece_refs = refs[:chans]
        proj_ref, k_ref, in_ref, out_ref, d_ref, gs_ref, ds_ref, gib_ref, gob_ref, gk_ref, gi_ref, go_ref = refs[chans:]
        me = ids_ref[0]

        @pl.when(pl.program_id(0) == 0)
        def _():
            gi_ref[...] = jnp.zeros_like(gi_ref)
            go_ref[...] = jnp.zeros_like(go_ref)
            gk_ref[...] = jnp.zeros_like(gk_ref)

        field = None
        for offset, piece in enumerate(piece_refs):
            start = pl.multiple_of((me ^ offset) * own, 16)
            term = mm(piece[0], proj_ref[pl.ds(start, own), :])
            field = term if field is None else field + term
        field = field.astype(bf16).astype(f32)
        spots = lax.broadcasted_iota(jnp.int32, (reach, 1), 0)
        moved = [row_moves(field, spots, step) for step in (-1, 0, 1)]
        smooth = None
        for t in range(9):
            term = k_ref[t : t + 1, :] * moved[t % 3][GRID * (t // 3) : GRID * (t // 3) + band]
            smooth = term if smooth is None else smooth + term
        rows = smooth.astype(bf16)
        act, slope = gelu_both(mm(rows, in_ref[...]))
        act = act.astype(bf16)
        value = jnp.tanh(mm(act, out_ref[...]))
        gs_ref[0] = value * smooth
        d = d_ref[0].astype(f32)
        d_logit = (d * smooth * (1.0 - value * value)).astype(bf16)
        d_gate = (mm_nt(d_logit, out_ref[...]) * slope).astype(bf16)
        d_smooth = d * value + mm_nt(d_gate, in_ref[...])
        ds_ref[0] = d_smooth.astype(bf16)
        go_ref[...] += mm_tn(act, d_logit)
        gi_ref[...] += mm_tn(rows, d_gate)
        for t in range(9):
            seen = moved[t % 3][GRID * (t // 3) : GRID * (t // 3) + band]
            gk_ref[t : t + 1, :] += jnp.sum(d_smooth * seen, axis=0, keepdims=True)

        @pl.when(pl.program_id(0) == images - 1)
        def _():
            gib_ref[...] = gi_ref[...].astype(bf16)
            gob_ref[...] = go_ref[...].astype(bf16)

    per = lambda rows, cols: pl.BlockSpec((1, rows, cols), lambda i, _: (i, 0, 0))
    kept = lambda *shape: pl.BlockSpec(shape, lambda i, _: (0, 0))
    return call(
        kernel,
        ids,
        (images,),
        (*pieces, w_proj, kernel_three, gate_in, gate_out, d_band),
        [per(reach, own)] * chans
        + [whole(w_proj.shape), whole(kernel_three.shape), whole(gate_in.shape), whole(gate_out.shape), per(band, width)],
        [
            shape_of((images, band, width), f32),
            shape_of((images, band, width)),
            shape_of((width, gate)),
            shape_of((gate, width)),
            shape_of((16, width), f32),
        ],
        [per(band, width), per(band, width), kept(width, gate), kept(gate, width), kept(16, width)],
        [pltpu.VMEM((width, gate), f32), pltpu.VMEM((gate, width), f32)],
        micros=13,
        earlier=earlier,
        through=through,
    )


def adapter_back(parts, w_own, kernel_three, pooled, d_out, branch, scale, ids, earlier=(), through=()):
    chans = len(parts)
    images, band, width = parts[0].shape
    own, lanes = d_out.shape
    cells = lanes // images
    tokens = band * chans
    table = jnp.asarray(pool_table().astype(bf16))

    def kernel(ids_ref, *refs):
        part_refs = refs[:chans]
        w_ref, k_ref, pooled_ref, do_ref, branch_ref, scale_ref, t_ref, dr_ref, db_ref, gpb_ref, gs_ref, f_ref, gp_ref = refs[chans:]
        me = ids_ref[0]

        @pl.when(pl.program_id(0) == 0)
        def _():
            gp_ref[...] = jnp.zeros_like(gp_ref)
            gs_ref[...] = jnp.zeros_like(gs_ref)
            f_ref[:GRID] = jnp.zeros((GRID, width), f32)
            f_ref[GRID + tokens :] = jnp.zeros((GRID, width), f32)

        for offset, part in enumerate(part_refs):
            start = pl.multiple_of((me ^ offset) * band + GRID, 8)
            f_ref[pl.ds(start, band), :] = part[0].astype(f32)
        field = f_ref[...]
        spots = lax.broadcasted_iota(jnp.int32, (tokens + 2 * GRID, 1), 0)
        moved = [row_moves(field, spots, -step) for step in (-1, 0, 1)]
        d_adapted = None
        for t in range(9):
            start = GRID * (2 - t // 3)
            term = k_ref[t : t + 1, :] * moved[t % 3][start : start + tokens]
            d_adapted = term if d_adapted is None else d_adapted + term
        d_adapted = d_adapted.astype(bf16)
        d_pooled = mm_nt(w_ref[...], d_adapted).astype(bf16)
        gp_ref[...] += mm(pooled_ref[0], d_adapted)
        d_result = do_ref[...].astype(f32) + mm(d_pooled, t_ref[...])
        dr_ref[...] = d_result
        db_ref[...] = (scale_ref[...] * d_result).astype(bf16)
        gs_ref[...] += jnp.sum(d_result * branch_ref[...].astype(f32), axis=1, keepdims=True)

        @pl.when(pl.program_id(0) == images - 1)
        def _():
            gpb_ref[...] = gp_ref[...].astype(bf16)

    flat = pl.BlockSpec((own, cells), lambda i, _: (0, i))
    per = lambda rows, cols: pl.BlockSpec((1, rows, cols), lambda i, _: (i, 0, 0))
    return call(
        kernel,
        ids,
        (images,),
        (*parts, w_own, kernel_three, pooled, d_out, branch, scale, table),
        [per(band, width)] * chans
        + [whole(w_own.shape), whole(kernel_three.shape), per(own, tokens), flat, flat, whole(scale.shape), whole(table.shape)],
        [
            shape_of((own, lanes), f32),
            shape_of((own, lanes)),
            shape_of((own, width)),
            shape_of((own, 128), f32),
        ],
        [flat, flat, pl.BlockSpec((own, width), lambda i, _: (0, 0)), pl.BlockSpec((own, 128), lambda i, _: (0, 0))],
        [pltpu.VMEM((tokens + 2 * GRID, width), f32), pltpu.VMEM((own, width), f32)],
        micros=14,
        earlier=earlier,
        through=through,
    )


def row_standard(values):
    center = values - jnp.mean(values, axis=-1, keepdims=True)
    inverse = lax.rsqrt(jnp.mean(center * center, axis=-1, keepdims=True) + vit_eps)
    return center * inverse


def stack_bands(stack_ref, values):
    count, band, _ = stack_ref.shape
    for b in range(count):
        stack_ref[b] = values[b * band : (b + 1) * band].astype(bf16)


def take_bands(rows_ref, part_refs, me):
    for offset, part in enumerate(part_refs):
        band = part.shape[1]
        start = pl.multiple_of((me ^ offset) * band, 8)
        rows_ref[pl.ds(start, band), :] = part[0].astype(f32)
    return rows_ref[...].astype(bf16)


def attention_forward(x, gain, w_qkv, w_attn, chans, ids, earlier=(), through=()):
    images, tokens, width = x.shape
    own = w_qkv.shape[2]
    heads = own // HEAD_DIM
    band = tokens // chans
    scale = 1.0 / math.sqrt(HEAD_DIM)

    def kernel(ids_ref, x_ref, gain_ref, qkv_w_ref, attn_ref, n_ref, qkv_ref, o_ref, log_ref, keep_ref, send_ref, stack_ref):
        normed = (row_standard(x_ref[0].astype(f32)) * gain_ref[...]).astype(bf16)
        n_ref[0] = normed
        q, k, v = (mm(normed, qkv_w_ref[t]).astype(bf16) for t in range(3))
        for t, part in enumerate((q, k, v)):
            qkv_ref[t, 0] = part
        mixed = []
        spot = lax.broadcasted_iota(jnp.int32, (tokens, 128), 1)
        logs = jnp.zeros((tokens, 128), f32)
        for h in range(heads):
            at = slice(h * HEAD_DIM, (h + 1) * HEAD_DIM)
            scores = mm_nt(q[:, at], k[:, at]) * scale
            most = jnp.max(scores, axis=-1, keepdims=True)
            powers = jnp.exp(scores - most)
            total = jnp.sum(powers, axis=-1, keepdims=True)
            logs = jnp.where(spot == h, most + jnp.log(total), logs)
            mixed.append(mm((powers * (1.0 / total)).astype(bf16), v[:, at]).astype(bf16))
        mixed = jnp.concatenate(mixed, axis=1)
        log_ref[0] = logs
        o_ref[0] = mixed
        stack_bands(stack_ref, mm_nt(mixed, attn_ref[...]))
        deal(stack_ref, keep_ref, send_ref, ids_ref[0] & 1, (0,))

    per = lambda cols: pl.BlockSpec((1, tokens, cols), lambda i, _: (i, 0, 0))
    half = pl.BlockSpec((chans // 2, 1, band, width), lambda i, _: (0, i, 0, 0))
    return call(
        kernel,
        ids,
        (images,),
        (x, gain, w_qkv, w_attn),
        [per(width), whole(gain.shape), whole(w_qkv.shape), whole(w_attn.shape)],
        [
            shape_of((images, tokens, width)),
            shape_of((3, images, tokens, own)),
            shape_of((images, tokens, own)),
            shape_of((images, tokens, 128), f32),
            shape_of((chans // 2, images, band, width)),
            shape_of((chans // 2, images, band, width)),
        ],
        [per(width), pl.BlockSpec((3, 1, tokens, own), lambda i, _: (0, i, 0, 0)), per(own), per(128), half, half],
        [pltpu.VMEM((chans, band, width), bf16)],
        micros=16,
        earlier=earlier,
        through=through,
    )


def feed_forward(parts, d_rows, w_up, w_down, patchs, ids, earlier=(), through=()):
    chans = len(parts)
    images, band, width = parts[0].shape
    tokens = band * chans
    hidden = w_up.shape[1]

    def kernel(ids_ref, *refs):
        part_refs = refs[:chans]
        (
            d_ref, up_ref, down_ref, keep_ref, send_ref, dkeep_ref, dsend_ref, *grad_refs,
            rows_ref, stack_ref, gu_ref, gd_ref, g_ref,
        ) = refs[chans:]
        me = ids_ref[0]
        step = pl.program_id(0)
        normed = take_bands(rows_ref, part_refs, me)
        act, slope = gelu_both(mm(normed, up_ref[...]))
        act = act.astype(bf16)
        stack_bands(stack_ref, mm_nt(act, down_ref[...]))
        deal(stack_ref, keep_ref, send_ref, me & 1, (0,))
        d = d_ref[0]
        d_pre = (mm(d, down_ref[...]) * slope).astype(bf16)
        stack_bands(stack_ref, mm_nt(d_pre, up_ref[...]))
        deal(stack_ref, dkeep_ref, dsend_ref, me & 1, (0,))
        gu = mm_tn(normed, d_pre)
        gd = mm_tn(d, act)

        @pl.when(step == 0)
        def _():
            gu_ref[...] = gu
            gd_ref[...] = gd

        @pl.when(step > 0)
        def _():
            gu_ref[...] += gu
            gd_ref[...] += gd

        @pl.when(step == images - 1)
        def _():
            for part in range(4):
                source = (gu_ref, gd_ref)[part // 2]
                columns = slice((part % 2) * part_width, (part % 2 + 1) * part_width)
                for b in range(patchs):
                    g_ref[b] = source[b * size : (b + 1) * size, columns].astype(bf16)
                deal(g_ref, grad_refs[2 * part], grad_refs[2 * part + 1], ids_ref[1] & 1)

    per = lambda rows: pl.BlockSpec((1, rows, width), lambda i, _: (i, 0, 0))
    half = pl.BlockSpec((chans // 2, 1, band, width), lambda i, _: (0, i, 0, 0))
    halves = shape_of((chans // 2, images, band, width))
    size = width // patchs
    part_width = hidden // 2
    grads = (patchs // 2, size, part_width)
    return call(
        kernel,
        ids,
        (images,),
        (*parts, d_rows, w_up, w_down),
        [per(band)] * chans + [per(tokens), whole(w_up.shape), whole(w_down.shape)],
        [halves] * 4 + [shape_of(grads)] * 8,
        [half] * 4 + [pl.BlockSpec(grads, lambda i, _: (0, 0, 0))] * 8,
        [
            pltpu.VMEM((tokens, width), f32),
            pltpu.VMEM((chans, band, width), bf16),
            pltpu.VMEM((width, hidden), f32),
            pltpu.VMEM((width, hidden), f32),
            pltpu.VMEM((patchs, size, part_width), bf16),
        ],
        micros=26,
        earlier=earlier,
        through=through,
    )


def attention_backward(parts, normed, qkv, mixed, logs, w_qkv, w_attn, patchs, ids, earlier=(), through=()):
    chans = len(parts)
    images, band, width = parts[0].shape
    tokens = band * chans
    own = w_attn.shape[1]
    heads = own // HEAD_DIM
    scale = 1.0 / math.sqrt(HEAD_DIM)

    def kernel(ids_ref, *refs):
        part_refs = refs[:chans]
        (
            n_ref, qkv_ref, o_ref, log_ref, qkv_w_ref, attn_ref, keep_ref, send_ref, gkeep_ref, gsend_ref,
            rows_ref, stack_ref, acc_ref, g_ref,
        ) = refs[chans:]
        me = ids_ref[0]
        step = pl.program_id(0)
        d = take_bands(rows_ref, part_refs, me)
        d_mixed = mm(d, attn_ref[...]).astype(bf16)
        q, k, v = (qkv_ref[t, 0] for t in range(3))
        grads = ([], [], [])
        for h in range(heads):
            at = slice(h * HEAD_DIM, (h + 1) * HEAD_DIM)
            soft = jnp.exp(mm_nt(q[:, at], k[:, at]) * scale - log_ref[0, :, h : h + 1])
            d_soft = mm_nt(d_mixed[:, at], v[:, at])
            across = jnp.sum(d_soft * soft, axis=-1, keepdims=True)
            d_scores = (soft * (d_soft - across)).astype(bf16)
            grads[0].append((mm(d_scores, k[:, at]) * scale).astype(bf16))
            grads[1].append((mm_tn(d_scores, q[:, at]) * scale).astype(bf16))
            grads[2].append(mm_tn(soft.astype(bf16), d_mixed[:, at]).astype(bf16))
        grads = [jnp.concatenate(v, axis=1) for v in grads]
        total = None
        for t in range(3):
            term = mm_nt(grads[t], qkv_w_ref[t])
            total = term if total is None else total + term
        stack_bands(stack_ref, total)
        deal(stack_ref, keep_ref, send_ref, me & 1, (0,))
        new = [mm_tn(n_ref[0], g) for g in grads] + [mm_tn(d, o_ref[0])]

        @pl.when(step == 0)
        def _():
            for t in range(4):
                acc_ref[:, t * own : (t + 1) * own] = new[t]

        @pl.when(step > 0)
        def _():
            for t in range(4):
                acc_ref[:, t * own : (t + 1) * own] += new[t]

        @pl.when(step == images - 1)
        def _():
            for b in range(patchs):
                g_ref[b] = acc_ref[b * size : (b + 1) * size].astype(bf16)
            deal(g_ref, gkeep_ref, gsend_ref, ids_ref[1] & 1)

    per = lambda rows, cols: pl.BlockSpec((1, rows, cols), lambda i, _: (i, 0, 0))
    half = pl.BlockSpec((chans // 2, 1, band, width), lambda i, _: (0, i, 0, 0))
    halves = shape_of((chans // 2, images, band, width))
    size = width // patchs
    out = (patchs // 2, size, 4 * own)
    return call(
        kernel,
        ids,
        (images,),
        (*parts, normed, qkv, mixed, logs, w_qkv, w_attn),
        [per(band, width)] * chans
        + [
            per(tokens, width),
            pl.BlockSpec((3, 1, tokens, own), lambda i, _: (0, i, 0, 0)),
            per(tokens, own),
            per(tokens, 128),
            whole(w_qkv.shape),
            whole(w_attn.shape),
        ],
        [halves] * 2 + [shape_of(out)] * 2,
        [half] * 2 + [pl.BlockSpec(out, lambda i, _: (0, 0, 0))] * 2,
        [
            pltpu.VMEM((tokens, width), f32),
            pltpu.VMEM((chans, band, width), bf16),
            pltpu.VMEM((width, 4 * own), f32),
            pltpu.VMEM((patchs, size, 4 * own), bf16),
        ],
        micros=24,
        earlier=earlier,
        through=through,
    )


def standardize(values, epsilon):
    center = values - jnp.mean(values, axis=-1, keepdims=True)
    inverse = lax.rsqrt(jnp.mean(center * center, axis=-1, keepdims=True) + epsilon)
    return center * inverse, inverse


def norm_back(grad, gain, unit, inverse):
    scaled = grad * gain
    return inverse * (
        scaled
        - jnp.mean(scaled, axis=-1, keepdims=True)
        - unit * jnp.mean(scaled * unit, axis=-1, keepdims=True)
    )


def body(
    vit_in,
    conv_in,
    ln_one,
    w_qkv,
    w_attn,
    ln_two,
    w_up,
    w_down,
    conv_kernel,
    conv_gain,
    conv_up,
    conv_down,
    layer_scale,
    w_proj,
    adapter_kernel,
    gate_in,
    gate_out,
    d_merged,
    d_conv_out,
):
    chans = lax.axis_size("chan")
    patchs = lax.axis_size("patch")
    me = lax.axis_index("chan")
    ids = jnp.stack([me, lax.axis_index("patch")]).astype(jnp.int32)
    tokens, images, width = vit_in.shape
    band = tokens // chans
    own_channels, _, cells = conv_in.shape
    channels = own_channels * chans
    lanes = images * cells
    hidden = w_up.shape[1]
    own_width = w_attn.shape[1]

    def own_rows(values, size):
        return lax.dynamic_slice_in_dim(values, me * size, size, 0)

    def own_band(values):
        return lax.dynamic_slice_in_dim(values, me * band, band, 0).swapaxes(0, 1)

    places = [(p * chans + c, c * patchs + p) for p in range(patchs) for c in range(chans)]

    def placed(values):
        return lax.ppermute(values, ("patch", "chan"), places)

    everywhere = patchs * chans
    rows = own_channels // patchs

    def share(shares, kind, unit):
        flat = [v.astype(kind).reshape(chans, patchs, -1) for v in shares]
        flat = jnp.concatenate(flat, axis=2)
        flat = jnp.pad(flat, ((0, 0), (0, 0), (0, -flat.shape[2] % (rows * unit))))
        flat = flat.reshape(chans, patchs, rows, -1)
        return halving_order(flat, "chan")

    def unshare(values, shares):
        flat = values.reshape(-1)
        out = []
        for v in shares:
            size = v.size // everywhere
            out.append(flat[:size].reshape((v.shape[0] // everywhere,) + v.shape[1:]).astype(f32))
            flat = flat[size:]
        return out

    def summed(pair):
        return pair[0].astype(f32) + pair[1].astype(f32)

    top = 1 << (bit_count(chans) - 1)

    conv_flat = conv_in.reshape(own_channels, lanes)
    weights = tap_weights(own_rows(conv_kernel, own_channels))
    mapped = depthwise(conv_flat, weights)

    gain_one = ln_one.astype(f32)[None]
    gain_two = ln_two.astype(f32)[None]
    w_three = w_qkv.swapaxes(0, 1)

    def attend():
        normed, qkv, mixed, logs, keep, send = attention_forward(
            vit_in.swapaxes(0, 1), gain_one, w_three, w_attn, chans, ids
        )
        pair = fold(keep, swap(send, "chan", 1), "chan", 0)
        return (normed, qkv, mixed, logs), pair, plain(conv_up.T)

    ((normed_one, qkv, mixed, logs), (keep, send), conv_up_t), (far, near) = beside(
        attend, [(mapped, "chan", top), (mapped, "chan", 1)]
    )
    mapped_parts = parts_beside(mapped, near, far)

    gain_all = conv_gain.astype(f32)[:, None]
    (conv_norm, conv_act, conv_slope, stats, conv_keep, conv_send), (got,) = beside(
        lambda: conv_forward(mapped_parts, conv_up_t, conv_down, gain_all, ids), [(send, "chan", 2)]
    )
    vit_band = own_band(vit_in).astype(f32)
    middle = vit_band + summed(finish(keep, got, "chan", 1))
    unit_two, inverse_two = standardize(middle, vit_eps)
    normed_band = (unit_two * gain_two).astype(bf16)
    ((conv_keep, conv_send), d_rows), (far, near) = beside(
        lambda: (fold(conv_keep, swap(conv_send, "chan", 1), "chan", 0), plain(d_merged.swapaxes(0, 1))),
        [(normed_band, "chan", top), (normed_band, "chan", 1)],
    )
    normed_parts = parts_beside(normed_band, near, far)

    def forward():
        out_keep, out_send, keep, send, *grads = feed_forward(
            normed_parts, d_rows, w_up, w_down, patchs, ids
        )
        out = fold(out_keep, swap(out_send, "chan", 1), "chan", 0)
        return out, fold(keep, swap(send, "chan", 1), "chan", 0), grads

    ((out_keep, out_send), (keep, send), grads), (got,) = beside(
        forward, [(conv_send, "chan", 2)]
    )

    own_scale = own_rows(layer_scale, own_channels).astype(f32)[:, None]
    conv_sum = finish(conv_keep, got, "chan", 1)
    vit = list(zip(grads[::2], grads[1::2]))
    (branch_maps, conv_result, pooled, *pieces), (got, vit_0) = beside(
        lambda: pool_forward(*conv_sum, conv_flat, own_scale, images, band, chans, ids),
        [(send, "chan", 2), (vit[0][1], "patch", 1)],
    )

    d_band = own_band(d_merged)
    d_two = finish(keep, got, "chan", 1)

    d_normed_two = summed(d_two)
    d_middle = d_band.astype(f32) + norm_back(d_normed_two, gain_two, unit_two, inverse_two)
    d_attended = d_middle.astype(bf16)
    g_ln_two = jnp.sum(d_normed_two * unit_two, axis=(0, 1))
    (w_own, conv_down_t, d_out), (vit_1, *got) = beside(
        lambda: (
            own_rows(w_proj, own_channels),
            plain(conv_down.T),
            plain(d_conv_out.reshape(own_channels, lanes)),
        ),
        [(vit[1][1], "patch", 1)] + [(pieces[offset], "chan", offset) for offset in range(1, chans)],
    )
    pieces[1:] = got

    kernel_three = jnp.pad(adapter_kernel.astype(f32).T, ((0, 7), (0, 0)))
    ((gated, d_smooth, g_gate_in, g_gate_out, g_adapter), vit_a, vit_b), (d_far, d_near, vit_2) = beside(
        lambda: (
            adapter(pieces, w_proj, kernel_three, gate_in, gate_out, d_band, ids),
            fold(vit[0][0], vit_0, "patch", 0),
            fold(vit[1][0], vit_1, "patch", 0),
        ),
        [(d_attended, "chan", top), (d_attended, "chan", 1), (vit[2][1], "patch", 1)],
    )
    d_parts = parts_beside(d_attended, d_near, d_far)
    vit_keep, vit_send = (jnp.concatenate(v, axis=2) for v in zip(vit_a, vit_b))
    shares = [g_gate_in, g_gate_out, g_adapter[:9].T, g_ln_two]
    (shared_keep, shared_send), (far, near, vit_3, vit_got) = beside(
        lambda: halves(share(shares, bf16, 128), "chan"),
        [(d_smooth, "chan", top), (d_smooth, "chan", 1), (vit[3][1], "patch", 1), (vit_send, "patch", 2)],
    )
    smooth_parts = parts_beside(d_smooth, near, far)
    vit_keep, vit_send = fold(vit_keep, vit_got, "patch", 1)
    shared_keep, shared_send = halves_at(shared_keep + swap(shared_send, "chan", 1), "chan", 1)

    ((d_result, d_branch, g_proj, g_scale), vit_a, vit_b), (shared_got, vit_got) = beside(
        lambda: (
            adapter_back(
                smooth_parts, w_own, kernel_three, pooled, d_out, branch_maps, own_scale, ids
            ),
            fold(vit[2][0], vit_2, "patch", 0),
            fold(vit[3][0], vit_3, "patch", 0),
        ),
        [(shared_send, "chan", 2), (vit_send, "patch", 4)],
    )
    up_sum = finish(vit_keep, vit_got, "patch", 2)
    vit_keep, vit_send = (jnp.concatenate(v, axis=2) for v in zip(vit_a, vit_b))
    shared = sum_scatter(shared_keep + shared_got, "chan", 2).reshape(own_channels, -1)
    early = jnp.concatenate([g_proj, shared], axis=1).reshape(patchs, rows, -1)
    early_keep, early_send = halves(halving_order(early, "patch"), "patch")

    def attend_back():
        keep, send, *grads = attention_backward(
            d_parts, normed_one, qkv, mixed, logs, w_three, w_attn, patchs, ids
        )
        return fold(keep, swap(send, "chan", 1), "chan", 0), grads

    ((one_keep, send), (att_keep, att_send)), (far, near, vit_got, early_got) = beside(
        attend_back,
        [(d_branch, "chan", top), (d_branch, "chan", 1), (vit_send, "patch", 2), (early_send, "patch", 1)],
    )
    branch_parts = parts_beside(d_branch, near, far)
    vit_keep, vit_send = fold(vit_keep, vit_got, "patch", 1)
    early_keep, early_send = fold(early_keep, early_got, "patch", 0)

    (d_all, *down), (one_got, got, att_got, vit_got, early_got) = beside(
        lambda: down_gradient(branch_parts, conv_act, patchs, ids),
        [
            (send, "chan", 2),
            (out_send, "chan", 2),
            (att_send, "patch", 1),
            (vit_send, "patch", 4),
            (early_send, "patch", 2),
        ],
    )
    down_sum = finish(vit_keep, vit_got, "patch", 2)
    out_sum = finish(out_keep, got, "chan", 1)
    att_keep, att_send = fold(att_keep, att_got, "patch", 0)
    early_keep, early_send = fold(early_keep, early_got, "patch", 1)

    (d_pre, conv_keep, conv_send, sums), (first_got, early_got, att_got) = beside(
        lambda: conv_backward(d_all, conv_down_t, conv_up, conv_slope, conv_norm, gain_all, ids),
        [(down[1], "patch", 1), (early_send, "patch", 4), (att_send, "patch", 2)],
    )
    early = summed(finish(early_keep, early_got, "patch", 2)).astype(bf16)
    att_keep, att_send = fold(att_keep, att_got, "patch", 1)

    def dealt():
        keep, sends = fold(conv_keep, swap(conv_send, "chan", 1), "chan", 0, 2)
        first = fold(down[0], first_got, "patch", 0)
        return keep, sends, first, sums + swap(sums, "chan", 1)

    (conv_keep, sends, (first_keep, first_send), sums), (att_got,) = beside(
        dealt, [(att_send, "patch", 4)]
    )
    att_sum = finish(att_keep, att_got, "patch", 2)
    (up, merged), (near_got, sums_got, second_got, first_got, own_early) = beside(
        lambda: (
            weight_gradient(conv_norm, d_pre, patchs, ids),
            (middle + summed(out_sum) + gated).astype(bf16).swapaxes(0, 1),
        ),
        [
            (sends[0], "chan", 2),
            (sums, "chan", 2),
            (down[3], "patch", 1),
            (first_send, "patch", 2),
            (early, ("patch", "chan"), places),
        ],
    )
    first_keep, first_send = fold(first_keep, first_got, "patch", 1)
    second_keep, second_send = fold(down[2], second_got, "patch", 0)

    def back_one():
        d_normed_one = summed(finish(one_keep, one_got, "chan", 1))
        unit_one, inverse_one = standardize(vit_band, vit_eps)
        g_vit = d_middle + norm_back(d_normed_one, gain_one, unit_one, inverse_one)
        return (
            g_vit.astype(bf16),
            halves(share([jnp.sum(d_normed_one * unit_one, axis=(0, 1))], f32, 1), "chan"),
            sum_all(sums + sums_got, "chan", 2) * (1.0 / channels),
            summed(att_sum),
            conv_result.reshape(conv_in.shape),
        )

    (g_vit, (one_keep, one_send), sums, att_grads, conv_out), (far_got, third_got, first_got, second_got) = beside(
        back_one,
        [
            (sends[1], "chan", 2),
            (up[1], "patch", 1),
            (first_send, "patch", 4),
            (second_send, "patch", 2),
        ],
    )
    first_sum = finish(first_keep, first_got, "patch", 2)
    second_keep, second_send = fold(second_keep, second_got, "patch", 1)
    third_keep, third_send = fold(up[0], third_got, "patch", 0)
    keep_near, keep_far = conv_keep[..., : lanes // 2], conv_keep[..., lanes // 2 :]
    (near, near_got), (far, far_got) = (
        finish(keep_near, near_got, "chan", 1), finish(keep_far, far_got, "chan", 1)
    ) if chans > 4 else ((conv_keep[0], near_got[0]), (None, far_got[0]))

    own_gain = own_rows(conv_gain, own_channels).astype(f32)[:, None]
    conv_sum = near if far is None else jnp.concatenate([near, far], axis=1)
    (g_conv_in, g_kernel, g_gain), (fourth_got, second_got, third_got, vit_far, vit_near, one_got) = beside(
        lambda: depthwise_back(
            conv_sum, near_got, far_got, mapped, stats, sums, own_gain, conv_flat, weights, d_result, images
        ),
        [
            (up[3], "patch", 1),
            (second_send, "patch", 4),
            (third_send, "patch", 2),
            (g_vit, "chan", top),
            (g_vit, "chan", 1),
            (one_send, "chan", 1),
        ],
    )
    second_sum = finish(second_keep, second_got, "patch", 2)
    third_keep, third_send = fold(third_keep, third_got, "patch", 1)
    fourth_keep, fourth_send = fold(up[2], fourth_got, "patch", 0)
    shared_one = sum_scatter(one_keep + one_got, "chan", 1).reshape(own_channels, -1)
    late = jnp.concatenate([g_kernel, g_gain[:, None], g_scale[:, :1], shared_one], axis=1)
    late = jnp.pad(late, ((0, 0), (0, -late.shape[1] % 128)))
    late = halving_order(late.reshape(patchs, rows, -1), "patch")
    late_keep, late_send = halves(late, "patch")

    def late_sum():
        total = sum_scatter(late_keep + swap(late_send, "patch", 1), "patch", 1)
        whole_rows = jnp.zeros((tokens, images, width), f32)
        for offset, part in enumerate(parts_beside(g_vit, vit_near, vit_far)):
            whole_rows = lax.dynamic_update_slice_in_dim(
                whole_rows, part.swapaxes(0, 1).astype(f32), (me ^ offset) * band, 0
            )
        return total, plain(whole_rows)

    (late, g_vit_in), (fourth_got, third_got) = beside(
        late_sum, [(fourth_send, "patch", 2), (third_send, "patch", 4)]
    )
    fourth_keep, fourth_send = fold(fourth_keep, fourth_got, "patch", 1)
    third_sum = finish(third_keep, third_got, "patch", 2)

    def last():
        own = own_early[:, :width].astype(f32), unshare(own_early[:, width:], shares)
        return summed(up_sum), summed(down_sum), summed(first_sum), summed(second_sum), summed(third_sum), own

    (g_up, g_down, first, second, third, (g_proj, pieces)), (fourth_got, own_late) = beside(
        last, [(fourth_send, "patch", 4), (late, ("patch", "chan"), places)]
    )
    g_conv_down = jnp.concatenate([first, second], axis=1)
    g_gate_in, g_gate_out, g_adapter, g_ln_two = pieces
    fourth_sum = finish(fourth_keep, fourth_got, "patch", 2)
    g_conv_up = jnp.concatenate([third, summed(fourth_sum)], axis=1)
    (g_ln_one,) = unshare(own_late[:, 51:52], [ln_one])
    qkv_width = 3 * own_width
    return (
        merged,
        conv_out,
        g_vit_in,
        g_conv_in,
        g_ln_one,
        att_grads[:, :qkv_width].reshape(-1, 3, own_width),
        att_grads[:, qkv_width:],
        g_ln_two,
        g_up,
        g_down,
        own_late[:, :49],
        own_late[:, 49],
        g_conv_up,
        g_conv_down,
        own_late[:, 50],
        g_proj,
        g_adapter,
        g_gate_in,
        g_gate_out,
    )


def solution(mesh):
    in_specs = (
        P(None, "patch", None),
        P("chan", "patch", None),
        P(),
        P(None, None, "chan"),
        P(None, "chan"),
        P(),
        P(None, "chan"),
        P(None, "chan"),
        P(),
        P(),
        P(None, "chan"),
        P(None, "chan"),
        P(),
        P(),
        P(),
        P(),
        P(),
        P(None, "patch", None),
        P("chan", "patch", None),
    )
    out_specs = (
        P("chan", "patch", None),
        P("chan", "patch", None),
        P(None, "patch", None),
        P("chan", "patch", None),
        P(("patch", "chan")),
        P("patch", None, "chan"),
        P("patch", "chan"),
        P(("patch", "chan")),
        P("patch", "chan"),
        P("patch", "chan"),
        P(("patch", "chan"), None),
        P(("patch", "chan")),
        P("patch", "chan"),
        P("patch", "chan"),
        P(("patch", "chan")),
        P(("patch", "chan"), None),
        P(("patch", "chan"), None),
        P(("patch", "chan"), None),
        P(("patch", "chan"), None),
    )
    return jax.shard_map(body, mesh=mesh, in_specs=in_specs, out_specs=out_specs, check_vma=False)
```

```python
import math

import jax
import jax.numpy as jnp
import numpy as np
from jax import lax
from jax.experimental import pallas as pl
from jax.experimental.layout import Layout, with_layout_constraint
from jax.experimental.pallas import tpu as pltpu
from jax.sharding import PartitionSpec as P

HEAD_DIM = 64
GRID = 24
MAP = 32
TAPS = 7
GROUP = 32
WIDE = 256

vit_eps = 1e-05
conv_eps = 1e-06
f32 = jnp.float32
bf16 = jnp.bfloat16
MIB = 2**20


def block_of(size, most, unit):
    best = unit
    for candidate in range(unit, most + 1, unit):
        if size % candidate == 0:
            best = candidate
    return best if size % best == 0 else size


def bit_count(size):
    return size.bit_length() - 1


def reverse_bits(value, bits):
    return sum(((value >> k) & 1) << (bits - 1 - k) for k in range(bits))


def swap(values, axis, other):
    count = lax.axis_size(axis)
    return lax.ppermute(values, axis, [(i, i ^ other) for i in range(count)])


def move(values, axis, other):
    return swap(values, axis, other) if isinstance(other, int) else lax.ppermute(values, axis, other)


def beside(work, sends):
    def run():
        return work(), [move(*send) for send in sends]

    def skip():
        return jax.tree.map(lambda v: jnp.zeros(v.shape, v.dtype), jax.eval_shape(run))

    return lax.optimization_barrier(lax.cond(lax.axis_index("chan") < lax.axis_size("chan"), run, skip))


def fold(keep, got, axis, bit, parts=1):
    shape = keep.shape
    half = shape[0] // 2
    flat = [v.reshape(shape[0], -1, shape[-1]) for v in (keep, got)]
    rows, columns = flat[0].shape[1:]
    step = block_of(rows, max(16, MIB // (2 * columns)), 8)
    mine = ((lax.axis_index(axis) >> (bit + 1)) & 1).astype(jnp.int32)[None]

    def kernel(_, kept, came, kept_far, came_far, keep_ref, *send_refs):
        keep_ref[...] = (kept[...].astype(f32) + came[...].astype(f32)).astype(keep_ref.dtype)
        total = (kept_far[...].astype(f32) + came_far[...].astype(f32)).astype(keep_ref.dtype)
        for part, ref in enumerate(send_refs):
            ref[...] = total[..., part * (columns // parts) : (part + 1) * (columns // parts)]

    near = pl.BlockSpec((1, step, columns), lambda i, r, own: (own[0] * half + i, r, 0))
    far = pl.BlockSpec((1, step, columns), lambda i, r, own: ((1 - own[0]) * half + i, r, 0))
    place = lambda width: pl.BlockSpec((1, step, width), lambda i, r, own: (i, r, 0))
    shape_of_part = lambda width: jax.ShapeDtypeStruct((half, rows, width), keep.dtype)
    out = pl.pallas_call(
        kernel,
        grid_spec=pltpu.PrefetchScalarGridSpec(
            num_scalar_prefetch=1,
            grid=(half, rows // step),
            in_specs=[near, near, far, far],
            out_specs=[place(columns)] + [place(columns // parts)] * parts,
        ),
        out_shape=[shape_of_part(columns)] + [shape_of_part(columns // parts)] * parts,
        compiler_params=pltpu.CompilerParams(vmem_limit_bytes=32 * MIB),
        cost_estimate=pl.CostEstimate(flops=int(2e9), bytes_accessed=6 * keep.size, transcendentals=0),
    )(mine, *flat, *flat)
    out = [v.reshape((half,) + shape[1:-1] + v.shape[-1:]) for v in out]
    return (out[0], out[1]) if parts == 1 else (out[0], out[1:])


def finish(keep, got, axis, bit):
    while bit + 1 < bit_count(lax.axis_size(axis)):
        keep, send = fold(keep, got, axis, bit)
        bit += 1
        got = swap(send, axis, 1 << bit)
    return keep[0], got[0]


def plain(values):
    return with_layout_constraint(values, Layout(tuple(range(values.ndim))))


def halves(blocks, axis):
    return halves_at(blocks, axis, 0)


def halves_at(blocks, axis, bit):
    mine = (lax.axis_index(axis) >> bit) & 1
    half = blocks.shape[0] // 2
    return tuple(lax.dynamic_slice_in_dim(blocks, which * half, half, 0) for which in (mine, 1 - mine))


def sum_scatter(values, axis, first=0):
    for bit in range(first, bit_count(lax.axis_size(axis))):
        mine = (lax.axis_index(axis) >> bit) & 1
        half = values.shape[0] // 2
        keep = lax.dynamic_slice_in_dim(values, mine * half, half, 0)
        send = lax.dynamic_slice_in_dim(values, (1 - mine) * half, half, 0)
        values = keep + swap(send, axis, 1 << bit)
    return values[0]


def halving_order(values, axis):
    count = lax.axis_size(axis)
    bits = bit_count(count)
    return jnp.stack([values[reverse_bits(j, bits)] for j in range(count)])


def parts_beside(block, near, far):
    top = bit_count(lax.axis_size("chan")) - 1
    parts = {0: block, 1 << top: far}
    for bit in reversed(range(1, top)):
        for offset in list(parts):
            parts[offset | (1 << bit)] = swap(parts[offset], "chan", 1 << bit)
    parts[1] = near
    for offset in list(parts):
        if offset > 1:
            parts[offset | 1] = swap(parts[offset], "chan", 1)
    return [parts[offset] for offset in sorted(parts)]


def sum_all(values, axis, first=0):
    for bit in range(first, bit_count(lax.axis_size(axis))):
        values = values + swap(values, axis, 1 << bit)
    return values


def lane_shift(values, step):
    count = values.shape[-1]
    step = step % count
    return values if step == 0 else pltpu.roll(values, count - step, 1)


def fill_masks(col_ref, row_ref):
    lanes = col_ref.shape[-1]
    place = lax.broadcasted_iota(jnp.int32, (GROUP, lanes), 1)
    col = place % MAP
    row = (place // MAP) % MAP
    for tap in range(TAPS):
        step = tap - TAPS // 2
        for ref, spot in ((col_ref, col), (row_ref, row)):
            ref[tap] = ((spot + step >= 0) & (spot + step < MAP)).astype(f32).astype(bf16)


def tap_weights(kernel):
    tap = np.arange(TAPS * TAPS)[:, None]
    spot = np.arange(TAPS * WIDE)[None, :]
    pick = (tap == (spot // WIDE) * TAPS + (spot % WIDE) // GROUP) & (spot % WIDE < TAPS * GROUP)
    own = (jnp.arange(kernel.shape[0])[:, None] % GROUP) == jnp.asarray(spot % GROUP)
    spread = jnp.dot(kernel, jnp.asarray(pick.astype(bf16)), preferred_element_type=f32)
    return jnp.where(own, spread, 0.0).astype(bf16)


def stacked_weights(k_ref):
    blocks = [k_ref[:, r * WIDE : r * WIDE + TAPS * GROUP] for r in range(TAPS)]
    return jnp.concatenate(blocks, axis=0)


def depthwise_kernel(x_ref, k_ref, o_ref, s_ref, col_ref, row_ref):
    @pl.when(pl.program_id(0) == 0)
    def _():
        fill_masks(col_ref, row_ref)

    x = x_ref[...]
    lanes = x.shape[1]
    for tap in range(TAPS):
        step = tap - TAPS // 2
        moved = lane_shift(x, step)
        s_ref[tap] = moved if step == 0 else moved * col_ref[tap]
    rows = jnp.dot(
        stacked_weights(k_ref), s_ref[...].reshape(TAPS * GROUP, lanes), preferred_element_type=f32
    )
    total = None
    for tap in range(TAPS):
        step = tap - TAPS // 2
        part = rows[tap * GROUP : (tap + 1) * GROUP]
        if step != 0:
            part = (lane_shift(part.astype(bf16), MAP * step) * row_ref[tap]).astype(f32)
        total = part if total is None else total + part
    o_ref[...] = total.astype(o_ref.dtype)


def depthwise(x, weights):
    channels, lanes = x.shape
    return pl.pallas_call(
        depthwise_kernel,
        grid=(channels // GROUP,),
        in_specs=[
            pl.BlockSpec((GROUP, lanes), lambda i: (i, 0)),
            pl.BlockSpec((GROUP, TAPS * WIDE), lambda i: (i, 0)),
        ],
        out_specs=pl.BlockSpec((GROUP, lanes), lambda i: (i, 0)),
        out_shape=jax.ShapeDtypeStruct((channels, lanes), bf16),
        scratch_shapes=[pltpu.VMEM((TAPS, GROUP, lanes), bf16)] * 3,
        compiler_params=pltpu.CompilerParams(vmem_limit_bytes=32 * MIB),
        cost_estimate=pl.CostEstimate(
            flops=int(8 * 1.1e9), bytes_accessed=4 * channels * lanes, transcendentals=0
        ),
    )(x, weights)


def depthwise_back_kernel(
    keep_ref, got_ref, m_ref, stat_ref, sum_ref, gain_ref, x_ref, k_ref, add_ref,
    gx_ref, gk_ref, gg_ref, t_ref, s_ref, col_ref, row_ref,
):
    @pl.when(pl.program_id(0) == 0)
    def _():
        fill_masks(col_ref, row_ref)

    x = x_ref[...]
    lanes = x.shape[1]
    inverse = stat_ref[1:2]
    unit = (m_ref[...].astype(f32) - stat_ref[0:1]) * inverse
    grad = keep_ref[...].astype(f32) + got_ref[...].astype(f32)
    gg_ref[...] = jnp.broadcast_to(jnp.sum(grad * unit, axis=1, keepdims=True), gg_ref.shape)
    d = (inverse * (grad * gain_ref[...] - sum_ref[0:1] - unit * sum_ref[1:2])).astype(bf16)
    last = TAPS - 1
    for tap in range(TAPS):
        step = tap - TAPS // 2
        moved = lane_shift(d, -step)
        t_ref[tap] = moved if step == 0 else moved * col_ref[last - tap]
        moved = lane_shift(x, MAP * step)
        s_ref[tap] = moved if step == 0 else moved * row_ref[tap]
    t = t_ref[...].reshape(TAPS * GROUP, lanes)
    rows = jnp.dot(stacked_weights(k_ref), t, preferred_element_type=f32)
    total = add_ref[...]
    for tap in range(TAPS):
        step = tap - TAPS // 2
        part = rows[tap * GROUP : (tap + 1) * GROUP]
        if step != 0:
            part = (lane_shift(part.astype(bf16), -MAP * step) * row_ref[last - tap]).astype(f32)
        total = total + part
    cells = gx_ref.shape[2]
    for i in range(gx_ref.shape[1]):
        gx_ref[:, i, :] = total[:, i * cells : (i + 1) * cells]
    pairs = lax.dot_general(
        t, s_ref[...].reshape(TAPS * GROUP, lanes), (((1,), (1,)), ((), ())), preferred_element_type=f32
    )
    side = TAPS * GROUP
    first = lax.broadcasted_iota(jnp.int32, (side, side), 0)
    second = lax.broadcasted_iota(jnp.int32, (side, side), 1)
    own = jnp.where(first % GROUP == second % GROUP, pairs, 0.0)
    source = lax.broadcasted_iota(jnp.int32, (side, 128), 0)
    target = lax.broadcasted_iota(jnp.int32, (side, 128), 1)
    pick = (source // GROUP == target).astype(f32).astype(bf16)
    high = own.astype(bf16)
    low = (own - high.astype(f32)).astype(bf16)
    gk_ref[0] = jnp.dot(high, pick, preferred_element_type=f32) + jnp.dot(
        low, pick, preferred_element_type=f32
    )


def depthwise_back(keep, got, mapped, stats, sums, gain, x, weights, add, images):
    channels, lanes = x.shape
    groups = channels // GROUP
    rows = pl.BlockSpec((GROUP, lanes), lambda i: (i, 0))
    fixed = pl.BlockSpec((8, lanes), lambda i: (0, 0))
    gx, gk, gg = pl.pallas_call(
        depthwise_back_kernel,
        grid=(groups,),
        in_specs=[
            rows, rows, rows, fixed, fixed,
            pl.BlockSpec((GROUP, 1), lambda i: (i, 0)),
            rows,
            pl.BlockSpec((GROUP, TAPS * WIDE), lambda i: (i, 0)),
            rows,
        ],
        out_specs=[
            pl.BlockSpec((GROUP, images, lanes // images), lambda i: (i, 0, 0)),
            pl.BlockSpec((1, TAPS * GROUP, 128), lambda i: (i, 0, 0)),
            pl.BlockSpec((GROUP, 128), lambda i: (i, 0)),
        ],
        out_shape=[
            jax.ShapeDtypeStruct((channels, images, lanes // images), f32),
            jax.ShapeDtypeStruct((groups, TAPS * GROUP, 128), f32),
            jax.ShapeDtypeStruct((channels, 128), f32),
        ],
        scratch_shapes=[pltpu.VMEM((TAPS, GROUP, lanes), bf16)] * 4,
        compiler_params=pltpu.CompilerParams(vmem_limit_bytes=56 * MIB),
        cost_estimate=pl.CostEstimate(
            flops=int(16 * 1.1e9), bytes_accessed=14 * channels * lanes, transcendentals=0
        ),
    )(keep, got, mapped, stats, sums, gain, x, weights, add)
    gk = gk[:, :, :TAPS].reshape(groups, TAPS, GROUP, TAPS).transpose(0, 2, 3, 1)
    return gx, gk.reshape(channels, TAPS * TAPS), gg[:, 0]


def gelu_both(u):
    share = 0.5 * (1.0 + lax.erf(u * (1.0 / math.sqrt(2.0))))
    return u * share, share + u * jnp.exp(-0.5 * u * u) * (1.0 / math.sqrt(2.0 * math.pi))


def pool_table():
    out_index = np.arange(GRID)
    first_row = out_index * MAP // GRID
    last_row = ((out_index + 1) * MAP + GRID - 1) // GRID
    source_index = np.arange(MAP)
    inside = (source_index[None, :] >= first_row[:, None]) & (
        source_index[None, :] < last_row[:, None]
    )
    single = inside.astype(np.float32) / (last_row - first_row)[:, None].astype(np.float32)
    table = single[:, None, :, None] * single[None, :, None, :]
    return table.reshape(GRID * GRID, MAP * MAP)


PACE = 1.1e9


def mm(a, b):
    return jnp.dot(a, b, preferred_element_type=f32)


def mm_nt(a, b):
    return lax.dot_general(a, b, (((1,), (1,)), ((), ())), preferred_element_type=f32)


def mm_tn(a, b):
    return lax.dot_general(a, b, (((0,), (0,)), ((), ())), preferred_element_type=f32)


def whole(shape):
    return pl.BlockSpec(shape, lambda *_: (0,) * len(shape), pipeline_mode=pl.Buffered(1))


def shape_of(shape, dtype=bf16):
    return jax.ShapeDtypeStruct(shape, dtype)


def call(kernel, ids, grid, args, in_specs, outs, out_specs, scratch=(), micros=10, vmem=56, earlier=(), through=(), into=()):
    count = len(earlier)
    passed = len(through)
    ins = len(args)
    results = len(outs)

    def run(ids_ref, *refs):
        refs = refs[count + passed + len(into) :]
        kernel(ids_ref, *refs[: ins + results], *refs[ins + results + passed :])

    bytes_accessed = sum(v.size * v.dtype.itemsize for v in list(args) + list(outs))
    return pl.pallas_call(
        run,
        grid_spec=pltpu.PrefetchScalarGridSpec(
            num_scalar_prefetch=1,
            grid=grid,
            in_specs=[pl.BlockSpec(memory_space=pl.ANY)] * (count + passed + len(into)) + in_specs,
            out_specs=out_specs + [pl.BlockSpec(memory_space=pl.ANY)] * passed,
            scratch_shapes=scratch,
        ),
        out_shape=outs + [jax.ShapeDtypeStruct(v.shape, v.dtype) for v in through],
        input_output_aliases={1 + count + i: results + i for i in range(passed)}
        | {1 + count + passed + i: i for i in range(len(into))},
        compiler_params=pltpu.CompilerParams(vmem_limit_bytes=vmem * MIB),
        cost_estimate=pl.CostEstimate(flops=int(micros * PACE), bytes_accessed=int(bytes_accessed), transcendentals=0),
    )(ids, *earlier, *through, *into, *args)


def deal(stack_ref, keep_ref, send_ref, mine, lead=()):
    half = stack_ref.shape[0] // 2
    for j in range(half):
        block = 2 * reverse_bits(j, bit_count(half))
        keep_ref[(j,) + lead] = stack_ref[block + mine]
        send_ref[(j,) + lead] = stack_ref[block + 1 - mine]


def dealt_rows(w_ref, own, refs, operand, mine):
    half = refs[0].shape[0]
    for ref, bit in zip(refs, (mine, 1 - mine)):
        for j in range(half):
            block = 2 * reverse_bits(j, bit_count(half)) + bit
            rows = w_ref[pl.ds(pl.multiple_of(block * own, 16), own), :]
            ref[j] = mm(rows, operand[...]).astype(bf16)


def conv_forward(parts, up_t, down, gain, ids, earlier=(), through=(), part=0, into=()):
    count = len(parts)
    own, lanes = parts[0].shape
    channels = own * count
    hidden = up_t.shape[0]
    bn = block_of(lanes // 2, 512, 128)
    first = part * (lanes // 2 // bn)
    step = block_of(hidden, 256, 128)

    def kernel(ids_ref, *refs):
        part_refs = refs[:count]
        up_ref, down_ref, gain_ref, cn_ref, h_ref, s_ref, stat_ref, keep_ref, send_ref = refs[count:]
        me = ids_ref[0]
        mean = sum(jnp.sum(part[...].astype(f32), axis=0, keepdims=True) for part in part_refs) * (1.0 / channels)
        square = sum(
            jnp.sum((part[...].astype(f32) - mean) ** 2, axis=0, keepdims=True) for part in part_refs
        ) * (1.0 / channels)
        inverse = lax.rsqrt(square + conv_eps)
        stat_ref[...] = jnp.concatenate([mean, inverse, jnp.zeros((6, bn), f32)], axis=0)
        for offset, part in enumerate(part_refs):
            rows = pl.ds(pl.multiple_of((me ^ offset) * own, 16), own)
            cn_ref[rows, :] = ((part[...].astype(f32) - mean) * inverse * gain_ref[rows, :]).astype(bf16)
        for f in range(0, hidden, step):
            act, slope = gelu_both(mm(up_ref[f : f + step], cn_ref[...]))
            h_ref[f : f + step] = act.astype(bf16)
            s_ref[f : f + step] = slope.astype(bf16)
        dealt_rows(down_ref, own, (keep_ref, send_ref), h_ref, me & 1)

    tall = lambda rows: pl.BlockSpec((rows, bn), lambda j, _: (0, j + first))
    half = pl.BlockSpec((count // 2, own, bn), lambda j, _: (0, 0, j + first))
    return call(
        kernel,
        ids,
        (lanes // 2 // bn,),
        (*parts, up_t, down, gain),
        [tall(own)] * count + [whole(up_t.shape), whole(down.shape), whole(gain.shape)],
        [
            shape_of((channels, lanes)),
            shape_of((hidden, lanes)),
            shape_of((hidden, lanes)),
            shape_of((8, lanes), f32),
            shape_of((count // 2, own, lanes)),
            shape_of((count // 2, own, lanes)),
        ],
        [tall(channels), tall(hidden), tall(hidden), tall(8), half, half],
        micros=36,
        earlier=earlier,
        through=through,
        into=into,
    )


def conv_backward(d_all, down_t, up, slope, normed, gain, ids, earlier=(), through=()):
    channels, lanes = d_all.shape
    hidden = down_t.shape[0]
    count = lax.axis_size("chan")
    own = channels // count
    bn = block_of(lanes, 512, 128)
    step = block_of(hidden, 512, 128)

    def kernel(ids_ref, d_ref, down_ref, up_ref, s_ref, n_ref, gain_ref, du_ref, keep_ref, send_ref, sum_ref):
        for f in range(0, hidden, step):
            du = mm(down_ref[f : f + step], d_ref[...]) * s_ref[f : f + step].astype(f32)
            du_ref[f : f + step] = du.astype(bf16)
        mine = ids_ref[0] & 1
        first = second = jnp.zeros((1, bn), f32)
        for ref, bit in ((keep_ref, mine), (send_ref, 1 - mine)):
            for j in range(count // 2):
                block = 2 * reverse_bits(j, bit_count(count // 2)) + bit
                rows = pl.ds(pl.multiple_of(block * own, 16), own)
                part = mm(up_ref[rows, :], du_ref[...])
                ref[j] = part.astype(bf16)
                first += jnp.sum(part * gain_ref[rows, :], axis=0, keepdims=True)
                second += jnp.sum(part * n_ref[rows, :].astype(f32), axis=0, keepdims=True)
        sum_ref[...] = jnp.concatenate([first, second, jnp.zeros((6, bn), f32)], axis=0)

    tall = lambda rows: pl.BlockSpec((rows, bn), lambda j, _: (0, j))
    half = pl.BlockSpec((count // 2, own, bn), lambda j, _: (0, 0, j))
    return call(
        kernel,
        ids,
        (lanes // bn,),
        (d_all, down_t, up, slope, normed, gain),
        [tall(channels), whole(down_t.shape), whole(up.shape), tall(hidden), tall(channels), whole(gain.shape)],
        [
            shape_of((hidden, lanes)),
            shape_of((count // 2, own, lanes)),
            shape_of((count // 2, own, lanes)),
            shape_of((8, lanes), f32),
        ],
        [tall(hidden), half, half, tall(8)],
        micros=28,
        earlier=earlier,
        through=through,
    )


def dealt_halves(size, patchs, columns, bn):
    half = pl.BlockSpec((patchs // 2, size, bn), lambda j, _: (0, 0, 0))

    def deal_columns(product, stack_ref, refs, mine):
        stack_ref[...] = product.astype(bf16).reshape(patchs, size, bn)
        for part in range(2):

            @pl.when(pl.program_id(0) == part)
            def _(part=part):
                deal(stack_ref, refs[2 * part], refs[2 * part + 1], mine)

    return [half] * 4, [shape_of((patchs // 2, size, columns // 2))] * 4, deal_columns


def down_gradient(parts, act, patchs, ids):
    count = len(parts)
    own, lanes = parts[0].shape
    channels = own * count
    hidden = act.shape[0]
    bn = hidden // 2
    size = channels // patchs
    specs, shapes, deal_columns = dealt_halves(size, patchs, hidden, bn)

    def kernel(ids_ref, *refs):
        part_refs = refs[:count]
        b_ref, d_ref, *out_refs, o_ref = refs[count:]

        @pl.when(pl.program_id(0) == 0)
        def _():
            for offset, part in enumerate(part_refs):
                d_ref[pl.ds(pl.multiple_of((ids_ref[0] ^ offset) * own, 16), own), :] = part[...]

        deal_columns(mm_nt(d_ref[...], b_ref[...]), o_ref, out_refs, ids_ref[1] & 1)

    return call(
        kernel,
        ids,
        (2,),
        (*parts, act),
        [whole(parts[0].shape)] * count + [pl.BlockSpec((bn, lanes), lambda j, _: (j, 0))],
        [shape_of((channels, lanes))] + shapes,
        [whole((channels, lanes))] + specs,
        [pltpu.VMEM((patchs, size, bn), bf16)],
        micros=18,
    )


def weight_gradient(a, b, patchs, ids):
    rows, depth = a.shape
    columns = b.shape[0]
    bn = columns // 2
    size = rows // patchs
    specs, shapes, deal_columns = dealt_halves(size, patchs, columns, bn)

    def kernel(ids_ref, a_ref, b_ref, *refs):
        deal_columns(mm_nt(a_ref[...], b_ref[...]), refs[-1], refs[:-1], ids_ref[1] & 1)

    return call(
        kernel,
        ids,
        (2,),
        (a, b),
        [whole(a.shape), pl.BlockSpec((bn, depth), lambda j, _: (j, 0))],
        shapes,
        specs,
        [pltpu.VMEM((patchs, size, bn), bf16)],
        micros=18,
    )


def pool_forward(keep, got, conv_flat, scale, images, band, chans, ids, earlier=(), through=()):
    own, lanes = keep.shape
    cells = lanes // images
    table = pool_table()
    tokens = table.shape[0]
    reach = band + 2 * GRID
    padded = jnp.asarray(np.pad(table, ((GRID, GRID), (0, 0))))

    def kernel(ids_ref, keep_ref, got_ref, c_ref, scale_ref, t_ref, p_ref, branch_ref, result_ref, pooled_ref, *pieces):
        branch = keep_ref[...].astype(f32) + got_ref[...].astype(f32)
        branch_ref[...] = branch.astype(bf16)
        result = (c_ref[...].astype(f32) + scale_ref[...] * branch).astype(bf16)
        result_ref[...] = result
        pooled_ref[0] = mm(result, t_ref[...]).astype(bf16)
        for offset, piece in enumerate(pieces):
            start = pl.multiple_of((ids_ref[0] ^ offset) * band, 8)
            rows = p_ref[pl.ds(start, reach), :].astype(bf16)
            piece[0] = mm_nt(rows, result).astype(bf16)

    flat = pl.BlockSpec((own, cells), lambda i, _: (0, i))
    return call(
        kernel,
        ids,
        (images,),
        (keep, got, conv_flat, scale, jnp.asarray(table.T.astype(bf16)), padded),
        [flat, flat, flat, whole(scale.shape), whole((cells, tokens)), whole(padded.shape)],
        [shape_of((own, lanes))] * 2
        + [shape_of((images, own, tokens))]
        + [shape_of((images, reach, own))] * chans,
        [flat, flat, pl.BlockSpec((1, own, tokens), lambda i, _: (i, 0, 0))]
        + [pl.BlockSpec((1, reach, own), lambda i, _: (i, 0, 0))] * chans,
        micros=9,
        earlier=earlier,
        through=through,
    )


def row_moves(field, spots, step):
    if step == 0:
        return field
    count = field.shape[0]
    moved = pltpu.roll(field, (-step) % count, 0)
    column = spots % GRID + step
    return jnp.where((column >= 0) & (column < GRID), moved, 0.0)


def adapter(pieces, w_proj, kernel_three, gate_in, gate_out, d_band, ids, earlier=(), through=()):
    chans = len(pieces)
    images, reach, own = pieces[0].shape
    width = w_proj.shape[1]
    gate = gate_in.shape[1]
    band = reach - 2 * GRID

    def kernel(ids_ref, *refs):
        piece_refs = refs[:chans]
        proj_ref, k_ref, in_ref, out_ref, d_ref, gs_ref, ds_ref, gib_ref, gob_ref, gk_ref, gi_ref, go_ref = refs[chans:]
        me = ids_ref[0]

        @pl.when(pl.program_id(0) == 0)
        def _():
            gi_ref[...] = jnp.zeros_like(gi_ref)
            go_ref[...] = jnp.zeros_like(go_ref)
            gk_ref[...] = jnp.zeros_like(gk_ref)

        field = None
        for offset, piece in enumerate(piece_refs):
            start = pl.multiple_of((me ^ offset) * own, 16)
            term = mm(piece[0], proj_ref[pl.ds(start, own), :])
            field = term if field is None else field + term
        field = field.astype(bf16).astype(f32)
        spots = lax.broadcasted_iota(jnp.int32, (reach, 1), 0)
        moved = [row_moves(field, spots, step) for step in (-1, 0, 1)]
        smooth = None
        for t in range(9):
            term = k_ref[t : t + 1, :] * moved[t % 3][GRID * (t // 3) : GRID * (t // 3) + band]
            smooth = term if smooth is None else smooth + term
        rows = smooth.astype(bf16)
        act, slope = gelu_both(mm(rows, in_ref[...]))
        act = act.astype(bf16)
        value = jnp.tanh(mm(act, out_ref[...]))
        gs_ref[0] = value * smooth
        d = d_ref[0].astype(f32)
        d_logit = (d * smooth * (1.0 - value * value)).astype(bf16)
        d_gate = (mm_nt(d_logit, out_ref[...]) * slope).astype(bf16)
        d_smooth = d * value + mm_nt(d_gate, in_ref[...])
        ds_ref[0] = d_smooth.astype(bf16)
        go_ref[...] += mm_tn(act, d_logit)
        gi_ref[...] += mm_tn(rows, d_gate)
        for t in range(9):
            seen = moved[t % 3][GRID * (t // 3) : GRID * (t // 3) + band]
            gk_ref[t : t + 1, :] += jnp.sum(d_smooth * seen, axis=0, keepdims=True)

        @pl.when(pl.program_id(0) == images - 1)
        def _():
            gib_ref[...] = gi_ref[...].astype(bf16)
            gob_ref[...] = go_ref[...].astype(bf16)

    per = lambda rows, cols: pl.BlockSpec((1, rows, cols), lambda i, _: (i, 0, 0))
    kept = lambda *shape: pl.BlockSpec(shape, lambda i, _: (0, 0))
    return call(
        kernel,
        ids,
        (images,),
        (*pieces, w_proj, kernel_three, gate_in, gate_out, d_band),
        [per(reach, own)] * chans
        + [whole(w_proj.shape), whole(kernel_three.shape), whole(gate_in.shape), whole(gate_out.shape), per(band, width)],
        [
            shape_of((images, band, width), f32),
            shape_of((images, band, width)),
            shape_of((width, gate)),
            shape_of((gate, width)),
            shape_of((16, width), f32),
        ],
        [per(band, width), per(band, width), kept(width, gate), kept(gate, width), kept(16, width)],
        [pltpu.VMEM((width, gate), f32), pltpu.VMEM((gate, width), f32)],
        micros=13,
        earlier=earlier,
        through=through,
    )


def adapter_back(parts, w_own, kernel_three, pooled, d_out, branch, scale, ids, earlier=(), through=()):
    chans = len(parts)
    images, band, width = parts[0].shape
    own, lanes = d_out.shape
    cells = lanes // images
    tokens = band * chans
    table = jnp.asarray(pool_table().astype(bf16))

    def kernel(ids_ref, *refs):
        part_refs = refs[:chans]
        w_ref, k_ref, pooled_ref, do_ref, branch_ref, scale_ref, t_ref, dr_ref, db_ref, gpb_ref, gs_ref, f_ref, gp_ref = refs[chans:]
        me = ids_ref[0]

        @pl.when(pl.program_id(0) == 0)
        def _():
            gp_ref[...] = jnp.zeros_like(gp_ref)
            gs_ref[...] = jnp.zeros_like(gs_ref)
            f_ref[:GRID] = jnp.zeros((GRID, width), f32)
            f_ref[GRID + tokens :] = jnp.zeros((GRID, width), f32)

        for offset, part in enumerate(part_refs):
            start = pl.multiple_of((me ^ offset) * band + GRID, 8)
            f_ref[pl.ds(start, band), :] = part[0].astype(f32)
        field = f_ref[...]
        spots = lax.broadcasted_iota(jnp.int32, (tokens + 2 * GRID, 1), 0)
        moved = [row_moves(field, spots, -step) for step in (-1, 0, 1)]
        d_adapted = None
        for t in range(9):
            start = GRID * (2 - t // 3)
            term = k_ref[t : t + 1, :] * moved[t % 3][start : start + tokens]
            d_adapted = term if d_adapted is None else d_adapted + term
        d_adapted = d_adapted.astype(bf16)
        d_pooled = mm_nt(w_ref[...], d_adapted).astype(bf16)
        gp_ref[...] += mm(pooled_ref[0], d_adapted)
        d_result = do_ref[...].astype(f32) + mm(d_pooled, t_ref[...])
        dr_ref[...] = d_result
        db_ref[...] = (scale_ref[...] * d_result).astype(bf16)
        gs_ref[...] += jnp.sum(d_result * branch_ref[...].astype(f32), axis=1, keepdims=True)

        @pl.when(pl.program_id(0) == images - 1)
        def _():
            gpb_ref[...] = gp_ref[...].astype(bf16)

    flat = pl.BlockSpec((own, cells), lambda i, _: (0, i))
    per = lambda rows, cols: pl.BlockSpec((1, rows, cols), lambda i, _: (i, 0, 0))
    return call(
        kernel,
        ids,
        (images,),
        (*parts, w_own, kernel_three, pooled, d_out, branch, scale, table),
        [per(band, width)] * chans
        + [whole(w_own.shape), whole(kernel_three.shape), per(own, tokens), flat, flat, whole(scale.shape), whole(table.shape)],
        [
            shape_of((own, lanes), f32),
            shape_of((own, lanes)),
            shape_of((own, width)),
            shape_of((own, 128), f32),
        ],
        [flat, flat, pl.BlockSpec((own, width), lambda i, _: (0, 0)), pl.BlockSpec((own, 128), lambda i, _: (0, 0))],
        [pltpu.VMEM((tokens + 2 * GRID, width), f32), pltpu.VMEM((own, width), f32)],
        micros=14,
        earlier=earlier,
        through=through,
    )


def row_standard(values):
    center = values - jnp.mean(values, axis=-1, keepdims=True)
    inverse = lax.rsqrt(jnp.mean(center * center, axis=-1, keepdims=True) + vit_eps)
    return center * inverse


def stack_bands(stack_ref, values):
    count, band, _ = stack_ref.shape
    for b in range(count):
        stack_ref[b] = values[b * band : (b + 1) * band].astype(bf16)


def take_bands(rows_ref, part_refs, me):
    for offset, part in enumerate(part_refs):
        band = part.shape[1]
        start = pl.multiple_of((me ^ offset) * band, 8)
        rows_ref[pl.ds(start, band), :] = part[0].astype(f32)
    return rows_ref[...].astype(bf16)


def attention_forward(x, gain, w_qkv, w_attn, chans, ids, earlier=(), through=()):
    images, tokens, width = x.shape
    own = w_qkv.shape[2]
    heads = own // HEAD_DIM
    band = tokens // chans
    scale = 1.0 / math.sqrt(HEAD_DIM)

    def kernel(ids_ref, x_ref, gain_ref, qkv_w_ref, attn_ref, n_ref, qkv_ref, o_ref, log_ref, keep_ref, send_ref, stack_ref):
        normed = (row_standard(x_ref[0].astype(f32)) * gain_ref[...]).astype(bf16)
        n_ref[0] = normed
        q, k, v = (mm(normed, qkv_w_ref[t]).astype(bf16) for t in range(3))
        for t, part in enumerate((q, k, v)):
            qkv_ref[t, 0] = part
        mixed = []
        spot = lax.broadcasted_iota(jnp.int32, (tokens, 128), 1)
        logs = jnp.zeros((tokens, 128), f32)
        for h in range(heads):
            at = slice(h * HEAD_DIM, (h + 1) * HEAD_DIM)
            scores = mm_nt(q[:, at], k[:, at]) * scale
            most = jnp.max(scores, axis=-1, keepdims=True)
            powers = jnp.exp(scores - most)
            total = jnp.sum(powers, axis=-1, keepdims=True)
            logs = jnp.where(spot == h, most + jnp.log(total), logs)
            mixed.append(mm((powers * (1.0 / total)).astype(bf16), v[:, at]).astype(bf16))
        mixed = jnp.concatenate(mixed, axis=1)
        log_ref[0] = logs
        o_ref[0] = mixed
        stack_bands(stack_ref, mm_nt(mixed, attn_ref[...]))
        deal(stack_ref, keep_ref, send_ref, ids_ref[0] & 1, (0,))

    per = lambda cols: pl.BlockSpec((1, tokens, cols), lambda i, _: (i, 0, 0))
    half = pl.BlockSpec((chans // 2, 1, band, width), lambda i, _: (0, i, 0, 0))
    return call(
        kernel,
        ids,
        (images,),
        (x, gain, w_qkv, w_attn),
        [per(width), whole(gain.shape), whole(w_qkv.shape), whole(w_attn.shape)],
        [
            shape_of((images, tokens, width)),
            shape_of((3, images, tokens, own)),
            shape_of((images, tokens, own)),
            shape_of((images, tokens, 128), f32),
            shape_of((chans // 2, images, band, width)),
            shape_of((chans // 2, images, band, width)),
        ],
        [per(width), pl.BlockSpec((3, 1, tokens, own), lambda i, _: (0, i, 0, 0)), per(own), per(128), half, half],
        [pltpu.VMEM((chans, band, width), bf16)],
        micros=16,
        earlier=earlier,
        through=through,
    )


def feed_forward(parts, d_rows, w_up, w_down, patchs, ids, earlier=(), through=()):
    chans = len(parts)
    images, band, width = parts[0].shape
    tokens = band * chans
    hidden = w_up.shape[1]

    def kernel(ids_ref, *refs):
        part_refs = refs[:chans]
        (
            d_ref, up_ref, down_ref, keep_ref, send_ref, dkeep_ref, dsend_ref, *grad_refs,
            rows_ref, stack_ref, gu_ref, gd_ref, g_ref,
        ) = refs[chans:]
        me = ids_ref[0]
        step = pl.program_id(0)
        normed = take_bands(rows_ref, part_refs, me)
        act, slope = gelu_both(mm(normed, up_ref[...]))
        act = act.astype(bf16)
        stack_bands(stack_ref, mm_nt(act, down_ref[...]))
        deal(stack_ref, keep_ref, send_ref, me & 1, (0,))
        d = d_ref[0]
        d_pre = (mm(d, down_ref[...]) * slope).astype(bf16)
        stack_bands(stack_ref, mm_nt(d_pre, up_ref[...]))
        deal(stack_ref, dkeep_ref, dsend_ref, me & 1, (0,))
        gu = mm_tn(normed, d_pre)
        gd = mm_tn(d, act)

        @pl.when(step == 0)
        def _():
            gu_ref[...] = gu
            gd_ref[...] = gd

        @pl.when(step > 0)
        def _():
            gu_ref[...] += gu
            gd_ref[...] += gd

        @pl.when(step == images - 1)
        def _():
            for part in range(4):
                source = (gu_ref, gd_ref)[part // 2]
                columns = slice((part % 2) * part_width, (part % 2 + 1) * part_width)
                for b in range(patchs):
                    g_ref[b] = source[b * size : (b + 1) * size, columns].astype(bf16)
                deal(g_ref, grad_refs[2 * part], grad_refs[2 * part + 1], ids_ref[1] & 1)

    per = lambda rows: pl.BlockSpec((1, rows, width), lambda i, _: (i, 0, 0))
    half = pl.BlockSpec((chans // 2, 1, band, width), lambda i, _: (0, i, 0, 0))
    halves = shape_of((chans // 2, images, band, width))
    size = width // patchs
    part_width = hidden // 2
    grads = (patchs // 2, size, part_width)
    return call(
        kernel,
        ids,
        (images,),
        (*parts, d_rows, w_up, w_down),
        [per(band)] * chans + [per(tokens), whole(w_up.shape), whole(w_down.shape)],
        [halves] * 4 + [shape_of(grads)] * 8,
        [half] * 4 + [pl.BlockSpec(grads, lambda i, _: (0, 0, 0))] * 8,
        [
            pltpu.VMEM((tokens, width), f32),
            pltpu.VMEM((chans, band, width), bf16),
            pltpu.VMEM((width, hidden), f32),
            pltpu.VMEM((width, hidden), f32),
            pltpu.VMEM((patchs, size, part_width), bf16),
        ],
        micros=26,
        earlier=earlier,
        through=through,
    )


def attention_backward(parts, normed, qkv, mixed, logs, w_qkv, w_attn, patchs, ids, earlier=(), through=()):
    chans = len(parts)
    images, band, width = parts[0].shape
    tokens = band * chans
    own = w_attn.shape[1]
    heads = own // HEAD_DIM
    scale = 1.0 / math.sqrt(HEAD_DIM)

    def kernel(ids_ref, *refs):
        part_refs = refs[:chans]
        (
            n_ref, qkv_ref, o_ref, log_ref, qkv_w_ref, attn_ref, keep_ref, send_ref, gkeep_ref, gsend_ref,
            rows_ref, stack_ref, acc_ref, g_ref,
        ) = refs[chans:]
        me = ids_ref[0]
        step = pl.program_id(0)
        d = take_bands(rows_ref, part_refs, me)
        d_mixed = mm(d, attn_ref[...]).astype(bf16)
        q, k, v = (qkv_ref[t, 0] for t in range(3))
        grads = ([], [], [])
        for h in range(heads):
            at = slice(h * HEAD_DIM, (h + 1) * HEAD_DIM)
            soft = jnp.exp(mm_nt(q[:, at], k[:, at]) * scale - log_ref[0, :, h : h + 1])
            d_soft = mm_nt(d_mixed[:, at], v[:, at])
            across = jnp.sum(d_soft * soft, axis=-1, keepdims=True)
            d_scores = (soft * (d_soft - across)).astype(bf16)
            grads[0].append((mm(d_scores, k[:, at]) * scale).astype(bf16))
            grads[1].append((mm_tn(d_scores, q[:, at]) * scale).astype(bf16))
            grads[2].append(mm_tn(soft.astype(bf16), d_mixed[:, at]).astype(bf16))
        grads = [jnp.concatenate(v, axis=1) for v in grads]
        total = None
        for t in range(3):
            term = mm_nt(grads[t], qkv_w_ref[t])
            total = term if total is None else total + term
        stack_bands(stack_ref, total)
        deal(stack_ref, keep_ref, send_ref, me & 1, (0,))
        new = [mm_tn(n_ref[0], g) for g in grads] + [mm_tn(d, o_ref[0])]

        @pl.when(step == 0)
        def _():
            for t in range(4):
                acc_ref[:, t * own : (t + 1) * own] = new[t]

        @pl.when(step > 0)
        def _():
            for t in range(4):
                acc_ref[:, t * own : (t + 1) * own] += new[t]

        @pl.when(step == images - 1)
        def _():
            for b in range(patchs):
                g_ref[b] = acc_ref[b * size : (b + 1) * size].astype(bf16)
            deal(g_ref, gkeep_ref, gsend_ref, ids_ref[1] & 1)

    per = lambda rows, cols: pl.BlockSpec((1, rows, cols), lambda i, _: (i, 0, 0))
    half = pl.BlockSpec((chans // 2, 1, band, width), lambda i, _: (0, i, 0, 0))
    halves = shape_of((chans // 2, images, band, width))
    size = width // patchs
    out = (patchs // 2, size, 4 * own)
    return call(
        kernel,
        ids,
        (images,),
        (*parts, normed, qkv, mixed, logs, w_qkv, w_attn),
        [per(band, width)] * chans
        + [
            per(tokens, width),
            pl.BlockSpec((3, 1, tokens, own), lambda i, _: (0, i, 0, 0)),
            per(tokens, own),
            per(tokens, 128),
            whole(w_qkv.shape),
            whole(w_attn.shape),
        ],
        [halves] * 2 + [shape_of(out)] * 2,
        [half] * 2 + [pl.BlockSpec(out, lambda i, _: (0, 0, 0))] * 2,
        [
            pltpu.VMEM((tokens, width), f32),
            pltpu.VMEM((chans, band, width), bf16),
            pltpu.VMEM((width, 4 * own), f32),
            pltpu.VMEM((patchs, size, 4 * own), bf16),
        ],
        micros=24,
        earlier=earlier,
        through=through,
    )


def standardize(values, epsilon):
    center = values - jnp.mean(values, axis=-1, keepdims=True)
    inverse = lax.rsqrt(jnp.mean(center * center, axis=-1, keepdims=True) + epsilon)
    return center * inverse, inverse


def norm_back(grad, gain, unit, inverse):
    scaled = grad * gain
    return inverse * (
        scaled
        - jnp.mean(scaled, axis=-1, keepdims=True)
        - unit * jnp.mean(scaled * unit, axis=-1, keepdims=True)
    )


def body(
    vit_in,
    conv_in,
    ln_one,
    w_qkv,
    w_attn,
    ln_two,
    w_up,
    w_down,
    conv_kernel,
    conv_gain,
    conv_up,
    conv_down,
    layer_scale,
    w_proj,
    adapter_kernel,
    gate_in,
    gate_out,
    d_merged,
    d_conv_out,
):
    chans = lax.axis_size("chan")
    patchs = lax.axis_size("patch")
    me = lax.axis_index("chan")
    ids = jnp.stack([me, lax.axis_index("patch")]).astype(jnp.int32)
    tokens, images, width = vit_in.shape
    band = tokens // chans
    own_channels, _, cells = conv_in.shape
    channels = own_channels * chans
    lanes = images * cells
    hidden = w_up.shape[1]
    own_width = w_attn.shape[1]

    def own_rows(values, size):
        return lax.dynamic_slice_in_dim(values, me * size, size, 0)

    def own_band(values):
        return lax.dynamic_slice_in_dim(values, me * band, band, 0).swapaxes(0, 1)

    places = [(p * chans + c, c * patchs + p) for p in range(patchs) for c in range(chans)]

    def placed(values):
        return lax.ppermute(values, ("patch", "chan"), places)

    everywhere = patchs * chans
    rows = own_channels // patchs

    def share(shares, kind, unit):
        flat = [v.astype(kind).reshape(chans, patchs, -1) for v in shares]
        flat = jnp.concatenate(flat, axis=2)
        flat = jnp.pad(flat, ((0, 0), (0, 0), (0, -flat.shape[2] % (rows * unit))))
        flat = flat.reshape(chans, patchs, rows, -1)
        return halving_order(flat, "chan")

    def unshare(values, shares):
        flat = values.reshape(-1)
        out = []
        for v in shares:
            size = v.size // everywhere
            out.append(flat[:size].reshape((v.shape[0] // everywhere,) + v.shape[1:]).astype(f32))
            flat = flat[size:]
        return out

    def summed(pair):
        return pair[0].astype(f32) + pair[1].astype(f32)

    top = 1 << (bit_count(chans) - 1)

    conv_flat = conv_in.reshape(own_channels, lanes)
    weights = tap_weights(own_rows(conv_kernel, own_channels))
    mapped = depthwise(conv_flat, weights)

    gain_one = ln_one.astype(f32)[None]
    gain_two = ln_two.astype(f32)[None]
    w_three = w_qkv.swapaxes(0, 1)

    def attend():
        normed, qkv, mixed, logs, keep, send = attention_forward(
            vit_in.swapaxes(0, 1), gain_one, w_three, w_attn, chans, ids
        )
        pair = fold(keep, swap(send, "chan", 1), "chan", 0)
        return (normed, qkv, mixed, logs), pair, plain(conv_up.T), plain(d_merged.swapaxes(0, 1))

    ((normed_one, qkv, mixed, logs), (keep, send), conv_up_t, d_rows), (far, near) = beside(
        attend, [(mapped, "chan", top), (mapped, "chan", 1)]
    )
    mapped_parts = parts_beside(mapped, near, far)

    gain_all = conv_gain.astype(f32)[:, None]
    vit_band = own_band(vit_in).astype(f32)

    def conv():
        got = swap(send, "chan", 2)
        *half, kept = conv_forward(mapped_parts, conv_up_t, conv_down, gain_all, ids, (), (keep,))
        total = finish(kept, got, "chan", 1)
        normed = (standardize(vit_band + summed(total), vit_eps)[0] * gain_two).astype(bf16)
        exchanged = swap(normed, "chan", top), swap(normed, "chan", 1)
        whole = conv_forward(
            mapped_parts, conv_up_t, conv_down, gain_all, ids, (normed,), part=1, into=half
        )
        return whole, total, normed, exchanged

    (conv_norm, conv_act, conv_slope, stats, conv_keep, conv_send), attended, normed_band, (far, near) = beside(
        conv, []
    )[0]
    middle = vit_band + summed(attended)
    unit_two, inverse_two = standardize(middle, vit_eps)
    normed_parts = parts_beside(normed_band, near, far)
    conv_keep, conv_send = fold(conv_keep, swap(conv_send, "chan", 1), "chan", 0)

    def forward():
        out_keep, out_send, keep, send, *grads = feed_forward(
            normed_parts, d_rows, w_up, w_down, patchs, ids
        )
        out = fold(out_keep, swap(out_send, "chan", 1), "chan", 0)
        return out, fold(keep, swap(send, "chan", 1), "chan", 0), grads

    ((out_keep, out_send), (keep, send), grads), (got,) = beside(
        forward, [(conv_send, "chan", 2)]
    )

    own_scale = own_rows(layer_scale, own_channels).astype(f32)[:, None]
    conv_sum = finish(conv_keep, got, "chan", 1)
    vit = list(zip(grads[::2], grads[1::2]))
    (branch_maps, conv_result, pooled, *pieces), (got, vit_0) = beside(
        lambda: pool_forward(*conv_sum, conv_flat, own_scale, images, band, chans, ids),
        [(send, "chan", 2), (vit[0][1], "patch", 1)],
    )

    d_band = own_band(d_merged)
    d_two = finish(keep, got, "chan", 1)

    d_normed_two = summed(d_two)
    d_middle = d_band.astype(f32) + norm_back(d_normed_two, gain_two, unit_two, inverse_two)
    d_attended = d_middle.astype(bf16)
    g_ln_two = jnp.sum(d_normed_two * unit_two, axis=(0, 1))
    (w_own, conv_down_t, d_out), (vit_1, *got) = beside(
        lambda: (
            own_rows(w_proj, own_channels),
            plain(conv_down.T),
            plain(d_conv_out.reshape(own_channels, lanes)),
        ),
        [(vit[1][1], "patch", 1)] + [(pieces[offset], "chan", offset) for offset in range(1, chans)],
    )
    pieces[1:] = got

    kernel_three = jnp.pad(adapter_kernel.astype(f32).T, ((0, 7), (0, 0)))
    ((gated, d_smooth, g_gate_in, g_gate_out, g_adapter), vit_a, vit_b), (d_far, d_near, vit_2) = beside(
        lambda: (
            adapter(pieces, w_proj, kernel_three, gate_in, gate_out, d_band, ids),
            fold(vit[0][0], vit_0, "patch", 0),
            fold(vit[1][0], vit_1, "patch", 0),
        ),
        [(d_attended, "chan", top), (d_attended, "chan", 1), (vit[2][1], "patch", 1)],
    )
    d_parts = parts_beside(d_attended, d_near, d_far)
    vit_keep, vit_send = (jnp.concatenate(v, axis=2) for v in zip(vit_a, vit_b))
    shares = [g_gate_in, g_gate_out, g_adapter[:9].T, g_ln_two]
    ((shared_keep, shared_send), vit_a), (far, near, vit_3, vit_got) = beside(
        lambda: (halves(share(shares, bf16, 128), "chan"), fold(vit[2][0], vit_2, "patch", 0)),
        [(d_smooth, "chan", top), (d_smooth, "chan", 1), (vit[3][1], "patch", 1), (vit_send, "patch", 2)],
    )
    smooth_parts = parts_beside(d_smooth, near, far)
    vit_keep, vit_send = fold(vit_keep, vit_got, "patch", 1)
    shared_keep, shared_send = halves_at(shared_keep + swap(shared_send, "chan", 1), "chan", 1)

    ((d_result, d_branch, g_proj, g_scale), vit_b), (shared_got, vit_got) = beside(
        lambda: (
            adapter_back(
                smooth_parts, w_own, kernel_three, pooled, d_out, branch_maps, own_scale, ids
            ),
            fold(vit[3][0], vit_3, "patch", 0),
        ),
        [(shared_send, "chan", 2), (vit_send, "patch", 4)],
    )
    up_sum = finish(vit_keep, vit_got, "patch", 2)
    vit_keep, vit_send = (jnp.concatenate(v, axis=2) for v in zip(vit_a, vit_b))
    shared = sum_scatter(shared_keep + shared_got, "chan", 2).reshape(own_channels, -1)
    early = jnp.concatenate([g_proj, shared], axis=1).reshape(patchs, rows, -1)
    early_keep, early_send = halves(halving_order(early, "patch"), "patch")

    (one_keep, one_send, att_keep, att_send), (far, near, early_got, vit_got) = beside(
        lambda: attention_backward(
            d_parts, normed_one, qkv, mixed, logs, w_three, w_attn, patchs, ids
        ),
        [
            (d_branch, "chan", top),
            (d_branch, "chan", 1),
            (early_send, "patch", 1),
            (vit_send, "patch", 2),
        ],
    )
    branch_parts = parts_beside(d_branch, near, far)
    vit_keep, vit_send = fold(vit_keep, vit_got, "patch", 1)
    early_keep, early_send = fold(early_keep, early_got, "patch", 0)

    (d_all, *down), (got, one_got, att_got, vit_got, early_got) = beside(
        lambda: down_gradient(branch_parts, conv_act, patchs, ids),
        [
            (out_send, "chan", 2),
            (one_send, "chan", 1),
            (att_send, "patch", 1),
            (vit_send, "patch", 4),
            (early_send, "patch", 2),
        ],
    )
    down_sum = finish(vit_keep, vit_got, "patch", 2)
    out_sum = finish(out_keep, got, "chan", 1)
    att_keep, att_send = fold(att_keep, att_got, "patch", 0)
    early_keep, early_send = fold(early_keep, early_got, "patch", 1)
    one_keep, one_send = fold(one_keep, one_got, "chan", 0)

    (d_pre, conv_keep, conv_send, sums), (first_got, one_got, early_got, att_got) = beside(
        lambda: conv_backward(d_all, conv_down_t, conv_up, conv_slope, conv_norm, gain_all, ids),
        [
            (down[1], "patch", 1),
            (one_send, "chan", 2),
            (early_send, "patch", 4),
            (att_send, "patch", 2),
        ],
    )
    first_keep, first_send = fold(down[0], first_got, "patch", 0)
    att_keep, att_send = fold(att_keep, att_got, "patch", 1)

    def dealt():
        pair = fold(conv_keep, swap(conv_send, "chan", 1), "chan", 0)
        early = summed(finish(early_keep, early_got, "patch", 2)).astype(bf16)
        return pair, sums + swap(sums, "chan", 1), early, weight_gradient(conv_norm, d_pre, patchs, ids)

    ((conv_keep, conv_send), sums, early, up), (second_got, first_got, att_got) = beside(
        dealt, [(down[3], "patch", 1), (first_send, "patch", 2), (att_send, "patch", 4)]
    )
    att_sum = finish(att_keep, att_got, "patch", 2)
    first_keep, first_send = fold(first_keep, first_got, "patch", 1)
    second_keep, second_send = fold(down[2], second_got, "patch", 0)

    def back_one():
        d_normed_one = summed(finish(one_keep, one_got, "chan", 1))
        unit_one, inverse_one = standardize(vit_band, vit_eps)
        g_vit = d_middle + norm_back(d_normed_one, gain_one, unit_one, inverse_one)
        return (
            g_vit.astype(bf16),
            halves(share([jnp.sum(d_normed_one * unit_one, axis=(0, 1))], f32, 1), "chan"),
            summed(att_sum),
            conv_result.reshape(conv_in.shape),
            (middle + summed(out_sum) + gated).astype(bf16).swapaxes(0, 1),
        )

    (g_vit, (one_keep, one_send), att_grads, conv_out, merged), (
        conv_got, third_got, sums_got, first_got, second_got
    ) = beside(
        back_one,
        [
            (conv_send, "chan", 2),
            (up[1], "patch", 1),
            (sums, "chan", 2),
            (first_send, "patch", 4),
            (second_send, "patch", 2),
        ],
    )
    sums = sum_all(sums + sums_got, "chan", 2) * (1.0 / channels)
    first_sum = finish(first_keep, first_got, "patch", 2)
    second_keep, second_send = fold(second_keep, second_got, "patch", 1)
    third_keep, third_send = fold(up[0], third_got, "patch", 0)

    own_gain = own_rows(conv_gain, own_channels).astype(f32)[:, None]
    conv_sum = finish(conv_keep, conv_got, "chan", 1)
    (g_conv_in, g_kernel, g_gain), (fourth_got, second_got, third_got, vit_far, vit_near, one_got) = beside(
        lambda: depthwise_back(
            *conv_sum, mapped, stats, sums, own_gain, conv_flat, weights, d_result, images
        ),
        [
            (up[3], "patch", 1),
            (second_send, "patch", 4),
            (third_send, "patch", 2),
            (g_vit, "chan", top),
            (g_vit, "chan", 1),
            (one_send, "chan", 1),
        ],
    )
    second_sum = finish(second_keep, second_got, "patch", 2)
    third_keep, third_send = fold(third_keep, third_got, "patch", 1)
    fourth_keep, fourth_send = fold(up[2], fourth_got, "patch", 0)

    def late_sum():
        shared_one = sum_scatter(one_keep + one_got, "chan", 1).reshape(own_channels, -1)
        late = jnp.concatenate([g_kernel, g_gain[:, None], g_scale[:, :1], shared_one], axis=1)
        late = jnp.pad(late, ((0, 0), (0, -late.shape[1] % 128)))
        late = halving_order(late.reshape(patchs, rows, -1), "patch")
        total = sum_scatter(late, "patch")
        whole_rows = jnp.zeros((tokens, images, width), f32)
        for offset, part in enumerate(parts_beside(g_vit, vit_near, vit_far)):
            whole_rows = lax.dynamic_update_slice_in_dim(
                whole_rows, part.swapaxes(0, 1).astype(f32), (me ^ offset) * band, 0
            )
        return total, plain(whole_rows)

    (late, g_vit_in), (fourth_got, third_got) = beside(
        late_sum, [(fourth_send, "patch", 2), (third_send, "patch", 4)]
    )
    fourth_keep, fourth_send = fold(fourth_keep, fourth_got, "patch", 1)
    third_sum = finish(third_keep, third_got, "patch", 2)

    def last():
        return [summed(v) for v in (up_sum, down_sum, first_sum, second_sum, third_sum)]

    (g_up, g_down, first, second, third), (fourth_got, own_late, own_early) = beside(
        last,
        [(fourth_send, "patch", 4), (late, ("patch", "chan"), places), (early, ("patch", "chan"), places)],
    )
    g_conv_down = jnp.concatenate([first, second], axis=1)
    g_proj = own_early[:, :width].astype(f32)
    g_gate_in, g_gate_out, g_adapter, g_ln_two = unshare(own_early[:, width:], shares)
    fourth_sum = finish(fourth_keep, fourth_got, "patch", 2)
    g_conv_up = jnp.concatenate([third, summed(fourth_sum)], axis=1)
    (g_ln_one,) = unshare(own_late[:, 51:52], [ln_one])
    qkv_width = 3 * own_width
    return (
        merged,
        conv_out,
        g_vit_in,
        g_conv_in,
        g_ln_one,
        att_grads[:, :qkv_width].reshape(-1, 3, own_width),
        att_grads[:, qkv_width:],
        g_ln_two,
        g_up,
        g_down,
        own_late[:, :49],
        own_late[:, 49],
        g_conv_up,
        g_conv_down,
        own_late[:, 50],
        g_proj,
        g_adapter,
        g_gate_in,
        g_gate_out,
    )


def solution(mesh):
    in_specs = (
        P(None, "patch", None),
        P("chan", "patch", None),
        P(),
        P(None, None, "chan"),
        P(None, "chan"),
        P(),
        P(None, "chan"),
        P(None, "chan"),
        P(),
        P(),
        P(None, "chan"),
        P(None, "chan"),
        P(),
        P(),
        P(),
        P(),
        P(),
        P(None, "patch", None),
        P("chan", "patch", None),
    )
    out_specs = (
        P("chan", "patch", None),
        P("chan", "patch", None),
        P(None, "patch", None),
        P("chan", "patch", None),
        P(("patch", "chan")),
        P("patch", None, "chan"),
        P("patch", "chan"),
        P(("patch", "chan")),
        P("patch", "chan"),
        P("patch", "chan"),
        P(("patch", "chan"), None),
        P(("patch", "chan")),
        P("patch", "chan"),
        P("patch", "chan"),
        P(("patch", "chan")),
        P(("patch", "chan"), None),
        P(("patch", "chan"), None),
        P(("patch", "chan"), None),
        P(("patch", "chan"), None),
    )
    return jax.shard_map(body, mesh=mesh, in_specs=in_specs, out_specs=out_specs, check_vma=False)
```

```python
import math

import jax
import jax.numpy as jnp
import numpy as np
from jax import lax
from jax.experimental import pallas as pl
from jax.experimental.layout import Layout, with_layout_constraint
from jax.experimental.pallas import tpu as pltpu
from jax.sharding import PartitionSpec as P

HEAD_DIM = 64
GRID = 24
MAP = 32
TAPS = 7
GROUP = 32
WIDE = 256

vit_eps = 1e-05
conv_eps = 1e-06
f32 = jnp.float32
bf16 = jnp.bfloat16
MIB = 2**20


def block_of(size, most, unit):
    best = unit
    for candidate in range(unit, most + 1, unit):
        if size % candidate == 0:
            best = candidate
    return best if size % best == 0 else size


def bit_count(size):
    return size.bit_length() - 1


def reverse_bits(value, bits):
    return sum(((value >> k) & 1) << (bits - 1 - k) for k in range(bits))


def swap(values, axis, other):
    count = lax.axis_size(axis)
    return lax.ppermute(values, axis, [(i, i ^ other) for i in range(count)])


def move(values, axis, other):
    return swap(values, axis, other) if isinstance(other, int) else lax.ppermute(values, axis, other)


def beside(work, sends):
    def run():
        return work(), [move(*send) for send in sends]

    def skip():
        return jax.tree.map(lambda v: jnp.zeros(v.shape, v.dtype), jax.eval_shape(run))

    return lax.optimization_barrier(lax.cond(lax.axis_index("chan") < lax.axis_size("chan"), run, skip))


def fold(keep, got, axis, bit, parts=1):
    shape = keep.shape
    half = shape[0] // 2
    flat = [v.reshape(shape[0], -1, shape[-1]) for v in (keep, got)]
    rows, columns = flat[0].shape[1:]
    step = block_of(rows, max(16, MIB // (2 * columns)), 8)
    mine = ((lax.axis_index(axis) >> (bit + 1)) & 1).astype(jnp.int32)[None]

    def kernel(_, kept, came, kept_far, came_far, keep_ref, *send_refs):
        keep_ref[...] = (kept[...].astype(f32) + came[...].astype(f32)).astype(keep_ref.dtype)
        total = (kept_far[...].astype(f32) + came_far[...].astype(f32)).astype(keep_ref.dtype)
        for part, ref in enumerate(send_refs):
            ref[...] = total[..., part * (columns // parts) : (part + 1) * (columns // parts)]

    near = pl.BlockSpec((1, step, columns), lambda i, r, own: (own[0] * half + i, r, 0))
    far = pl.BlockSpec((1, step, columns), lambda i, r, own: ((1 - own[0]) * half + i, r, 0))
    place = lambda width: pl.BlockSpec((1, step, width), lambda i, r, own: (i, r, 0))
    shape_of_part = lambda width: jax.ShapeDtypeStruct((half, rows, width), keep.dtype)
    out = pl.pallas_call(
        kernel,
        grid_spec=pltpu.PrefetchScalarGridSpec(
            num_scalar_prefetch=1,
            grid=(half, rows // step),
            in_specs=[near, near, far, far],
            out_specs=[place(columns)] + [place(columns // parts)] * parts,
        ),
        out_shape=[shape_of_part(columns)] + [shape_of_part(columns // parts)] * parts,
        compiler_params=pltpu.CompilerParams(vmem_limit_bytes=32 * MIB),
        cost_estimate=pl.CostEstimate(flops=int(2e9), bytes_accessed=6 * keep.size, transcendentals=0),
    )(mine, *flat, *flat)
    out = [v.reshape((half,) + shape[1:-1] + v.shape[-1:]) for v in out]
    return (out[0], out[1]) if parts == 1 else (out[0], out[1:])


def finish(keep, got, axis, bit):
    while bit + 1 < bit_count(lax.axis_size(axis)):
        keep, send = fold(keep, got, axis, bit)
        bit += 1
        got = swap(send, axis, 1 << bit)
    return keep[0], got[0]


def plain(values):
    return with_layout_constraint(values, Layout(tuple(range(values.ndim))))


def halves(blocks, axis):
    return halves_at(blocks, axis, 0)


def halves_at(blocks, axis, bit):
    mine = (lax.axis_index(axis) >> bit) & 1
    half = blocks.shape[0] // 2
    return tuple(lax.dynamic_slice_in_dim(blocks, which * half, half, 0) for which in (mine, 1 - mine))


def sum_scatter(values, axis, first=0):
    for bit in range(first, bit_count(lax.axis_size(axis))):
        mine = (lax.axis_index(axis) >> bit) & 1
        half = values.shape[0] // 2
        keep = lax.dynamic_slice_in_dim(values, mine * half, half, 0)
        send = lax.dynamic_slice_in_dim(values, (1 - mine) * half, half, 0)
        values = keep + swap(send, axis, 1 << bit)
    return values[0]


def halving_order(values, axis):
    count = lax.axis_size(axis)
    bits = bit_count(count)
    return jnp.stack([values[reverse_bits(j, bits)] for j in range(count)])


def parts_beside(block, near, far):
    top = bit_count(lax.axis_size("chan")) - 1
    parts = {0: block, 1 << top: far}
    for bit in reversed(range(1, top)):
        for offset in list(parts):
            parts[offset | (1 << bit)] = swap(parts[offset], "chan", 1 << bit)
    parts[1] = near
    for offset in list(parts):
        if offset > 1:
            parts[offset | 1] = swap(parts[offset], "chan", 1)
    return [parts[offset] for offset in sorted(parts)]


def sum_all(values, axis, first=0):
    for bit in range(first, bit_count(lax.axis_size(axis))):
        values = values + swap(values, axis, 1 << bit)
    return values


def lane_shift(values, step):
    count = values.shape[-1]
    step = step % count
    return values if step == 0 else pltpu.roll(values, count - step, 1)


def fill_masks(col_ref, row_ref):
    lanes = col_ref.shape[-1]
    place = lax.broadcasted_iota(jnp.int32, (GROUP, lanes), 1)
    col = place % MAP
    row = (place // MAP) % MAP
    for tap in range(TAPS):
        step = tap - TAPS // 2
        for ref, spot in ((col_ref, col), (row_ref, row)):
            ref[tap] = ((spot + step >= 0) & (spot + step < MAP)).astype(f32).astype(bf16)


def tap_weights(kernel):
    tap = np.arange(TAPS * TAPS)[:, None]
    spot = np.arange(TAPS * WIDE)[None, :]
    pick = (tap == (spot // WIDE) * TAPS + (spot % WIDE) // GROUP) & (spot % WIDE < TAPS * GROUP)
    own = (jnp.arange(kernel.shape[0])[:, None] % GROUP) == jnp.asarray(spot % GROUP)
    spread = jnp.dot(kernel, jnp.asarray(pick.astype(bf16)), preferred_element_type=f32)
    return jnp.where(own, spread, 0.0).astype(bf16)


def stacked_weights(k_ref):
    blocks = [k_ref[:, r * WIDE : r * WIDE + TAPS * GROUP] for r in range(TAPS)]
    return jnp.concatenate(blocks, axis=0)


def depthwise_kernel(x_ref, k_ref, o_ref, s_ref, col_ref, row_ref):
    @pl.when(pl.program_id(0) == 0)
    def _():
        fill_masks(col_ref, row_ref)

    x = x_ref[...]
    lanes = x.shape[1]
    for tap in range(TAPS):
        step = tap - TAPS // 2
        moved = lane_shift(x, step)
        s_ref[tap] = moved if step == 0 else moved * col_ref[tap]
    rows = jnp.dot(
        stacked_weights(k_ref), s_ref[...].reshape(TAPS * GROUP, lanes), preferred_element_type=f32
    )
    total = None
    for tap in range(TAPS):
        step = tap - TAPS // 2
        part = rows[tap * GROUP : (tap + 1) * GROUP]
        if step != 0:
            part = (lane_shift(part.astype(bf16), MAP * step) * row_ref[tap]).astype(f32)
        total = part if total is None else total + part
    o_ref[...] = total.astype(o_ref.dtype)


def depthwise(x, weights):
    channels, lanes = x.shape
    return pl.pallas_call(
        depthwise_kernel,
        grid=(channels // GROUP,),
        in_specs=[
            pl.BlockSpec((GROUP, lanes), lambda i: (i, 0)),
            pl.BlockSpec((GROUP, TAPS * WIDE), lambda i: (i, 0)),
        ],
        out_specs=pl.BlockSpec((GROUP, lanes), lambda i: (i, 0)),
        out_shape=jax.ShapeDtypeStruct((channels, lanes), bf16),
        scratch_shapes=[pltpu.VMEM((TAPS, GROUP, lanes), bf16)] * 3,
        compiler_params=pltpu.CompilerParams(vmem_limit_bytes=32 * MIB),
        cost_estimate=pl.CostEstimate(
            flops=int(8 * 1.1e9), bytes_accessed=4 * channels * lanes, transcendentals=0
        ),
    )(x, weights)


def depthwise_back_kernel(
    keep_ref, got_ref, m_ref, stat_ref, sum_ref, gain_ref, x_ref, k_ref, add_ref,
    gx_ref, gk_ref, gg_ref, t_ref, s_ref, col_ref, row_ref,
):
    @pl.when(pl.program_id(0) == 0)
    def _():
        fill_masks(col_ref, row_ref)

    x = x_ref[...]
    lanes = x.shape[1]
    inverse = stat_ref[1:2]
    unit = (m_ref[...].astype(f32) - stat_ref[0:1]) * inverse
    grad = keep_ref[...].astype(f32) + got_ref[...].astype(f32)
    gg_ref[...] = jnp.broadcast_to(jnp.sum(grad * unit, axis=1, keepdims=True), gg_ref.shape)
    d = (inverse * (grad * gain_ref[...] - sum_ref[0:1] - unit * sum_ref[1:2])).astype(bf16)
    last = TAPS - 1
    for tap in range(TAPS):
        step = tap - TAPS // 2
        moved = lane_shift(d, -step)
        t_ref[tap] = moved if step == 0 else moved * col_ref[last - tap]
        moved = lane_shift(x, MAP * step)
        s_ref[tap] = moved if step == 0 else moved * row_ref[tap]
    t = t_ref[...].reshape(TAPS * GROUP, lanes)
    rows = jnp.dot(stacked_weights(k_ref), t, preferred_element_type=f32)
    total = add_ref[...]
    for tap in range(TAPS):
        step = tap - TAPS // 2
        part = rows[tap * GROUP : (tap + 1) * GROUP]
        if step != 0:
            part = (lane_shift(part.astype(bf16), -MAP * step) * row_ref[last - tap]).astype(f32)
        total = total + part
    cells = gx_ref.shape[2]
    for i in range(gx_ref.shape[1]):
        gx_ref[:, i, :] = total[:, i * cells : (i + 1) * cells]
    pairs = lax.dot_general(
        t, s_ref[...].reshape(TAPS * GROUP, lanes), (((1,), (1,)), ((), ())), preferred_element_type=f32
    )
    side = TAPS * GROUP
    first = lax.broadcasted_iota(jnp.int32, (side, side), 0)
    second = lax.broadcasted_iota(jnp.int32, (side, side), 1)
    own = jnp.where(first % GROUP == second % GROUP, pairs, 0.0)
    source = lax.broadcasted_iota(jnp.int32, (side, 128), 0)
    target = lax.broadcasted_iota(jnp.int32, (side, 128), 1)
    pick = (source // GROUP == target).astype(f32).astype(bf16)
    high = own.astype(bf16)
    low = (own - high.astype(f32)).astype(bf16)
    gk_ref[0] = jnp.dot(high, pick, preferred_element_type=f32) + jnp.dot(
        low, pick, preferred_element_type=f32
    )


def depthwise_back(keep, got, mapped, stats, sums, gain, x, weights, add, images):
    channels, lanes = x.shape
    groups = channels // GROUP
    rows = pl.BlockSpec((GROUP, lanes), lambda i: (i, 0))
    fixed = pl.BlockSpec((8, lanes), lambda i: (0, 0))
    gx, gk, gg = pl.pallas_call(
        depthwise_back_kernel,
        grid=(groups,),
        in_specs=[
            rows, rows, rows, fixed, fixed,
            pl.BlockSpec((GROUP, 1), lambda i: (i, 0)),
            rows,
            pl.BlockSpec((GROUP, TAPS * WIDE), lambda i: (i, 0)),
            rows,
        ],
        out_specs=[
            pl.BlockSpec((GROUP, images, lanes // images), lambda i: (i, 0, 0)),
            pl.BlockSpec((1, TAPS * GROUP, 128), lambda i: (i, 0, 0)),
            pl.BlockSpec((GROUP, 128), lambda i: (i, 0)),
        ],
        out_shape=[
            jax.ShapeDtypeStruct((channels, images, lanes // images), f32),
            jax.ShapeDtypeStruct((groups, TAPS * GROUP, 128), f32),
            jax.ShapeDtypeStruct((channels, 128), f32),
        ],
        scratch_shapes=[pltpu.VMEM((TAPS, GROUP, lanes), bf16)] * 4,
        compiler_params=pltpu.CompilerParams(vmem_limit_bytes=56 * MIB),
        cost_estimate=pl.CostEstimate(
            flops=int(16 * 1.1e9), bytes_accessed=14 * channels * lanes, transcendentals=0
        ),
    )(keep, got, mapped, stats, sums, gain, x, weights, add)
    gk = gk[:, :, :TAPS].reshape(groups, TAPS, GROUP, TAPS).transpose(0, 2, 3, 1)
    return gx, gk.reshape(channels, TAPS * TAPS), gg[:, 0]


def gelu_both(u):
    share = 0.5 * (1.0 + lax.erf(u * (1.0 / math.sqrt(2.0))))
    return u * share, share + u * jnp.exp(-0.5 * u * u) * (1.0 / math.sqrt(2.0 * math.pi))


def pool_table():
    out_index = np.arange(GRID)
    first_row = out_index * MAP // GRID
    last_row = ((out_index + 1) * MAP + GRID - 1) // GRID
    source_index = np.arange(MAP)
    inside = (source_index[None, :] >= first_row[:, None]) & (
        source_index[None, :] < last_row[:, None]
    )
    single = inside.astype(np.float32) / (last_row - first_row)[:, None].astype(np.float32)
    table = single[:, None, :, None] * single[None, :, None, :]
    return table.reshape(GRID * GRID, MAP * MAP)


PACE = 1.1e9


def mm(a, b):
    return jnp.dot(a, b, preferred_element_type=f32)


def mm_nt(a, b):
    return lax.dot_general(a, b, (((1,), (1,)), ((), ())), preferred_element_type=f32)


def mm_tn(a, b):
    return lax.dot_general(a, b, (((0,), (0,)), ((), ())), preferred_element_type=f32)


def whole(shape):
    return pl.BlockSpec(shape, lambda *_: (0,) * len(shape), pipeline_mode=pl.Buffered(1))


def shape_of(shape, dtype=bf16):
    return jax.ShapeDtypeStruct(shape, dtype)


def call(kernel, ids, grid, args, in_specs, outs, out_specs, scratch=(), micros=10, vmem=56, earlier=(), through=(), into=()):
    count = len(earlier)
    passed = len(through)
    ins = len(args)
    results = len(outs)

    def run(ids_ref, *refs):
        refs = refs[count + passed + len(into) :]
        kernel(ids_ref, *refs[: ins + results], *refs[ins + results + passed :])

    bytes_accessed = sum(v.size * v.dtype.itemsize for v in list(args) + list(outs))
    return pl.pallas_call(
        run,
        grid_spec=pltpu.PrefetchScalarGridSpec(
            num_scalar_prefetch=1,
            grid=grid,
            in_specs=[pl.BlockSpec(memory_space=pl.ANY)] * (count + passed + len(into)) + in_specs,
            out_specs=out_specs + [pl.BlockSpec(memory_space=pl.ANY)] * passed,
            scratch_shapes=scratch,
        ),
        out_shape=outs + [jax.ShapeDtypeStruct(v.shape, v.dtype) for v in through],
        input_output_aliases={1 + count + i: results + i for i in range(passed)}
        | {1 + count + passed + i: i for i in range(len(into))},
        compiler_params=pltpu.CompilerParams(vmem_limit_bytes=vmem * MIB),
        cost_estimate=pl.CostEstimate(flops=int(micros * PACE), bytes_accessed=int(bytes_accessed), transcendentals=0),
    )(ids, *earlier, *through, *into, *args)


def deal(stack_ref, keep_ref, send_ref, mine, lead=()):
    half = stack_ref.shape[0] // 2
    for j in range(half):
        block = 2 * reverse_bits(j, bit_count(half))
        keep_ref[(j,) + lead] = stack_ref[block + mine]
        send_ref[(j,) + lead] = stack_ref[block + 1 - mine]


def dealt_rows(w_ref, own, refs, operand, mine):
    half = refs[0].shape[0]
    for ref, bit in zip(refs, (mine, 1 - mine)):
        for j in range(half):
            block = 2 * reverse_bits(j, bit_count(half)) + bit
            rows = w_ref[pl.ds(pl.multiple_of(block * own, 16), own), :]
            ref[j] = mm(rows, operand[...]).astype(bf16)


def conv_forward(parts, up_t, down, gain, ids, earlier=(), through=(), part=0, into=()):
    count = len(parts)
    own, lanes = parts[0].shape
    channels = own * count
    hidden = up_t.shape[0]
    bn = block_of(lanes // 2, 512, 128)
    first = part * (lanes // 2 // bn)
    step = block_of(hidden, 256, 128)

    def kernel(ids_ref, *refs):
        part_refs = refs[:count]
        up_ref, down_ref, gain_ref, cn_ref, h_ref, s_ref, stat_ref, keep_ref, send_ref = refs[count:]
        me = ids_ref[0]
        mean = sum(jnp.sum(part[...].astype(f32), axis=0, keepdims=True) for part in part_refs) * (1.0 / channels)
        square = sum(
            jnp.sum((part[...].astype(f32) - mean) ** 2, axis=0, keepdims=True) for part in part_refs
        ) * (1.0 / channels)
        inverse = lax.rsqrt(square + conv_eps)
        stat_ref[...] = jnp.concatenate([mean, inverse, jnp.zeros((6, bn), f32)], axis=0)
        for offset, part in enumerate(part_refs):
            rows = pl.ds(pl.multiple_of((me ^ offset) * own, 16), own)
            cn_ref[rows, :] = ((part[...].astype(f32) - mean) * inverse * gain_ref[rows, :]).astype(bf16)
        for f in range(0, hidden, step):
            act, slope = gelu_both(mm(up_ref[f : f + step], cn_ref[...]))
            h_ref[f : f + step] = act.astype(bf16)
            s_ref[f : f + step] = slope.astype(bf16)
        dealt_rows(down_ref, own, (keep_ref, send_ref), h_ref, me & 1)

    tall = lambda rows: pl.BlockSpec((rows, bn), lambda j, _: (0, j + first))
    half = pl.BlockSpec((count // 2, own, bn), lambda j, _: (0, 0, j + first))
    return call(
        kernel,
        ids,
        (lanes // 2 // bn,),
        (*parts, up_t, down, gain),
        [tall(own)] * count + [whole(up_t.shape), whole(down.shape), whole(gain.shape)],
        [
            shape_of((channels, lanes)),
            shape_of((hidden, lanes)),
            shape_of((hidden, lanes)),
            shape_of((8, lanes), f32),
            shape_of((count // 2, own, lanes)),
            shape_of((count // 2, own, lanes)),
        ],
        [tall(channels), tall(hidden), tall(hidden), tall(8), half, half],
        micros=36,
        earlier=earlier,
        through=through,
        into=into,
    )


def conv_backward(d_all, down_t, up, slope, normed, gain, ids, earlier=(), through=()):
    channels, lanes = d_all.shape
    hidden = down_t.shape[0]
    count = lax.axis_size("chan")
    own = channels // count
    bn = block_of(lanes, 512, 128)
    step = block_of(hidden, 512, 128)

    def kernel(ids_ref, d_ref, down_ref, up_ref, s_ref, n_ref, gain_ref, du_ref, keep_ref, send_ref, sum_ref):
        for f in range(0, hidden, step):
            du = mm(down_ref[f : f + step], d_ref[...]) * s_ref[f : f + step].astype(f32)
            du_ref[f : f + step] = du.astype(bf16)
        mine = ids_ref[0] & 1
        first = second = jnp.zeros((1, bn), f32)
        for ref, bit in ((keep_ref, mine), (send_ref, 1 - mine)):
            for j in range(count // 2):
                block = 2 * reverse_bits(j, bit_count(count // 2)) + bit
                rows = pl.ds(pl.multiple_of(block * own, 16), own)
                part = mm(up_ref[rows, :], du_ref[...])
                ref[j] = part.astype(bf16)
                first += jnp.sum(part * gain_ref[rows, :], axis=0, keepdims=True)
                second += jnp.sum(part * n_ref[rows, :].astype(f32), axis=0, keepdims=True)
        sum_ref[...] = jnp.concatenate([first, second, jnp.zeros((6, bn), f32)], axis=0)

    tall = lambda rows: pl.BlockSpec((rows, bn), lambda j, _: (0, j))
    half = pl.BlockSpec((count // 2, own, bn), lambda j, _: (0, 0, j))
    return call(
        kernel,
        ids,
        (lanes // bn,),
        (d_all, down_t, up, slope, normed, gain),
        [tall(channels), whole(down_t.shape), whole(up.shape), tall(hidden), tall(channels), whole(gain.shape)],
        [
            shape_of((hidden, lanes)),
            shape_of((count // 2, own, lanes)),
            shape_of((count // 2, own, lanes)),
            shape_of((8, lanes), f32),
        ],
        [tall(hidden), half, half, tall(8)],
        micros=28,
        earlier=earlier,
        through=through,
    )


def dealt_halves(size, patchs, columns, bn):
    half = pl.BlockSpec((patchs // 2, size, bn), lambda j, _: (0, 0, 0))

    def deal_columns(product, stack_ref, refs, mine):
        stack_ref[...] = product.astype(bf16).reshape(patchs, size, bn)
        for part in range(2):

            @pl.when(pl.program_id(0) == part)
            def _(part=part):
                deal(stack_ref, refs[2 * part], refs[2 * part + 1], mine)

    return [half] * 4, [shape_of((patchs // 2, size, columns // 2))] * 4, deal_columns


def down_gradient(parts, act, patchs, ids):
    count = len(parts)
    own, lanes = parts[0].shape
    channels = own * count
    hidden = act.shape[0]
    bn = hidden // 2
    size = channels // patchs
    specs, shapes, deal_columns = dealt_halves(size, patchs, hidden, bn)

    def kernel(ids_ref, *refs):
        part_refs = refs[:count]
        b_ref, d_ref, *out_refs, o_ref = refs[count:]

        @pl.when(pl.program_id(0) == 0)
        def _():
            for offset, part in enumerate(part_refs):
                d_ref[pl.ds(pl.multiple_of((ids_ref[0] ^ offset) * own, 16), own), :] = part[...]

        deal_columns(mm_nt(d_ref[...], b_ref[...]), o_ref, out_refs, ids_ref[1] & 1)

    return call(
        kernel,
        ids,
        (2,),
        (*parts, act),
        [whole(parts[0].shape)] * count + [pl.BlockSpec((bn, lanes), lambda j, _: (j, 0))],
        [shape_of((channels, lanes))] + shapes,
        [whole((channels, lanes))] + specs,
        [pltpu.VMEM((patchs, size, bn), bf16)],
        micros=18,
    )


def weight_gradient(a, b, patchs, ids):
    rows, depth = a.shape
    columns = b.shape[0]
    bn = columns // 2
    size = rows // patchs
    specs, shapes, deal_columns = dealt_halves(size, patchs, columns, bn)

    def kernel(ids_ref, a_ref, b_ref, *refs):
        deal_columns(mm_nt(a_ref[...], b_ref[...]), refs[-1], refs[:-1], ids_ref[1] & 1)

    return call(
        kernel,
        ids,
        (2,),
        (a, b),
        [whole(a.shape), pl.BlockSpec((bn, depth), lambda j, _: (j, 0))],
        shapes,
        specs,
        [pltpu.VMEM((patchs, size, bn), bf16)],
        micros=18,
    )


def pool_forward(keep, got, conv_flat, scale, images, band, chans, ids, earlier=(), through=()):
    own, lanes = keep.shape
    cells = lanes // images
    table = pool_table()
    tokens = table.shape[0]
    reach = band + 2 * GRID
    padded = jnp.asarray(np.pad(table, ((GRID, GRID), (0, 0))))

    def kernel(ids_ref, keep_ref, got_ref, c_ref, scale_ref, t_ref, p_ref, branch_ref, result_ref, pooled_ref, *pieces):
        branch = keep_ref[...].astype(f32) + got_ref[...].astype(f32)
        branch_ref[...] = branch.astype(bf16)
        result = (c_ref[...].astype(f32) + scale_ref[...] * branch).astype(bf16)
        result_ref[...] = result
        pooled_ref[0] = mm(result, t_ref[...]).astype(bf16)
        for offset, piece in enumerate(pieces):
            start = pl.multiple_of((ids_ref[0] ^ offset) * band, 8)
            rows = p_ref[pl.ds(start, reach), :].astype(bf16)
            piece[0] = mm_nt(rows, result).astype(bf16)

    flat = pl.BlockSpec((own, cells), lambda i, _: (0, i))
    return call(
        kernel,
        ids,
        (images,),
        (keep, got, conv_flat, scale, jnp.asarray(table.T.astype(bf16)), padded),
        [flat, flat, flat, whole(scale.shape), whole((cells, tokens)), whole(padded.shape)],
        [shape_of((own, lanes))] * 2
        + [shape_of((images, own, tokens))]
        + [shape_of((images, reach, own))] * chans,
        [flat, flat, pl.BlockSpec((1, own, tokens), lambda i, _: (i, 0, 0))]
        + [pl.BlockSpec((1, reach, own), lambda i, _: (i, 0, 0))] * chans,
        micros=9,
        earlier=earlier,
        through=through,
    )


def row_moves(field, spots, step):
    if step == 0:
        return field
    count = field.shape[0]
    moved = pltpu.roll(field, (-step) % count, 0)
    column = spots % GRID + step
    return jnp.where((column >= 0) & (column < GRID), moved, 0.0)


def adapter(pieces, w_proj, kernel_three, gate_in, gate_out, d_band, ids, earlier=(), through=()):
    chans = len(pieces)
    images, reach, own = pieces[0].shape
    width = w_proj.shape[1]
    gate = gate_in.shape[1]
    band = reach - 2 * GRID

    def kernel(ids_ref, *refs):
        piece_refs = refs[:chans]
        proj_ref, k_ref, in_ref, out_ref, d_ref, gs_ref, ds_ref, gib_ref, gob_ref, gk_ref, gi_ref, go_ref = refs[chans:]
        me = ids_ref[0]

        @pl.when(pl.program_id(0) == 0)
        def _():
            gi_ref[...] = jnp.zeros_like(gi_ref)
            go_ref[...] = jnp.zeros_like(go_ref)
            gk_ref[...] = jnp.zeros_like(gk_ref)

        field = None
        for offset, piece in enumerate(piece_refs):
            start = pl.multiple_of((me ^ offset) * own, 16)
            term = mm(piece[0], proj_ref[pl.ds(start, own), :])
            field = term if field is None else field + term
        field = field.astype(bf16).astype(f32)
        spots = lax.broadcasted_iota(jnp.int32, (reach, 1), 0)
        moved = [row_moves(field, spots, step) for step in (-1, 0, 1)]
        smooth = None
        for t in range(9):
            term = k_ref[t : t + 1, :] * moved[t % 3][GRID * (t // 3) : GRID * (t // 3) + band]
            smooth = term if smooth is None else smooth + term
        rows = smooth.astype(bf16)
        act, slope = gelu_both(mm(rows, in_ref[...]))
        act = act.astype(bf16)
        value = jnp.tanh(mm(act, out_ref[...]))
        gs_ref[0] = value * smooth
        d = d_ref[0].astype(f32)
        d_logit = (d * smooth * (1.0 - value * value)).astype(bf16)
        d_gate = (mm_nt(d_logit, out_ref[...]) * slope).astype(bf16)
        d_smooth = d * value + mm_nt(d_gate, in_ref[...])
        ds_ref[0] = d_smooth.astype(bf16)
        go_ref[...] += mm_tn(act, d_logit)
        gi_ref[...] += mm_tn(rows, d_gate)
        for t in range(9):
            seen = moved[t % 3][GRID * (t // 3) : GRID * (t // 3) + band]
            gk_ref[t : t + 1, :] += jnp.sum(d_smooth * seen, axis=0, keepdims=True)

        @pl.when(pl.program_id(0) == images - 1)
        def _():
            gib_ref[...] = gi_ref[...].astype(bf16)
            gob_ref[...] = go_ref[...].astype(bf16)

    per = lambda rows, cols: pl.BlockSpec((1, rows, cols), lambda i, _: (i, 0, 0))
    kept = lambda *shape: pl.BlockSpec(shape, lambda i, _: (0, 0))
    return call(
        kernel,
        ids,
        (images,),
        (*pieces, w_proj, kernel_three, gate_in, gate_out, d_band),
        [per(reach, own)] * chans
        + [whole(w_proj.shape), whole(kernel_three.shape), whole(gate_in.shape), whole(gate_out.shape), per(band, width)],
        [
            shape_of((images, band, width), f32),
            shape_of((images, band, width)),
            shape_of((width, gate)),
            shape_of((gate, width)),
            shape_of((16, width), f32),
        ],
        [per(band, width), per(band, width), kept(width, gate), kept(gate, width), kept(16, width)],
        [pltpu.VMEM((width, gate), f32), pltpu.VMEM((gate, width), f32)],
        micros=13,
        earlier=earlier,
        through=through,
    )


def adapter_back(parts, w_own, kernel_three, pooled, d_out, branch, scale, ids, earlier=(), through=()):
    chans = len(parts)
    images, band, width = parts[0].shape
    own, lanes = d_out.shape
    cells = lanes // images
    tokens = band * chans
    table = jnp.asarray(pool_table().astype(bf16))

    def kernel(ids_ref, *refs):
        part_refs = refs[:chans]
        w_ref, k_ref, pooled_ref, do_ref, branch_ref, scale_ref, t_ref, dr_ref, db_ref, gpb_ref, gs_ref, f_ref, gp_ref = refs[chans:]
        me = ids_ref[0]

        @pl.when(pl.program_id(0) == 0)
        def _():
            gp_ref[...] = jnp.zeros_like(gp_ref)
            gs_ref[...] = jnp.zeros_like(gs_ref)
            f_ref[:GRID] = jnp.zeros((GRID, width), f32)
            f_ref[GRID + tokens :] = jnp.zeros((GRID, width), f32)

        for offset, part in enumerate(part_refs):
            start = pl.multiple_of((me ^ offset) * band + GRID, 8)
            f_ref[pl.ds(start, band), :] = part[0].astype(f32)
        field = f_ref[...]
        spots = lax.broadcasted_iota(jnp.int32, (tokens + 2 * GRID, 1), 0)
        moved = [row_moves(field, spots, -step) for step in (-1, 0, 1)]
        d_adapted = None
        for t in range(9):
            start = GRID * (2 - t // 3)
            term = k_ref[t : t + 1, :] * moved[t % 3][start : start + tokens]
            d_adapted = term if d_adapted is None else d_adapted + term
        d_adapted = d_adapted.astype(bf16)
        d_pooled = mm_nt(w_ref[...], d_adapted).astype(bf16)
        gp_ref[...] += mm(pooled_ref[0], d_adapted)
        d_result = do_ref[...].astype(f32) + mm(d_pooled, t_ref[...])
        dr_ref[...] = d_result
        db_ref[...] = (scale_ref[...] * d_result).astype(bf16)
        gs_ref[...] += jnp.sum(d_result * branch_ref[...].astype(f32), axis=1, keepdims=True)

        @pl.when(pl.program_id(0) == images - 1)
        def _():
            gpb_ref[...] = gp_ref[...].astype(bf16)

    flat = pl.BlockSpec((own, cells), lambda i, _: (0, i))
    per = lambda rows, cols: pl.BlockSpec((1, rows, cols), lambda i, _: (i, 0, 0))
    return call(
        kernel,
        ids,
        (images,),
        (*parts, w_own, kernel_three, pooled, d_out, branch, scale, table),
        [per(band, width)] * chans
        + [whole(w_own.shape), whole(kernel_three.shape), per(own, tokens), flat, flat, whole(scale.shape), whole(table.shape)],
        [
            shape_of((own, lanes), f32),
            shape_of((own, lanes)),
            shape_of((own, width)),
            shape_of((own, 128), f32),
        ],
        [flat, flat, pl.BlockSpec((own, width), lambda i, _: (0, 0)), pl.BlockSpec((own, 128), lambda i, _: (0, 0))],
        [pltpu.VMEM((tokens + 2 * GRID, width), f32), pltpu.VMEM((own, width), f32)],
        micros=14,
        earlier=earlier,
        through=through,
    )


def row_standard(values):
    center = values - jnp.mean(values, axis=-1, keepdims=True)
    inverse = lax.rsqrt(jnp.mean(center * center, axis=-1, keepdims=True) + vit_eps)
    return center * inverse


def stack_bands(stack_ref, values):
    count, band, _ = stack_ref.shape
    for b in range(count):
        stack_ref[b] = values[b * band : (b + 1) * band].astype(bf16)


def take_bands(rows_ref, part_refs, me):
    for offset, part in enumerate(part_refs):
        band = part.shape[1]
        start = pl.multiple_of((me ^ offset) * band, 8)
        rows_ref[pl.ds(start, band), :] = part[0].astype(f32)
    return rows_ref[...].astype(bf16)


def attention_forward(x, gain, w_qkv, w_attn, chans, ids, earlier=(), through=()):
    images, tokens, width = x.shape
    own = w_qkv.shape[2]
    heads = own // HEAD_DIM
    band = tokens // chans
    scale = 1.0 / math.sqrt(HEAD_DIM)

    def kernel(ids_ref, x_ref, gain_ref, qkv_w_ref, attn_ref, n_ref, qkv_ref, o_ref, log_ref, keep_ref, send_ref, stack_ref):
        normed = (row_standard(x_ref[0].astype(f32)) * gain_ref[...]).astype(bf16)
        n_ref[0] = normed
        q, k, v = (mm(normed, qkv_w_ref[t]).astype(bf16) for t in range(3))
        for t, part in enumerate((q, k, v)):
            qkv_ref[t, 0] = part
        mixed = []
        spot = lax.broadcasted_iota(jnp.int32, (tokens, 128), 1)
        logs = jnp.zeros((tokens, 128), f32)
        for h in range(heads):
            at = slice(h * HEAD_DIM, (h + 1) * HEAD_DIM)
            scores = mm_nt(q[:, at], k[:, at]) * scale
            most = jnp.max(scores, axis=-1, keepdims=True)
            powers = jnp.exp(scores - most)
            total = jnp.sum(powers, axis=-1, keepdims=True)
            logs = jnp.where(spot == h, most + jnp.log(total), logs)
            mixed.append(mm((powers * (1.0 / total)).astype(bf16), v[:, at]).astype(bf16))
        mixed = jnp.concatenate(mixed, axis=1)
        log_ref[0] = logs
        o_ref[0] = mixed
        stack_bands(stack_ref, mm_nt(mixed, attn_ref[...]))
        deal(stack_ref, keep_ref, send_ref, ids_ref[0] & 1, (0,))

    per = lambda cols: pl.BlockSpec((1, tokens, cols), lambda i, _: (i, 0, 0))
    half = pl.BlockSpec((chans // 2, 1, band, width), lambda i, _: (0, i, 0, 0))
    return call(
        kernel,
        ids,
        (images,),
        (x, gain, w_qkv, w_attn),
        [per(width), whole(gain.shape), whole(w_qkv.shape), whole(w_attn.shape)],
        [
            shape_of((images, tokens, width)),
            shape_of((3, images, tokens, own)),
            shape_of((images, tokens, own)),
            shape_of((images, tokens, 128), f32),
            shape_of((chans // 2, images, band, width)),
            shape_of((chans // 2, images, band, width)),
        ],
        [per(width), pl.BlockSpec((3, 1, tokens, own), lambda i, _: (0, i, 0, 0)), per(own), per(128), half, half],
        [pltpu.VMEM((chans, band, width), bf16)],
        micros=16,
        earlier=earlier,
        through=through,
    )


def feed_forward(parts, d_rows, w_up, w_down, patchs, ids, earlier=(), through=()):
    chans = len(parts)
    images, band, width = parts[0].shape
    tokens = band * chans
    hidden = w_up.shape[1]

    def kernel(ids_ref, *refs):
        part_refs = refs[:chans]
        (
            d_ref, up_ref, down_ref, keep_ref, send_ref, dkeep_ref, dsend_ref, *grad_refs,
            rows_ref, stack_ref, gu_ref, gd_ref, g_ref,
        ) = refs[chans:]
        me = ids_ref[0]
        step = pl.program_id(0)
        normed = take_bands(rows_ref, part_refs, me)
        act, slope = gelu_both(mm(normed, up_ref[...]))
        act = act.astype(bf16)
        stack_bands(stack_ref, mm_nt(act, down_ref[...]))
        deal(stack_ref, keep_ref, send_ref, me & 1, (0,))
        d = d_ref[0]
        d_pre = (mm(d, down_ref[...]) * slope).astype(bf16)
        stack_bands(stack_ref, mm_nt(d_pre, up_ref[...]))
        deal(stack_ref, dkeep_ref, dsend_ref, me & 1, (0,))
        gu = mm_tn(normed, d_pre)
        gd = mm_tn(d, act)

        @pl.when(step == 0)
        def _():
            gu_ref[...] = gu
            gd_ref[...] = gd

        @pl.when(step > 0)
        def _():
            gu_ref[...] += gu
            gd_ref[...] += gd

        @pl.when(step == images - 1)
        def _():
            for part in range(4):
                source = (gu_ref, gd_ref)[part // 2]
                columns = slice((part % 2) * part_width, (part % 2 + 1) * part_width)
                for b in range(patchs):
                    g_ref[b] = source[b * size : (b + 1) * size, columns].astype(bf16)
                deal(g_ref, grad_refs[2 * part], grad_refs[2 * part + 1], ids_ref[1] & 1)

    per = lambda rows: pl.BlockSpec((1, rows, width), lambda i, _: (i, 0, 0))
    half = pl.BlockSpec((chans // 2, 1, band, width), lambda i, _: (0, i, 0, 0))
    halves = shape_of((chans // 2, images, band, width))
    size = width // patchs
    part_width = hidden // 2
    grads = (patchs // 2, size, part_width)
    return call(
        kernel,
        ids,
        (images,),
        (*parts, d_rows, w_up, w_down),
        [per(band)] * chans + [per(tokens), whole(w_up.shape), whole(w_down.shape)],
        [halves] * 4 + [shape_of(grads)] * 8,
        [half] * 4 + [pl.BlockSpec(grads, lambda i, _: (0, 0, 0))] * 8,
        [
            pltpu.VMEM((tokens, width), f32),
            pltpu.VMEM((chans, band, width), bf16),
            pltpu.VMEM((width, hidden), f32),
            pltpu.VMEM((width, hidden), f32),
            pltpu.VMEM((patchs, size, part_width), bf16),
        ],
        micros=26,
        earlier=earlier,
        through=through,
    )


def attention_backward(parts, normed, qkv, mixed, logs, w_qkv, w_attn, patchs, ids, earlier=(), through=()):
    chans = len(parts)
    images, band, width = parts[0].shape
    tokens = band * chans
    own = w_attn.shape[1]
    heads = own // HEAD_DIM
    scale = 1.0 / math.sqrt(HEAD_DIM)

    def kernel(ids_ref, *refs):
        part_refs = refs[:chans]
        (
            n_ref, qkv_ref, o_ref, log_ref, qkv_w_ref, attn_ref, keep_ref, send_ref, gkeep_ref, gsend_ref,
            rows_ref, stack_ref, acc_ref, g_ref,
        ) = refs[chans:]
        me = ids_ref[0]
        step = pl.program_id(0)
        d = take_bands(rows_ref, part_refs, me)
        d_mixed = mm(d, attn_ref[...]).astype(bf16)
        q, k, v = (qkv_ref[t, 0] for t in range(3))
        grads = ([], [], [])
        for h in range(heads):
            at = slice(h * HEAD_DIM, (h + 1) * HEAD_DIM)
            soft = jnp.exp(mm_nt(q[:, at], k[:, at]) * scale - log_ref[0, :, h : h + 1])
            d_soft = mm_nt(d_mixed[:, at], v[:, at])
            across = jnp.sum(d_soft * soft, axis=-1, keepdims=True)
            d_scores = (soft * (d_soft - across)).astype(bf16)
            grads[0].append((mm(d_scores, k[:, at]) * scale).astype(bf16))
            grads[1].append((mm_tn(d_scores, q[:, at]) * scale).astype(bf16))
            grads[2].append(mm_tn(soft.astype(bf16), d_mixed[:, at]).astype(bf16))
        grads = [jnp.concatenate(v, axis=1) for v in grads]
        total = None
        for t in range(3):
            term = mm_nt(grads[t], qkv_w_ref[t])
            total = term if total is None else total + term
        stack_bands(stack_ref, total)
        deal(stack_ref, keep_ref, send_ref, me & 1, (0,))
        new = [mm_tn(n_ref[0], g) for g in grads] + [mm_tn(d, o_ref[0])]

        @pl.when(step == 0)
        def _():
            for t in range(4):
                acc_ref[:, t * own : (t + 1) * own] = new[t]

        @pl.when(step > 0)
        def _():
            for t in range(4):
                acc_ref[:, t * own : (t + 1) * own] += new[t]

        @pl.when(step == images - 1)
        def _():
            for b in range(patchs):
                g_ref[b] = acc_ref[b * size : (b + 1) * size].astype(bf16)
            deal(g_ref, gkeep_ref, gsend_ref, ids_ref[1] & 1)

    per = lambda rows, cols: pl.BlockSpec((1, rows, cols), lambda i, _: (i, 0, 0))
    half = pl.BlockSpec((chans // 2, 1, band, width), lambda i, _: (0, i, 0, 0))
    halves = shape_of((chans // 2, images, band, width))
    size = width // patchs
    out = (patchs // 2, size, 4 * own)
    return call(
        kernel,
        ids,
        (images,),
        (*parts, normed, qkv, mixed, logs, w_qkv, w_attn),
        [per(band, width)] * chans
        + [
            per(tokens, width),
            pl.BlockSpec((3, 1, tokens, own), lambda i, _: (0, i, 0, 0)),
            per(tokens, own),
            per(tokens, 128),
            whole(w_qkv.shape),
            whole(w_attn.shape),
        ],
        [halves] * 2 + [shape_of(out)] * 2,
        [half] * 2 + [pl.BlockSpec(out, lambda i, _: (0, 0, 0))] * 2,
        [
            pltpu.VMEM((tokens, width), f32),
            pltpu.VMEM((chans, band, width), bf16),
            pltpu.VMEM((width, 4 * own), f32),
            pltpu.VMEM((patchs, size, 4 * own), bf16),
        ],
        micros=24,
        earlier=earlier,
        through=through,
    )


def standardize(values, epsilon):
    center = values - jnp.mean(values, axis=-1, keepdims=True)
    inverse = lax.rsqrt(jnp.mean(center * center, axis=-1, keepdims=True) + epsilon)
    return center * inverse, inverse


def norm_back(grad, gain, unit, inverse):
    scaled = grad * gain
    return inverse * (
        scaled
        - jnp.mean(scaled, axis=-1, keepdims=True)
        - unit * jnp.mean(scaled * unit, axis=-1, keepdims=True)
    )


def body(
    vit_in,
    conv_in,
    ln_one,
    w_qkv,
    w_attn,
    ln_two,
    w_up,
    w_down,
    conv_kernel,
    conv_gain,
    conv_up,
    conv_down,
    layer_scale,
    w_proj,
    adapter_kernel,
    gate_in,
    gate_out,
    d_merged,
    d_conv_out,
):
    chans = lax.axis_size("chan")
    patchs = lax.axis_size("patch")
    me = lax.axis_index("chan")
    ids = jnp.stack([me, lax.axis_index("patch")]).astype(jnp.int32)
    tokens, images, width = vit_in.shape
    band = tokens // chans
    own_channels, _, cells = conv_in.shape
    channels = own_channels * chans
    lanes = images * cells
    hidden = w_up.shape[1]
    own_width = w_attn.shape[1]

    def own_rows(values, size):
        return lax.dynamic_slice_in_dim(values, me * size, size, 0)

    def own_band(values):
        return lax.dynamic_slice_in_dim(values, me * band, band, 0).swapaxes(0, 1)

    places = [(p * chans + c, c * patchs + p) for p in range(patchs) for c in range(chans)]

    def placed(values):
        return lax.ppermute(values, ("patch", "chan"), places)

    everywhere = patchs * chans
    rows = own_channels // patchs

    def share(shares, kind, unit):
        flat = [v.astype(kind).reshape(chans, patchs, -1) for v in shares]
        flat = jnp.concatenate(flat, axis=2)
        flat = jnp.pad(flat, ((0, 0), (0, 0), (0, -flat.shape[2] % (rows * unit))))
        flat = flat.reshape(chans, patchs, rows, -1)
        return halving_order(flat, "chan")

    def unshare(values, shares):
        flat = values.reshape(-1)
        out = []
        for v in shares:
            size = v.size // everywhere
            out.append(flat[:size].reshape((v.shape[0] // everywhere,) + v.shape[1:]).astype(f32))
            flat = flat[size:]
        return out

    def summed(pair):
        return pair[0].astype(f32) + pair[1].astype(f32)

    top = 1 << (bit_count(chans) - 1)

    conv_flat = conv_in.reshape(own_channels, lanes)
    weights = tap_weights(own_rows(conv_kernel, own_channels))
    mapped = depthwise(conv_flat, weights)

    gain_one = ln_one.astype(f32)[None]
    gain_two = ln_two.astype(f32)[None]
    w_three = w_qkv.swapaxes(0, 1)

    def attend():
        normed, qkv, mixed, logs, keep, send = attention_forward(
            vit_in.swapaxes(0, 1), gain_one, w_three, w_attn, chans, ids
        )
        pair = fold(keep, swap(send, "chan", 1), "chan", 0)
        return (normed, qkv, mixed, logs), pair, plain(conv_up.T), plain(d_merged.swapaxes(0, 1))

    ((normed_one, qkv, mixed, logs), (keep, send), conv_up_t, d_rows), (far, near) = beside(
        attend, [(mapped, "chan", top), (mapped, "chan", 1)]
    )
    mapped_parts = parts_beside(mapped, near, far)

    gain_all = conv_gain.astype(f32)[:, None]
    vit_band = own_band(vit_in).astype(f32)

    def conv():
        got = swap(send, "chan", 2)
        *half, kept = conv_forward(mapped_parts, conv_up_t, conv_down, gain_all, ids, (), (keep,))
        total = finish(kept, got, "chan", 1)
        normed = (standardize(vit_band + summed(total), vit_eps)[0] * gain_two).astype(bf16)
        exchanged = swap(normed, "chan", top), swap(normed, "chan", 1)
        whole = conv_forward(
            mapped_parts, conv_up_t, conv_down, gain_all, ids, (normed,), part=1, into=half
        )
        return whole, total, normed, exchanged

    (conv_norm, conv_act, conv_slope, stats, conv_keep, conv_send), attended, normed_band, (far, near) = beside(
        conv, []
    )[0]
    middle = vit_band + summed(attended)
    unit_two, inverse_two = standardize(middle, vit_eps)
    normed_parts = parts_beside(normed_band, near, far)
    conv_keep, conv_send = fold(conv_keep, swap(conv_send, "chan", 1), "chan", 0)

    def forward():
        out_keep, out_send, keep, send, *grads = feed_forward(
            normed_parts, d_rows, w_up, w_down, patchs, ids
        )
        out = fold(out_keep, swap(out_send, "chan", 1), "chan", 0)
        return out, fold(keep, swap(send, "chan", 1), "chan", 0), grads

    ((out_keep, out_send), (keep, send), grads), (got,) = beside(
        forward, [(conv_send, "chan", 2)]
    )

    own_scale = own_rows(layer_scale, own_channels).astype(f32)[:, None]
    conv_sum = finish(conv_keep, got, "chan", 1)
    vit = list(zip(grads[::2], grads[1::2]))
    (branch_maps, conv_result, pooled, *pieces), (got, vit_0) = beside(
        lambda: pool_forward(*conv_sum, conv_flat, own_scale, images, band, chans, ids),
        [(send, "chan", 2), (vit[0][1], "patch", 1)],
    )

    d_band = own_band(d_merged)
    d_two = finish(keep, got, "chan", 1)

    d_normed_two = summed(d_two)
    d_middle = d_band.astype(f32) + norm_back(d_normed_two, gain_two, unit_two, inverse_two)
    d_attended = d_middle.astype(bf16)
    g_ln_two = jnp.sum(d_normed_two * unit_two, axis=(0, 1))
    (w_own, conv_down_t, d_out), (vit_1, *got) = beside(
        lambda: (
            own_rows(w_proj, own_channels),
            plain(conv_down.T),
            plain(d_conv_out.reshape(own_channels, lanes)),
        ),
        [(vit[1][1], "patch", 1)] + [(pieces[offset], "chan", offset) for offset in range(1, chans)],
    )
    pieces[1:] = got

    kernel_three = jnp.pad(adapter_kernel.astype(f32).T, ((0, 7), (0, 0)))
    ((gated, d_smooth, g_gate_in, g_gate_out, g_adapter), vit_a, vit_b), (d_far, d_near, vit_2) = beside(
        lambda: (
            adapter(pieces, w_proj, kernel_three, gate_in, gate_out, d_band, ids),
            fold(vit[0][0], vit_0, "patch", 0),
            fold(vit[1][0], vit_1, "patch", 0),
        ),
        [(d_attended, "chan", top), (d_attended, "chan", 1), (vit[2][1], "patch", 1)],
    )
    d_parts = parts_beside(d_attended, d_near, d_far)
    vit_keep, vit_send = (jnp.concatenate(v, axis=2) for v in zip(vit_a, vit_b))
    shares = [g_gate_in, g_gate_out, g_adapter[:9].T, g_ln_two]
    ((shared_keep, shared_send), vit_a), (far, near, vit_3, vit_got) = beside(
        lambda: (halves(share(shares, bf16, 128), "chan"), fold(vit[2][0], vit_2, "patch", 0)),
        [(d_smooth, "chan", top), (d_smooth, "chan", 1), (vit[3][1], "patch", 1), (vit_send, "patch", 2)],
    )
    smooth_parts = parts_beside(d_smooth, near, far)
    vit_keep, vit_send = fold(vit_keep, vit_got, "patch", 1)
    shared_keep, shared_send = halves_at(shared_keep + swap(shared_send, "chan", 1), "chan", 1)

    ((d_result, d_branch, g_proj, g_scale), vit_b), (shared_got, vit_got) = beside(
        lambda: (
            adapter_back(
                smooth_parts, w_own, kernel_three, pooled, d_out, branch_maps, own_scale, ids
            ),
            fold(vit[3][0], vit_3, "patch", 0),
        ),
        [(shared_send, "chan", 2), (vit_send, "patch", 4)],
    )
    up_sum = finish(vit_keep, vit_got, "patch", 2)
    vit_keep, vit_send = (jnp.concatenate(v, axis=2) for v in zip(vit_a, vit_b))
    shared = sum_scatter(shared_keep + shared_got, "chan", 2).reshape(own_channels, -1)
    early = jnp.concatenate([g_proj, shared], axis=1).reshape(patchs, rows, -1)
    early_keep, early_send = halves(halving_order(early, "patch"), "patch")

    (one_keep, one_send, att_keep, att_send), (far, near, early_got, vit_got) = beside(
        lambda: attention_backward(
            d_parts, normed_one, qkv, mixed, logs, w_three, w_attn, patchs, ids
        ),
        [
            (d_branch, "chan", top),
            (d_branch, "chan", 1),
            (early_send, "patch", 1),
            (vit_send, "patch", 2),
        ],
    )
    branch_parts = parts_beside(d_branch, near, far)
    vit_keep, vit_send = fold(vit_keep, vit_got, "patch", 1)
    early_keep, early_send = fold(early_keep, early_got, "patch", 0)

    (d_all, *down), (got, one_got, att_got, vit_got, early_got) = beside(
        lambda: down_gradient(branch_parts, conv_act, patchs, ids),
        [
            (out_send, "chan", 2),
            (one_send, "chan", 1),
            (att_send, "patch", 1),
            (vit_send, "patch", 4),
            (early_send, "patch", 2),
        ],
    )
    down_sum = finish(vit_keep, vit_got, "patch", 2)
    out_sum = finish(out_keep, got, "chan", 1)
    att_keep, att_send = fold(att_keep, att_got, "patch", 0)
    early_keep, early_send = fold(early_keep, early_got, "patch", 1)
    one_keep, one_send = fold(one_keep, one_got, "chan", 0)

    (d_pre, conv_keep, conv_send, sums), (first_got, one_got, early_got, att_got) = beside(
        lambda: conv_backward(d_all, conv_down_t, conv_up, conv_slope, conv_norm, gain_all, ids),
        [
            (down[1], "patch", 1),
            (one_send, "chan", 2),
            (early_send, "patch", 4),
            (att_send, "patch", 2),
        ],
    )
    first_keep, first_send = fold(down[0], first_got, "patch", 0)
    att_keep, att_send = fold(att_keep, att_got, "patch", 1)

    def dealt():
        pair = fold(conv_keep, swap(conv_send, "chan", 1), "chan", 0)
        early = summed(finish(early_keep, early_got, "patch", 2)).astype(bf16)
        return pair, sums + swap(sums, "chan", 1), early, weight_gradient(conv_norm, d_pre, patchs, ids)

    ((conv_keep, conv_send), sums, early, up), (second_got, first_got, att_got) = beside(
        dealt, [(down[3], "patch", 1), (first_send, "patch", 2), (att_send, "patch", 4)]
    )
    att_sum = finish(att_keep, att_got, "patch", 2)
    first_keep, first_send = fold(first_keep, first_got, "patch", 1)
    second_keep, second_send = fold(down[2], second_got, "patch", 0)

    def back_one():
        d_normed_one = summed(finish(one_keep, one_got, "chan", 1))
        unit_one, inverse_one = standardize(vit_band, vit_eps)
        g_vit = d_middle + norm_back(d_normed_one, gain_one, unit_one, inverse_one)
        return (
            g_vit.astype(bf16),
            halves(share([jnp.sum(d_normed_one * unit_one, axis=(0, 1))], f32, 1), "chan"),
            summed(att_sum),
            conv_result.reshape(conv_in.shape),
            plain((middle + summed(out_sum) + gated).astype(bf16).swapaxes(0, 1)),
        )

    (g_vit, (one_keep, one_send), att_grads, conv_out, merged), (
        conv_got, third_got, sums_got, first_got, second_got
    ) = beside(
        back_one,
        [
            (conv_send, "chan", 2),
            (up[1], "patch", 1),
            (sums, "chan", 2),
            (first_send, "patch", 4),
            (second_send, "patch", 2),
        ],
    )
    sums = sum_all(sums + sums_got, "chan", 2) * (1.0 / channels)
    first_sum = finish(first_keep, first_got, "patch", 2)
    second_keep, second_send = fold(second_keep, second_got, "patch", 1)
    third_keep, third_send = fold(up[0], third_got, "patch", 0)

    own_gain = own_rows(conv_gain, own_channels).astype(f32)[:, None]
    conv_sum = finish(conv_keep, conv_got, "chan", 1)
    (g_conv_in, g_kernel, g_gain), (fourth_got, second_got, third_got, vit_far, vit_near, one_got, own_early) = beside(
        lambda: depthwise_back(
            *conv_sum, mapped, stats, sums, own_gain, conv_flat, weights, d_result, images
        ),
        [
            (up[3], "patch", 1),
            (second_send, "patch", 4),
            (third_send, "patch", 2),
            (g_vit, "chan", top),
            (g_vit, "chan", 1),
            (one_send, "chan", 1),
            (early, ("patch", "chan"), places),
        ],
    )
    second_sum = finish(second_keep, second_got, "patch", 2)
    third_keep, third_send = fold(third_keep, third_got, "patch", 1)
    fourth_keep, fourth_send = fold(up[2], fourth_got, "patch", 0)

    def late_sum():
        shared_one = sum_scatter(one_keep + one_got, "chan", 1).reshape(own_channels, -1)
        late = jnp.concatenate([g_kernel, g_gain[:, None], g_scale[:, :1], shared_one], axis=1)
        late = jnp.pad(late, ((0, 0), (0, -late.shape[1] % 128)))
        late = halving_order(late.reshape(patchs, rows, -1), "patch")
        total = sum_scatter(late, "patch")
        whole_rows = jnp.zeros((tokens, images, width), f32)
        for offset, part in enumerate(parts_beside(g_vit, vit_near, vit_far)):
            whole_rows = lax.dynamic_update_slice_in_dim(
                whole_rows, part.swapaxes(0, 1).astype(f32), (me ^ offset) * band, 0
            )
        return total, plain(whole_rows)

    (late, g_vit_in), (fourth_got, third_got) = beside(
        late_sum, [(fourth_send, "patch", 2), (third_send, "patch", 4)]
    )
    fourth_keep, fourth_send = fold(fourth_keep, fourth_got, "patch", 1)
    third_sum = finish(third_keep, third_got, "patch", 2)

    def last():
        sums = [summed(v) for v in (up_sum, down_sum, first_sum, second_sum, third_sum)]
        return sums, own_early[:, :width].astype(f32), unshare(own_early[:, width:], shares)

    ((g_up, g_down, first, second, third), g_proj, pieces), (fourth_got, own_late) = beside(
        last,
        [(fourth_send, "patch", 4), (late, ("patch", "chan"), places)],
    )
    g_conv_down = jnp.concatenate([first, second], axis=1)
    g_gate_in, g_gate_out, g_adapter, g_ln_two = pieces
    fourth_sum = finish(fourth_keep, fourth_got, "patch", 2)
    g_conv_up = jnp.concatenate([third, summed(fourth_sum)], axis=1)
    (g_ln_one,) = unshare(own_late[:, 51:52], [ln_one])
    qkv_width = 3 * own_width
    return (
        merged,
        conv_out,
        g_vit_in,
        g_conv_in,
        g_ln_one,
        att_grads[:, :qkv_width].reshape(-1, 3, own_width),
        att_grads[:, qkv_width:],
        g_ln_two,
        g_up,
        g_down,
        own_late[:, :49],
        own_late[:, 49],
        g_conv_up,
        g_conv_down,
        own_late[:, 50],
        g_proj,
        g_adapter,
        g_gate_in,
        g_gate_out,
    )


def solution(mesh):
    in_specs = (
        P(None, "patch", None),
        P("chan", "patch", None),
        P(),
        P(None, None, "chan"),
        P(None, "chan"),
        P(),
        P(None, "chan"),
        P(None, "chan"),
        P(),
        P(),
        P(None, "chan"),
        P(None, "chan"),
        P(),
        P(),
        P(),
        P(),
        P(),
        P(None, "patch", None),
        P("chan", "patch", None),
    )
    out_specs = (
        P("chan", "patch", None),
        P("chan", "patch", None),
        P(None, "patch", None),
        P("chan", "patch", None),
        P(("patch", "chan")),
        P("patch", None, "chan"),
        P("patch", "chan"),
        P(("patch", "chan")),
        P("patch", "chan"),
        P("patch", "chan"),
        P(("patch", "chan"), None),
        P(("patch", "chan")),
        P("patch", "chan"),
        P("patch", "chan"),
        P(("patch", "chan")),
        P(("patch", "chan"), None),
        P(("patch", "chan"), None),
        P(("patch", "chan"), None),
        P(("patch", "chan"), None),
    )
    return jax.shard_map(body, mesh=mesh, in_specs=in_specs, out_specs=out_specs, check_vma=False)
```
